128 devices in a mesh: ctx: 8 (over y_lo, x), exp: 4 (over y_hi, core), fsdp: 4 (over z).
Axes of the slice: x: 4, y: 4 (y_hi: 2, y_lo: 2; y = y_hi * 2 + y_lo), z: 4, core: 2. Of those that a mesh axis runs over, the one named last changes fastest.
Arguments:
- inputs: bfloat16 [16, 1024, 1024], P(('exp', 'fsdp'), 'ctx'), may hold values from -6 to 6
- cotangent: bfloat16 [16, 1024, 1024], P(('exp', 'fsdp'), 'ctx'), may hold values from -6 to 6
- w_query: bfloat16 [1024, 1024], P(('ctx', 'exp', 'fsdp')), may hold values from -0.1875 to 0.1875
- key_weight: bfloat16 [1024, 512], P(('ctx', 'exp', 'fsdp')), may hold values from -0.1875 to 0.1875
- value_weight: bfloat16 [1024, 512], P(('ctx', 'exp', 'fsdp')), may hold values from -0.1875 to 0.1875
- w_output: bfloat16 [1024, 1024], P(None, ('ctx', 'exp', 'fsdp')), may hold values from -1.5 to 1.5
- w_router: bfloat16 [1024, 32], P(('ctx', 'exp', 'fsdp')), may hold values from -0.09375 to 0.09375
- norm_gains: bfloat16 [2176], P(('ctx', 'exp', 'fsdp')), may hold values from 0.5 to 1.5
- w_gate_up: bfloat16 [32, 1024, 1024], P('exp', ('ctx', 'fsdp')), may hold values from -0.1875 to 0.1875
- w_down: bfloat16 [32, 512, 1024], P('exp', None, ('ctx', 'fsdp')), may hold values from -1 to 1
- seq_lengths: int32 [16, 4], P(('exp', 'fsdp')), may hold values from 1 to 897, 1024 in all within a row
- block_map: int32 [16, 8], P(('exp', 'fsdp')), may hold values from 0 to 7, each once within a row
- routes: int32 [16, 1024, 8], P(('exp', 'fsdp'), 'ctx'), may hold values from 0 to 31, all different within a row; in each aligned block of 128 rows (0 to 127, 128 to 255, ..., all dimensions but the last counted through in order) at most 80 rows name the same one
- priority: int32 [16, 8, 128], P(('exp', 'fsdp'), 'ctx'), may hold values from 0 to 127, each once within a row
Outputs:
- output: bfloat16 [16, 1024, 1024], P(('exp', 'fsdp'), 'ctx')
- grad_inputs: bfloat16 [16, 1024, 1024], P(('exp', 'fsdp'), 'ctx')
- grad_query: float32 [1024, 1024], P(('ctx', 'exp', 'fsdp'))
- grad_key: float32 [1024, 512], P(('ctx', 'exp', 'fsdp'))
- grad_value: float32 [1024, 512], P(('ctx', 'exp', 'fsdp'))
- grad_w_output: float32 [1024, 1024], P(None, ('ctx', 'exp', 'fsdp'))
- grad_router: float32 [1024, 32], P(('ctx', 'exp', 'fsdp'))
- grad_gains: float32 [2176], P(('ctx', 'exp', 'fsdp'))
- grad_gate_up: float32 [32, 1024, 1024], P('exp', ('ctx', 'fsdp'))
- grad_down: float32 [32, 512, 1024], P('exp', None, ('ctx', 'fsdp'))
The draws below stay inside these ranges and needn't reach their ends.
Inputs may be any that keep to these rules, and one draw needn't show every extreme that they name: `seq_lengths`: the 4 lengths of a group add up to 1024; the longest has exactly 897 tokens. `block_map`: each row is a permutation of the 8 blocks. `routes`: each slot names 8 different experts; among the slots of one place no expert is named more than 2 * 40 times, and some expert exactly that often. `priority`: each place's row is a permutation.
All inputs are finite; a program needn't handle non-finite values.
Results may differ from the reference program's by a relative error of at most 0.03.
Values may be sent and summed in bfloat16 or wider, within the bound.
A program may use at most 192 MiB of HBM per device.

```python
import math
import jax
import jax.numpy as jnp
import numpy as np
from jax import lax

MODEL_DIM = 1024
QUERY_HEADS = 16
KEY_VALUE_HEADS = 8
HEAD_DIM = 64
FF = 512
TOPK = 8
BLK = 128
NSEQ = 4
EXPERTS = 32
GTOK = 1024
ROWS = 128
NBLK = 8
GROUPS = 16
CAP = 40
GAIN_LEN = 2176
N_CTX = 8


def level_of(own_key, shape, shards, smallest, high):
    def one(dim, blocks):
        heights = jax.random.uniform(jax.random.fold_in(jax.random.fold_in(own_key, 6), dim), (blocks,), jnp.float32, smallest / len(shards), high / len(shards))
        return jnp.repeat(jnp.exp(heights), shape[dim] // blocks).reshape((-1,) + (1,) * (len(shape) - dim - 1))

    factor_of = one(*shards[0])
    for cut in shards[1:]:
        factor_of = factor_of * one(*cut)
    return factor_of


def profile(amount, total, bound, slope):
    weights = [(1 << 20) // math.isqrt(rank ** slope) + 1 for rank in range(2, amount + 1)]
    spare, given = total - bound - (amount - 1), [1] * (amount - 1)
    while spare > 0:
        candidates = [i for i in range(amount - 1) if given[i] < bound]
        whole, left = sum([weights[i] for i in candidates]), spare
        for i in candidates:
            more = min(bound - given[i], max(1, left * weights[i] // whole), spare)
            given[i] = given[i] + more
            spare = spare - more
    return np.array([bound] + given)


def ragged_sizes(rng, amount, total, most, lean):
    if amount == 2:
        one = jax.random.randint(rng, (), max(1, total - most), min(most, total - 1) + 1)
        return jnp.stack([one, total - one])
    tallies = jnp.asarray(profile(amount, total, most, lean), jnp.int32)
    couples = (amount - 1) // 2
    donor, receiver = tallies[1:1 + 2 * couples:2], tallies[2:2 + 2 * couples:2]
    room = jnp.minimum(donor - 1, most - receiver)
    moved = jax.random.randint(jax.random.fold_in(rng, 1), (couples,), 0, 1 << 20) % (room + 1)
    tallies = tallies.at[1:1 + 2 * couples:2].set(donor - moved).at[2:2 + 2 * couples:2].set(receiver + moved)
    return tallies[jax.random.permutation(jax.random.fold_in(rng, 2), amount)]


def shared_out(own_key, own, number, rows, count, top, reach, slope):
    order = jax.random.permutation(own_key, count)
    crowded, usual = load_shares(count, rows * top, reach, slope, True), load_shares(count, rows * top, reach, slope, False)
    places = jnp.arange(count)

    def named(lengths, rotation):
        used = int((lengths > 0).sum())
        fixed = max(1, used // 4)
        moved = fixed + (places - fixed + rotation * (used - fixed)) % max(1, count - fixed)
        return jnp.zeros((count,), jnp.int32).at[order[jnp.where(places < fixed, places, moved)]].set(jnp.asarray(lengths, jnp.int32))

    lengths = jnp.where(number % 4 == 0, named(crowded, number // 4), named(usual, number - number // 4 - 1))
    mixed = jax.random.permutation(jax.random.fold_in(own, 3), count)
    donor, receiver = mixed[0:count // 2 * 2:2], mixed[1:count // 2 * 2:2]
    room = jnp.minimum(lengths[donor] - 1, reach - lengths[receiver]) // 2
    room = jnp.where((donor == order[0]) | (receiver == order[0]) | (lengths[receiver] == 0), 0, jnp.maximum(room, 0))
    moved = jax.random.randint(jax.random.fold_in(own, 4), (count // 2,), 0, 1 << 20) % (room + 1)
    lengths = lengths.at[donor].add(-moved).at[receiver].add(moved)
    members = jnp.searchsorted(jnp.cumsum(lengths), jnp.arange(rows * top), side="right").astype(jnp.int32)
    listing = members.reshape(top, rows).T
    listing = listing[jax.random.permutation(jax.random.fold_in(own, 1), rows)]
    rotation = jax.random.randint(jax.random.fold_in(own, 2), (rows, 1), 0, top)
    return jnp.take_along_axis(listing, (jnp.arange(top)[None, :] + rotation) % top, axis=1)


def load_shares(number_of, total, bound, slope, full):
    portions = [(1 << 20) // math.isqrt(grade ** slope) + 1 for grade in range(1, number_of + 1)]
    largest = bound if full else min(bound, max(-(-total // number_of), total * portions[0] // sum(portions)))
    least = 1 if total - largest >= number_of - 1 else 0
    holding, spare = [largest] + [least] * (number_of - 1), total - largest - least * (number_of - 1)
    while spare > 0:
        candidates = [i for i in range(1, number_of) if holding[i] < largest] or [i for i in range(1, number_of) if holding[i] < bound]
        mass, budget = sum([portions[i] for i in candidates]), spare
        for i in candidates:
            extra = min(bound - holding[i], max(1, budget * portions[i] // mass), spare)
            holding[i] = holding[i] + extra
            spare = spare - extra
    return np.array(holding)


def centred(stream_key, dims, deviation, reach, cuts=(), held_as=jnp.bfloat16):
    entries = deviation * jax.random.normal(stream_key, dims, jnp.float32)
    if cuts:
        entries = entries * level_of(stream_key, dims, cuts, -0.22, 0.18)
    return jnp.clip(entries, -reach, reach).astype(held_as)


def setup_inputs(seed: int = 0) -> dict:
    key_of = jax.random.split(jax.random.key(seed), 15)
    inputs = centred(key_of[0], (GROUPS, GTOK, MODEL_DIM), 1.0, 6.0, ((0, 16), (1, 8)))
    cotangent = centred(key_of[1], (GROUPS, GTOK, MODEL_DIM), 1.0, 6.0, ((0, 16), (1, 8)))
    w_query = centred(key_of[2], (MODEL_DIM, QUERY_HEADS * HEAD_DIM), MODEL_DIM ** -0.5, 0.1875, ((0, 128),))
    key_weight = centred(key_of[3], (MODEL_DIM, KEY_VALUE_HEADS * HEAD_DIM), MODEL_DIM ** -0.5, 0.1875, ((0, 128),))
    value_weight = centred(key_of[4], (MODEL_DIM, KEY_VALUE_HEADS * HEAD_DIM), MODEL_DIM ** -0.5, 0.1875, ((0, 128),))
    w_output = centred(key_of[5], (QUERY_HEADS * HEAD_DIM, MODEL_DIM), (QUERY_HEADS * HEAD_DIM // 64) ** -0.5, 1.5, ((1, 128),))
    w_router = centred(key_of[6], (MODEL_DIM, EXPERTS), (4 * MODEL_DIM) ** -0.5, 0.09375, ((0, 128),))
    norm_gains = jnp.clip(1.0 + 0.1 * jax.random.normal(key_of[7], (GAIN_LEN,), jnp.float32), 0.5, 1.5).astype(jnp.bfloat16)
    w_gate_up = centred(key_of[8], (EXPERTS, MODEL_DIM, 2 * FF), MODEL_DIM ** -0.5, 0.1875, ((0, 4), (1, 32)))
    w_down = centred(key_of[9], (EXPERTS, FF, MODEL_DIM), (FF // 16) ** -0.5, 1.0, ((0, 4), (2, 32)))
    seq_lengths = jax.vmap(lambda own: ragged_sizes(own, NSEQ, GTOK, GTOK - ROWS + 1, 2))(jax.random.split(key_of[10], GROUPS)).reshape((GROUPS, NSEQ)).astype(jnp.int32)
    block_map = jax.vmap(lambda own: jax.random.permutation(own, NBLK))(jax.random.split(key_of[11], GROUPS)).reshape((GROUPS, NBLK)).astype(jnp.int32)
    routes_keys = jax.random.split(jax.random.fold_in(key_of[12], 1), GROUPS * GTOK // ROWS)
    routes_turns = jax.random.permutation(jax.random.fold_in(key_of[12], 3), GROUPS * GTOK // ROWS)
    routes = jax.vmap(lambda own, number: shared_out(jax.random.fold_in(key_of[12], 2), own, number, ROWS, EXPERTS, TOPK, 2 * CAP, 1))(routes_keys, routes_turns).reshape((GROUPS, GTOK, TOPK))
    priority = jax.vmap(lambda own: jax.random.permutation(own, ROWS))(jax.random.split(key_of[13], GROUPS * N_CTX)).reshape((GROUPS, N_CTX, ROWS)).astype(jnp.int32)
    return {"inputs": inputs, "cotangent": cotangent, "w_query": w_query, "key_weight": key_weight, "value_weight": value_weight, "w_output": w_output, "w_router": w_router, "norm_gains": norm_gains, "w_gate_up": w_gate_up, "w_down": w_down, "seq_lengths": seq_lengths, "block_map": block_map, "routes": routes, "priority": priority}


@jax.custom_vjp
def lower_precision(v):
    return lax.optimization_barrier(v.astype(jnp.bfloat16)).astype(jnp.float32)

@jax.custom_vjp
def lower_precision_back(v):
    return v

def low_keep(v):
    return (lower_precision(v), None)

def low_pass(kept, grad):
    return (grad,)

def back_keep(v):
    return (v, None)

def back_low(kept, grad):
    return (lower_precision(grad),)
lower_precision.defvjp(low_keep, low_pass)
lower_precision_back.defvjp(back_keep, back_low)
highest = lax.Precision.HIGHEST

def matrix_product(left, right):
    return jnp.dot(left, right, precision=highest)

def rms_scale(value_entries):
    return lax.rsqrt(lax.optimization_barrier(jnp.mean(value_entries * value_entries, axis=-1, keepdims=True)) + 1e-06)

def rope_tables(position):
    index_half = jnp.arange(HEAD_DIM // 2, dtype=jnp.float32)
    frequency = jnp.exp(index_half * (-2.0 * math.log(10000.0) / HEAD_DIM))
    angles = position.astype(jnp.float32)[:, None] * frequency[None, :]
    return (jnp.cos(angles), jnp.sin(angles))

def rotate(value_entries, cos_table, sin_table):
    half_width = value_entries.shape[-1] // 2
    first_half = value_entries[..., :half_width]
    second_half = value_entries[..., half_width:]
    return jnp.concatenate([first_half * cos_table - second_half * sin_table, second_half * cos_table + first_half * sin_table], axis=-1)

def layout(lengths_row, block_row):
    slot_ids = jnp.arange(GTOK, dtype=jnp.int32)
    token_ids = (block_row[slot_ids // BLK] * BLK + slot_ids % BLK).astype(jnp.int32)
    seq_ends = jnp.cumsum(lengths_row).astype(jnp.int32)
    passed = (token_ids[:, None] >= seq_ends[None, :]).astype(jnp.int32)
    sequence = lax.optimization_barrier(jnp.sum(passed, axis=1, dtype=jnp.int32))
    position = token_ids - lax.optimization_barrier(jnp.sum(passed * lengths_row[None, :], axis=1, dtype=jnp.int32))
    return (token_ids, sequence, position)

def attention(normalized_input, w_query, key_weight, value_weight, w_output, query_gain, key_gain, token_ids, sequence, position):
    grand_total = normalized_input.shape[0]
    query_pre = lower_precision_back(matrix_product(normalized_input, w_query)).reshape(grand_total, QUERY_HEADS, HEAD_DIM)
    key_prenorm = lower_precision_back(matrix_product(normalized_input, key_weight)).reshape(grand_total, KEY_VALUE_HEADS, HEAD_DIM)
    value_entries = lower_precision(lower_precision_back(matrix_product(normalized_input, value_weight))).reshape(grand_total, KEY_VALUE_HEADS, HEAD_DIM)
    cos_table, sin_table = rope_tables(position)
    cos_table = cos_table[:, None, :]
    sin_table = sin_table[:, None, :]
    query_rows_all = lower_precision(rotate(query_pre * rms_scale(query_pre) * query_gain, cos_table, sin_table))
    keys_rot = lower_precision(rotate(key_prenorm * rms_scale(key_prenorm) * key_gain, cos_table, sin_table))
    query_rows_all = query_rows_all.reshape(grand_total, KEY_VALUE_HEADS, QUERY_HEADS // KEY_VALUE_HEADS, HEAD_DIM)
    scores = lower_precision_back(jnp.einsum('tkgd,ukd->kgtu', query_rows_all, keys_rot, precision=highest) * HEAD_DIM ** (-0.5))
    allowed = (sequence[:, None] == sequence[None, :]) & (token_ids[None, :] <= token_ids[:, None])
    weights = lower_precision(jax.nn.softmax(jnp.where(allowed, scores, -1e+30), axis=-1))
    mixed = jnp.einsum('kgtu,ukd->tkgd', weights, value_entries, precision=highest).reshape(grand_total, QUERY_HEADS * HEAD_DIM)
    return lower_precision_back(matrix_product(lower_precision(lower_precision_back(mixed)), w_output))

def slot_index(place_routes, place_priority):
    expert_ids = jnp.arange(EXPERTS, dtype=jnp.int32)
    named = lax.optimization_barrier(jnp.sum((place_routes[..., None] == expert_ids).astype(jnp.int32), axis=2, dtype=jnp.int32))
    before = (place_priority[:, None, :] < place_priority[:, :, None]).astype(jnp.int32)
    counts = jnp.einsum('crs,cse->cre', before, named).astype(jnp.int32)
    ranks = jnp.take_along_axis(counts, place_routes, axis=2)
    flat = jnp.where(ranks < CAP, place_routes * CAP + ranks, EXPERTS * CAP)
    return flat.reshape(N_CTX, ROWS * TOPK).astype(jnp.int32)

def fill_slots(pair_rows, flat):
    empty = jnp.zeros((EXPERTS * CAP, MODEL_DIM), pair_rows.dtype)
    return empty.at[flat].set(pair_rows, mode='drop')

def pick_slots(results, flat):
    padded = jnp.concatenate([results, jnp.zeros((1, MODEL_DIM), results.dtype)], axis=0)
    return padded[flat]

def experts(normalized_input, w_router, w_gate_up, w_down, route_rows, place_priority):
    probs = jax.nn.softmax(lower_precision_back(matrix_product(normalized_input, w_router)), axis=-1)
    chosen = jnp.take_along_axis(probs, route_rows, axis=1)
    gate_share = chosen / lax.optimization_barrier(jnp.sum(chosen, axis=1, keepdims=True))
    flat = slot_index(route_rows.reshape(N_CTX, ROWS, TOPK), place_priority)
    pair_rows = jnp.repeat(normalized_input.reshape(N_CTX, ROWS, MODEL_DIM), TOPK, axis=1)
    buffers = lower_precision_back(jax.vmap(fill_slots)(pair_rows, flat)).reshape(N_CTX, EXPERTS, CAP, MODEL_DIM)
    gate_up = lower_precision_back(jnp.einsum('cepd,edf->cepf', buffers, w_gate_up, precision=highest))
    hidden = lower_precision(jax.nn.silu(gate_up[..., :FF]) * gate_up[..., FF:])
    results = lower_precision_back(lower_precision(jnp.einsum('cepf,efd->cepd', hidden, w_down, precision=highest)))
    picked = jax.vmap(pick_slots)(results.reshape(N_CTX, EXPERTS * CAP, MODEL_DIM), flat)
    picked = picked.reshape(GTOK, TOPK, MODEL_DIM)
    return lax.optimization_barrier(jnp.sum(gate_share[:, :, None] * picked, axis=1))

def group_forward(weights, group_inputs, lengths_row, block_row, route_rows, place_priority):
    w_query, key_weight, value_weight, w_output, w_router, gain_values, w_gate_up, w_down = weights
    token_ids, sequence, position = layout(lengths_row, block_row)
    residual = group_inputs[token_ids]
    normed_one = lower_precision(residual * rms_scale(residual) * gain_values[:MODEL_DIM])
    branch = attention(normed_one, w_query, key_weight, value_weight, w_output, gain_values[2 * MODEL_DIM:2 * MODEL_DIM + HEAD_DIM], gain_values[2 * MODEL_DIM + HEAD_DIM:], token_ids, sequence, position)
    residual_two = residual + branch
    normed_two = lower_precision(residual_two * rms_scale(residual_two) * gain_values[MODEL_DIM:2 * MODEL_DIM])
    result_slots = residual_two + experts(normed_two, w_router, w_gate_up, w_down, route_rows, place_priority)
    return jnp.zeros_like(result_slots).at[token_ids].set(result_slots)

def reference(inputs, cotangent, w_query, key_weight, value_weight, w_output, w_router, norm_gains, w_gate_up, w_down, seq_lengths, block_map, routes, priority):
    floats = tuple((array_in.astype(jnp.float32) for array_in in (inputs, w_query, key_weight, value_weight, w_output, w_router, norm_gains, w_gate_up, w_down)))

    def forward(inputs_float, *weights):
        group_step = jax.checkpoint(lambda group_items: group_forward(weights, *group_items))
        return lax.map(group_step, (inputs_float, seq_lengths, block_map, routes, priority))
    result, pullback = jax.vjp(forward, *floats)
    gradients = pullback(cotangent.astype(jnp.float32))
    return (result.astype(jnp.bfloat16), gradients[0].astype(jnp.bfloat16), gradients[1], gradients[2], gradients[3], gradients[4], gradients[5], gradients[6], gradients[7], gradients[8])
```

```python
import math

import jax
import jax.numpy as jnp
from jax import lax
from jax.sharding import Mesh
from jax.sharding import PartitionSpec as P

HEADS = 16
KV_HEADS = 8
DIM = 1024
HEAD = 64
FF = 512
EXPERTS = 32
TOPK = 8
ROWS = 128
GTOK = 1024
CAP = 40
GAINS = 17
BF = jnp.bfloat16
F32 = jnp.float32

ALL = ("yl", "x", "yh", "co", "z")
SIZES = (2, 4, 2, 2, 4)
CTX = ("yl", "x")
EP = ("yh", "co", "yl", "z")
WT = ("yl", "x", "z")


def exchange(blocks, axes):
    return lax.all_to_all(blocks, axes, split_axis=0, concat_axis=0, tiled=True)


def dot(left, right, dims=((1,), (0,))):
    return lax.dot_general(left, right, (dims, ((), ())), preferred_element_type=F32)


def rms(v):
    return lax.rsqrt(jnp.mean(v * v, axis=-1, keepdims=True) + 1e-06)


def norm_back(v, scale, gain, upstream):
    weighted = upstream * gain
    inner = jnp.mean(weighted * v, axis=-1, keepdims=True)
    return scale * weighted - v * (scale * scale * scale) * inner, upstream * v * scale


def turn(v, cos, sin):
    a, b = v[..., : HEAD // 2], v[..., HEAD // 2 :]
    return jnp.concatenate([a * cos - b * sin, b * cos + a * sin], axis=-1)


def layout(tokens, lengths):
    ends = jnp.cumsum(lengths)
    passed = (tokens[:, None] >= ends[None, :]).astype(jnp.int32)
    return jnp.sum(passed, axis=1), tokens - jnp.sum(passed * lengths[None, :], axis=1)


def shards(
    inputs,
    cotangent,
    w_query,
    key_weight,
    value_weight,
    w_output,
    w_router,
    norm_gains,
    w_gate_up,
    w_down,
    seq_lengths,
    block_map,
    routes,
    priority,
):
    place = lax.axis_index("yl") * 4 + lax.axis_index("x")
    x_own = inputs[0]
    dz_low = cotangent[0]
    dz = dz_low.astype(F32)

    x_all = exchange(jnp.broadcast_to(x_own[None], (8, ROWS, DIM)), CTX).reshape(GTOK, DIM)
    head_rows = jnp.concatenate(
        [
            w_query.reshape(8, 8, 128),
            key_weight.reshape(8, 8, 64),
            value_weight.reshape(8, 8, 64),
            jnp.broadcast_to(w_router[:, None], (8, 8, EXPERTS)),
            jnp.broadcast_to(
                jnp.pad(norm_gains[None, :], ((0, 7), (0, 96 - GAINS)))[:, None], (8, 8, 96)
            ),
        ],
        axis=-1,
    ).transpose(1, 0, 2)
    head_rows = exchange(
        jnp.broadcast_to(head_rows[:, None], (8, 16, 8, 384)).reshape(128, 8, 384), ALL
    )
    w_heads = head_rows[:, :, :256].reshape(DIM, 256)
    router = head_rows[:, :, 256:288].reshape(DIM, EXPERTS)
    gains = head_rows[:, 0, 288 : 288 + GAINS].reshape(128 * GAINS).astype(F32)
    gain_one, gain_two = gains[:DIM], gains[DIM : 2 * DIM]
    gain_q, gain_k = gains[2 * DIM : 2 * DIM + HEAD], gains[2 * DIM + HEAD :]

    picks = jnp.concatenate([routes[0], priority[0, 0][:, None]], axis=1)
    picks = exchange(jnp.broadcast_to(picks[None], (8, ROWS, TOPK + 1)), CTX)
    mine = (block_map[0] == place).astype(jnp.int32)
    picks = jnp.sum(picks * mine[:, None, None], axis=0)
    route, order = picks[:, :TOPK], picks[:, TOPK]
    named = jnp.any(route[:, :, None] == jnp.arange(EXPERTS, dtype=jnp.int32), axis=1)
    before = (order[None, :] < order[:, None]).astype(BF)
    rank = dot(before, named.astype(BF)).astype(jnp.int32)
    slots = named.T[:, None, :] & (
        rank.T[:, None, :] == jnp.arange(CAP, dtype=jnp.int32)[None, :, None]
    )
    spread = slots.astype(BF).reshape(EXPERTS * CAP, ROWS)

    dz_slots = exchange(
        dot(spread, dz_low).astype(BF).reshape(EXPERTS, CAP, DIM), EP
    ).reshape(EXPERTS * CAP, DIM)
    expert_rows = jnp.concatenate([w_gate_up, jnp.swapaxes(w_down, 1, 2)], axis=-1)
    expert_rows = jnp.broadcast_to(
        expert_rows.reshape(2, 1, 4, 32, 3 * FF), (2, 4, 4, 32, 3 * FF)
    )
    expert_rows = exchange(expert_rows.reshape(32, 32, 3 * FF), WT).reshape(DIM, 3 * FF)
    w_gu, w_dn = expert_rows[:, : 2 * FF], expert_rows[:, 2 * FF :]
    w_out = exchange(
        jnp.broadcast_to(w_output.T[None], (128, 8, HEADS * HEAD)), ALL
    ).reshape(DIM, HEADS * HEAD)

    x_all = x_all.astype(F32)
    scale_all = rms(x_all)
    a_all = (x_all * scale_all * gain_one).astype(BF)
    qkv = dot(a_all, w_heads)
    q0, k0 = qkv[:, :128].reshape(GTOK, 2, HEAD), qkv[:, 128:192]
    v = qkv[:, 192:].astype(BF)
    tokens = jnp.arange(GTOK, dtype=jnp.int32)
    sequence, position = layout(tokens, seq_lengths[0])
    frequency = jnp.exp(
        jnp.arange(HEAD // 2, dtype=F32) * (-2.0 * math.log(10000.0) / HEAD)
    )
    angles = position.astype(F32)[:, None] * frequency[None, :]
    cos, sin = jnp.cos(angles), jnp.sin(angles)
    rq, rk = rms(q0), rms(k0)
    qr = turn(q0 * rq * gain_q, cos[:, None], sin[:, None]).astype(BF)
    kr = turn(k0 * rk * gain_k, cos, sin).astype(BF)
    allowed = (sequence[:, None] == sequence[None, :]) & (tokens[None, :] <= tokens[:, None])
    scores = jnp.einsum("thd,ud->htu", qr, kr, preferred_element_type=F32) * HEAD**-0.5
    probs_at = jax.nn.softmax(jnp.where(allowed[None], scores, -1e30), axis=-1)
    probs_low = probs_at.astype(BF)
    mixed = jnp.einsum("htu,ud->thd", probs_low, v, preferred_element_type=F32)
    mixed_low = mixed.astype(BF).reshape(8, ROWS, 128)
    ob = exchange(mixed_low, CTX).transpose(1, 0, 2).reshape(ROWS, HEADS * HEAD)

    x_f32 = x_own.astype(F32)
    x1 = x_f32 + dot(ob, w_out, ((1,), (1,)))
    r2 = rms(x1)
    a2 = (x1 * r2 * gain_two).astype(BF)
    probs = jax.nn.softmax(dot(a2, router), axis=-1)
    chosen = jnp.where(named, probs, 0.0)
    total = jnp.sum(chosen, axis=1, keepdims=True)
    gate = chosen / total

    slot_gate = jnp.sum(jnp.where(slots, gate.T[:, None, :], 0.0), axis=2)
    slot_gate = exchange(slot_gate, EP).reshape(EXPERTS * CAP, 1)
    a2_slots = exchange(
        dot(spread, a2).astype(BF).reshape(EXPERTS, CAP, DIM), EP
    ).reshape(EXPERTS * CAP, DIM)
    gu = dot(a2_slots, w_gu)
    g, up = gu[:, :FF], gu[:, FF:]
    s = jax.nn.sigmoid(g)
    hid = (g * s * up).astype(BF)
    y = dot(hid, w_dn, ((1,), (1,))).astype(BF)
    y = exchange(y.reshape(EXPERTS, CAP, DIM), EP).reshape(EXPERTS * CAP, DIM)
    dy = (slot_gate * dz_slots.astype(F32)).astype(BF)
    dhid = dot(dy, w_dn)
    dgu = jnp.concatenate([dhid * up * s * (1.0 + g * (1.0 - s)), dhid * g * s], axis=-1)
    dgu = dgu.astype(BF)
    da = dot(dgu, w_gu, ((1,), (1,))).astype(BF)
    da = exchange(da.reshape(EXPERTS, CAP, DIM), EP).reshape(EXPERTS * CAP, DIM)
    expert_grad = jnp.concatenate(
        [dot(a2_slots, dgu, ((0,), (0,))), dot(dy, hid, ((0,), (0,)))], axis=-1
    ).astype(BF)
    expert_grad = exchange(expert_grad.reshape(32, 32, 3 * FF), WT)
    expert_grad = jnp.sum(
        expert_grad.reshape(2, 4, 4, 32, 3 * FF).astype(F32), axis=1
    ).reshape(8, 32, 3 * FF)
    grad_gate_up = expert_grad[..., : 2 * FF]
    grad_down = jnp.swapaxes(expert_grad[..., 2 * FF :], 1, 2)

    weigh = jnp.where(slots, gate.T[:, None, :], 0.0).reshape(EXPERTS * CAP, ROWS)
    weigh_high = weigh.astype(BF)
    weigh_low = (weigh - weigh_high.astype(F32)).astype(BF)
    mixture = dot(weigh_high, y, ((0,), (0,))) + dot(weigh_low, y, ((0,), (0,)))
    output = (x1 + mixture).astype(BF)
    pair = dot(y, dz_low, ((1,), (1,))).reshape(EXPERTS, CAP, ROWS)
    dgate = jnp.sum(jnp.where(slots, pair, 0.0), axis=1).T
    dc = jnp.where(named, dgate - jnp.sum(gate * dgate, axis=1, keepdims=True), 0.0) / total
    dl = (probs * (dc - jnp.sum(probs * dc, axis=-1, keepdims=True))).astype(BF)
    da2 = dot(spread, da, ((0,), (0,))) + dot(dl, router, ((1,), (1,)))
    grad_router = dot(a2, dl, ((0,), (0,)))
    dx_two, gain_two_terms = norm_back(x1, r2, gain_two, da2)
    dx1 = dz + dx_two
    db = dx1.astype(BF)

    do_rows = dot(db, w_out).astype(BF)
    do_rows = exchange(do_rows.reshape(ROWS, 8, 128).transpose(1, 0, 2), CTX)
    do_rows = do_rows.reshape(GTOK, 2, HEAD)
    out_grad = exchange(
        dot(db, ob, ((0,), (0,))).astype(BF).reshape(128, 8, HEADS * HEAD), ALL
    )
    grad_w_output = jnp.sum(out_grad.astype(F32), axis=0).T
    dv = jnp.einsum("htu,thd->ud", probs_low, do_rows, preferred_element_type=F32)
    dp = jnp.einsum("thd,ud->htu", do_rows, v, preferred_element_type=F32)
    delta = jnp.sum(do_rows.astype(F32) * mixed, axis=-1).T
    ds = (probs_at * (dp - delta[..., None])).astype(BF)
    dqr = jnp.einsum("htu,ud->thd", ds, kr, preferred_element_type=F32) * HEAD**-0.5
    dkr = jnp.einsum("htu,thd->ud", ds, qr, preferred_element_type=F32) * HEAD**-0.5
    dq0, gain_q_terms = norm_back(q0, rq, gain_q, turn(dqr, cos[:, None], -sin[:, None]))
    dk0, gain_k_terms = norm_back(k0, rk, gain_k, turn(dkr, cos, -sin))
    dqkv = jnp.concatenate([dq0.reshape(GTOK, 128), dk0, dv], axis=-1).astype(BF)
    da1 = dot(dqkv, w_heads, ((1,), (1,)))
    gain_one_grad = jnp.sum(da1 * x_all * scale_all, axis=0)
    da1 = exchange(da1.astype(BF).reshape(8, ROWS, DIM), CTX)
    da1 = jnp.sum(da1.astype(F32), axis=0)
    dx_one, _ = norm_back(x_f32, rms(x_f32), gain_one, da1)
    grad_inputs = (dx1 + dx_one).astype(BF)

    grad_gains = jnp.concatenate(
        [
            gain_one_grad,
            jnp.sum(gain_two_terms, axis=0),
            jnp.sum(gain_q_terms, axis=(0, 1)),
            jnp.sum(gain_k_terms, axis=0),
        ]
    )
    head_grad = jnp.concatenate(
        [
            dot(a_all, dqkv, ((0,), (0,))).reshape(128, 8, 256),
            grad_router.reshape(128, 8, EXPERTS),
            jnp.pad(grad_gains.reshape(128, 1, GAINS), ((0, 0), (0, 7), (0, 96 - GAINS))),
        ],
        axis=-1,
    ).astype(BF)
    head_grad = jnp.sum(exchange(head_grad, ALL).astype(F32).reshape(8, 16, 8, 384), axis=1)
    rows = jnp.swapaxes(head_grad, 0, 1)
    shared = jnp.sum(head_grad, axis=0)
    return (
        output[None],
        grad_inputs[None],
        rows[..., :128].reshape(8, HEADS * HEAD),
        rows[..., 128:192].reshape(8, KV_HEADS * HEAD),
        rows[..., 192:256].reshape(8, KV_HEADS * HEAD),
        grad_w_output,
        shared[:, 256:288],
        shared[0, 288 : 288 + GAINS],
        grad_gate_up,
        grad_down,
    )


def solution(mesh):
    groups = ("yh", "co", "z")
    specs = (
        P(groups, CTX, None),
        P(groups, CTX, None),
        P(ALL, None),
        P(ALL, None),
        P(ALL, None),
        P(None, ALL),
        P(ALL, None),
        P(ALL),
        P(("yh", "co"), WT, None),
        P(("yh", "co"), None, WT),
        P(groups, None),
        P(groups, None),
        P(groups, CTX, None),
        P(groups, CTX, None),
    )
    return jax.shard_map(
        shards,
        mesh=Mesh(mesh.devices.reshape(SIZES), ALL),
        in_specs=specs,
        out_specs=specs[:10],
        check_vma=False,
    )
```

```python
import math

import jax
import jax.numpy as jnp
from jax import lax
from jax.experimental import pallas as pl
from jax.experimental.pallas import tpu as pltpu
from jax.sharding import Mesh
from jax.sharding import PartitionSpec as P

HEADS = 16
KV_HEADS = 8
DIM = 1024
HEAD = 64
FF = 512
EXPERTS = 32
TOPK = 8
ROWS = 128
GTOK = 1024
CAP = 40
GAINS = 17
BF = jnp.bfloat16
F32 = jnp.float32

ALL = ("yl", "x", "yh", "co", "z")
SIZES = (2, 4, 2, 2, 4)
CTX = ("yl", "x")
EP = ("yh", "co", "yl", "z")
WT = ("yl", "x", "z")


SPAN = dict(zip(ALL, SIZES))


def linear(axes):
    index = 0
    for axis in axes:
        index = index * SPAN[axis] + lax.axis_index(axis)
    return index


def device(axes, index):
    at = {}
    for axis in reversed(axes):
        at[axis] = lax.rem(index, SPAN[axis])
        index = index // SPAN[axis]
    return tuple(at[axis] if axis in at else lax.axis_index(axis) for axis in ALL)


def greet(axes):
    n = math.prod(SPAN[axis] for axis in axes)
    me = linear(axes)
    barrier = pltpu.get_barrier_semaphore()

    def signal(i, carry):
        pl.semaphore_signal(
            barrier,
            inc=1,
            device_id=device(axes, lax.rem(me + i, n)),
            device_id_type=pl.DeviceIdType.MESH,
        )
        return carry

    lax.fori_loop(1, n, signal, 0)
    pl.semaphore_wait(barrier, n - 1)


class Send:
    def __init__(self, axes, part, slot, sems):
        self.axes, self.part, self.slot, self.sems = axes, part, slot, sems
        self.n = math.prod(SPAN[axis] for axis in axes)
        self.me = linear(axes)

    def copy(self, i):
        to = lax.rem(self.me + i, self.n)
        return pltpu.make_async_remote_copy(
            src_ref=self.part(to),
            dst_ref=self.slot(self.me),
            send_sem=self.sems.at[0, i],
            recv_sem=self.sems.at[1, i],
            device_id=device(self.axes, to),
            device_id_type=pl.DeviceIdType.MESH,
        )

    def own(self):
        return pltpu.make_async_copy(self.part(self.me), self.slot(self.me), self.sems.at[0, 0])

    def start(self, own=True):
        def one(i, carry):
            self.copy(i).start()
            return carry

        if own:
            self.own().start()
        lax.fori_loop(1, self.n, one, 0)

    def wait(self, own=True):
        def one(i, carry):
            self.copy(i).wait()
            return carry

        if own:
            self.own().wait()
        lax.fori_loop(1, self.n, one, 0)


def sems(n):
    return pltpu.SemaphoreType.DMA((2, n))


def move(body, name, number, operands, results, scratch):
    hbm = pl.BlockSpec(memory_space=pl.ANY)
    return pl.pallas_call(
        body,
        out_shape=[jax.ShapeDtypeStruct(shape, kind) for shape, kind in results],
        in_specs=[hbm] * len(operands),
        out_specs=[hbm] * len(results),
        scratch_shapes=scratch,
        compiler_params=pltpu.CompilerParams(collective_id=number, has_side_effects=True),
        name=name,
    )(*operands)


def gather_kernel(x, heads, dz, wide, out, x_to, heads_to, dz_to, wide_to, out_to, s1, s2, s3, s4, s5, s6):
    greet(ALL)
    spot = lax.axis_index("x")
    send_heads = Send(ALL, lambda p: heads.at[p // 16], lambda q: heads_to.at[q], s1)
    send_x = Send(CTX, lambda p: x, lambda q: x_to.at[q], s2)
    send_dz = Send(EP, lambda p: dz.at[p], lambda q: dz_to.at[q], s3)
    first = Send(
        ("yl", "z"),
        lambda p: wide.at[p],
        lambda q: wide_to.at[q // 4, spot, lax.rem(q, 4)],
        s4,
    )
    second = Send(("x",), lambda p: wide_to.at[:, spot], lambda q: wide_to.at[:, q], s5)
    send_out = Send(ALL, lambda p: out, lambda q: out_to.at[q], s6)
    first.start()
    send_heads.start()
    send_x.start()
    first.wait()
    second.start(own=False)
    send_dz.start()
    send_out.start()
    for send in (send_heads, send_x, send_dz, send_out):
        send.wait()
    second.wait(own=False)


def gather(x, heads, dz, wide, out):
    return move(
        gather_kernel,
        "gather",
        0,
        (x, heads, dz, wide, out),
        [
            ((8, ROWS, DIM), BF),
            ((128, 8, 384), BF),
            ((EXPERTS, CAP, DIM), BF),
            ((2, 4, 4, 32, 3 * FF), BF),
            ((128, 8, DIM), BF),
        ],
        [sems(128), sems(8), sems(32), sems(8), sems(4), sems(128)],
    )


def dispatch_kernel(rows, gates, rows_to, gates_to, s1, s2):
    greet(EP)
    sends = [
        Send(EP, lambda p: gates.at[p], lambda q: gates_to.at[q], s2),
        Send(EP, lambda p: rows.at[p], lambda q: rows_to.at[q], s1),
    ]
    for send in sends:
        send.start()
    for send in sends:
        send.wait()


def dispatch(rows, gates):
    return move(
        dispatch_kernel,
        "dispatch",
        1,
        (rows, gates),
        [(rows.shape, rows.dtype), (gates.shape, gates.dtype)],
        [sems(32), sems(32)],
    )


def give_back_kernel(y, da, grad, y_to, da_to, grad_to, s1, s2, s3):
    greet(("yl", "x", "yh", "co", "z"))
    sends = [
        Send(EP, lambda p: y.at[p], lambda q: y_to.at[q], s1),
        Send(("x",), lambda p: grad.at[:, p], lambda q: grad_to.at[q], s3),
        Send(EP, lambda p: da.at[p], lambda q: da_to.at[q], s2),
    ]
    for send in sends:
        send.start()
    for send in sends:
        send.wait()


def give_back(y, da, grad):
    return move(
        give_back_kernel,
        "give_back",
        2,
        (y, da, grad),
        [(y.shape, BF), (da.shape, BF), ((4, 2, 4, 32, 3 * FF), BF)],
        [sems(32), sems(32), sems(4)],
    )


def collect_kernel(da, heads, out, da_to, heads_to, out_to, s1, s2, s3):
    greet(ALL)
    sends = [
        Send(CTX, lambda p: da.at[p], lambda q: da_to.at[q], s1),
        Send(ALL, lambda p: heads.at[p], lambda q: heads_to.at[q], s2),
        Send(ALL, lambda p: out.at[p], lambda q: out_to.at[q], s3),
    ]
    for send in sends:
        send.start()
    for send in sends:
        send.wait()


def collect(da, heads, out):
    return move(
        collect_kernel,
        "collect",
        3,
        (da, heads, out),
        [(da.shape, BF), (heads.shape, BF), (out.shape, BF)],
        [sems(8), sems(128), sems(128)],
    )


def exchange(blocks, axes):
    return lax.all_to_all(blocks, axes, split_axis=0, concat_axis=0, tiled=True)


def dot(left, right, dims=((1,), (0,))):
    return lax.dot_general(left, right, (dims, ((), ())), preferred_element_type=F32)


def rms(v):
    return lax.rsqrt(jnp.mean(v * v, axis=-1, keepdims=True) + 1e-06)


def norm_back(v, scale, gain, upstream):
    weighted = upstream * gain
    inner = jnp.mean(weighted * v, axis=-1, keepdims=True)
    return scale * weighted - v * (scale * scale * scale) * inner, upstream * v * scale


def turn(v, cos, sin):
    a, b = v[..., : HEAD // 2], v[..., HEAD // 2 :]
    return jnp.concatenate([a * cos - b * sin, b * cos + a * sin], axis=-1)


def layout(tokens, lengths):
    ends = jnp.cumsum(lengths)
    passed = (tokens[:, None] >= ends[None, :]).astype(jnp.int32)
    return jnp.sum(passed, axis=1), tokens - jnp.sum(passed * lengths[None, :], axis=1)


def shards(
    inputs,
    cotangent,
    w_query,
    key_weight,
    value_weight,
    w_output,
    w_router,
    norm_gains,
    w_gate_up,
    w_down,
    seq_lengths,
    block_map,
    routes,
    priority,
):
    place = lax.axis_index("yl") * 4 + lax.axis_index("x")
    x_own = inputs[0]
    dz_low = cotangent[0]
    dz = dz_low.astype(F32)

    head_rows = jnp.concatenate(
        [
            w_query.reshape(8, 8, 128),
            key_weight.reshape(8, 8, 64),
            value_weight.reshape(8, 8, 64),
            jnp.broadcast_to(w_router[:, None], (8, 8, EXPERTS)),
            jnp.broadcast_to(
                jnp.pad(norm_gains[None, :], ((0, 7), (0, 96 - GAINS)))[:, None], (8, 8, 96)
            ),
        ],
        axis=-1,
    ).transpose(1, 0, 2)
    picks = jnp.concatenate([routes[0], priority[0, 0][:, None]], axis=1)
    picks = exchange(jnp.broadcast_to(picks[None], (8, ROWS, TOPK + 1)), CTX)
    mine = (block_map[0] == place).astype(jnp.int32)
    picks = jnp.sum(picks * mine[:, None, None], axis=0)
    route, order = picks[:, :TOPK], picks[:, TOPK]
    named = jnp.any(route[:, :, None] == jnp.arange(EXPERTS, dtype=jnp.int32), axis=1)
    before = (order[None, :] < order[:, None]).astype(BF)
    rank = dot(before, named.astype(BF)).astype(jnp.int32)
    slots = named.T[:, None, :] & (
        rank.T[:, None, :] == jnp.arange(CAP, dtype=jnp.int32)[None, :, None]
    )
    spread = slots.astype(BF).reshape(EXPERTS * CAP, ROWS)

    expert_rows = jnp.concatenate([w_gate_up, jnp.swapaxes(w_down, 1, 2)], axis=-1)
    x_all, head_rows, dz_slots, expert_rows, w_out = gather(
        x_own,
        head_rows,
        dot(spread, dz_low).astype(BF).reshape(EXPERTS, CAP, DIM),
        expert_rows,
        w_output.T,
    )
    x_all = x_all.reshape(GTOK, DIM)
    dz_slots = dz_slots.reshape(EXPERTS * CAP, DIM)
    expert_rows = expert_rows.reshape(DIM, 3 * FF)
    w_gu, w_dn = expert_rows[:, : 2 * FF], expert_rows[:, 2 * FF :]
    w_out = w_out.reshape(DIM, HEADS * HEAD)
    w_heads = head_rows[:, :, :256].reshape(DIM, 256)
    router = head_rows[:, :, 256:288].reshape(DIM, EXPERTS)
    gains = head_rows[:, 0, 288 : 288 + GAINS].reshape(128 * GAINS).astype(F32)
    gain_one, gain_two = gains[:DIM], gains[DIM : 2 * DIM]
    gain_q, gain_k = gains[2 * DIM : 2 * DIM + HEAD], gains[2 * DIM + HEAD :]

    x_all = x_all.astype(F32)
    scale_all = rms(x_all)
    a_all = (x_all * scale_all * gain_one).astype(BF)
    qkv = dot(a_all, w_heads)
    q0, k0 = qkv[:, :128].reshape(GTOK, 2, HEAD), qkv[:, 128:192]
    v = qkv[:, 192:].astype(BF)
    tokens = jnp.arange(GTOK, dtype=jnp.int32)
    sequence, position = layout(tokens, seq_lengths[0])
    frequency = jnp.exp(
        jnp.arange(HEAD // 2, dtype=F32) * (-2.0 * math.log(10000.0) / HEAD)
    )
    angles = position.astype(F32)[:, None] * frequency[None, :]
    cos, sin = jnp.cos(angles), jnp.sin(angles)
    rq, rk = rms(q0), rms(k0)
    qr = turn(q0 * rq * gain_q, cos[:, None], sin[:, None]).astype(BF)
    kr = turn(k0 * rk * gain_k, cos, sin).astype(BF)
    allowed = (sequence[:, None] == sequence[None, :]) & (tokens[None, :] <= tokens[:, None])
    scores = jnp.einsum("thd,ud->htu", qr, kr, preferred_element_type=F32) * HEAD**-0.5
    probs_at = jax.nn.softmax(jnp.where(allowed[None], scores, -1e30), axis=-1)
    probs_low = probs_at.astype(BF)
    mixed = jnp.einsum("htu,ud->thd", probs_low, v, preferred_element_type=F32)
    mixed_low = mixed.astype(BF).reshape(8, ROWS, 128)
    ob = exchange(mixed_low, CTX).transpose(1, 0, 2).reshape(ROWS, HEADS * HEAD)

    x_f32 = x_own.astype(F32)
    x1 = x_f32 + dot(ob, w_out, ((1,), (1,)))
    r2 = rms(x1)
    a2 = (x1 * r2 * gain_two).astype(BF)
    probs = jax.nn.softmax(dot(a2, router), axis=-1)
    chosen = jnp.where(named, probs, 0.0)
    total = jnp.sum(chosen, axis=1, keepdims=True)
    gate = chosen / total

    slot_gate = jnp.sum(jnp.where(slots, gate.T[:, None, :], 0.0), axis=2)
    a2_slots, slot_gate = dispatch(
        dot(spread, a2).astype(BF).reshape(EXPERTS, CAP, DIM),
        jnp.pad(slot_gate, ((0, 0), (0, 128 - CAP)))[:, None],
    )
    a2_slots = a2_slots.reshape(EXPERTS * CAP, DIM)
    slot_gate = slot_gate[:, 0, :CAP].reshape(EXPERTS * CAP, 1)
    gu = dot(a2_slots, w_gu)
    g, up = gu[:, :FF], gu[:, FF:]
    s = jax.nn.sigmoid(g)
    hid = (g * s * up).astype(BF)
    y = dot(hid, w_dn, ((1,), (1,))).astype(BF)
    dy = (slot_gate * dz_slots.astype(F32)).astype(BF)
    dhid = dot(dy, w_dn)
    dgu = jnp.concatenate([dhid * up * s * (1.0 + g * (1.0 - s)), dhid * g * s], axis=-1)
    dgu = dgu.astype(BF)
    da = dot(dgu, w_gu, ((1,), (1,))).astype(BF)
    expert_grad = jnp.concatenate(
        [dot(a2_slots, dgu, ((0,), (0,))), dot(dy, hid, ((0,), (0,)))], axis=-1
    ).astype(BF)
    y, da, expert_grad = give_back(
        y.reshape(EXPERTS, CAP, DIM),
        da.reshape(EXPERTS, CAP, DIM),
        expert_grad.reshape(2, 4, 4, 32, 3 * FF),
    )
    y = y.reshape(EXPERTS * CAP, DIM)
    da = da.reshape(EXPERTS * CAP, DIM)
    expert_grad = jnp.sum(expert_grad.astype(F32), axis=0).astype(BF).reshape(8, 32, 3 * FF)
    expert_grad = exchange(expert_grad, ("yl", "z")).astype(F32)
    grad_gate_up = expert_grad[..., : 2 * FF]
    grad_down = jnp.swapaxes(expert_grad[..., 2 * FF :], 1, 2)

    weigh = jnp.where(slots, gate.T[:, None, :], 0.0).reshape(EXPERTS * CAP, ROWS)
    weigh_high = weigh.astype(BF)
    weigh_low = (weigh - weigh_high.astype(F32)).astype(BF)
    mixture = dot(weigh_high, y, ((0,), (0,))) + dot(weigh_low, y, ((0,), (0,)))
    output = (x1 + mixture).astype(BF)
    pair = dot(y, dz_low, ((1,), (1,))).reshape(EXPERTS, CAP, ROWS)
    dgate = jnp.sum(jnp.where(slots, pair, 0.0), axis=1).T
    dc = jnp.where(named, dgate - jnp.sum(gate * dgate, axis=1, keepdims=True), 0.0) / total
    dl = (probs * (dc - jnp.sum(probs * dc, axis=-1, keepdims=True))).astype(BF)
    da2 = dot(spread, da, ((0,), (0,))) + dot(dl, router, ((1,), (1,)))
    grad_router = dot(a2, dl, ((0,), (0,)))
    dx_two, gain_two_terms = norm_back(x1, r2, gain_two, da2)
    dx1 = dz + dx_two
    db = dx1.astype(BF)

    do_rows = dot(db, w_out).astype(BF)
    do_rows = exchange(do_rows.reshape(ROWS, 8, 128).transpose(1, 0, 2), CTX)
    do_rows = do_rows.reshape(GTOK, 2, HEAD)
    dv = jnp.einsum("htu,thd->ud", probs_low, do_rows, preferred_element_type=F32)
    dp = jnp.einsum("thd,ud->htu", do_rows, v, preferred_element_type=F32)
    delta = jnp.sum(do_rows.astype(F32) * mixed, axis=-1).T
    ds = (probs_at * (dp - delta[..., None])).astype(BF)
    dqr = jnp.einsum("htu,ud->thd", ds, kr, preferred_element_type=F32) * HEAD**-0.5
    dkr = jnp.einsum("htu,thd->ud", ds, qr, preferred_element_type=F32) * HEAD**-0.5
    dq0, gain_q_terms = norm_back(q0, rq, gain_q, turn(dqr, cos[:, None], -sin[:, None]))
    dk0, gain_k_terms = norm_back(k0, rk, gain_k, turn(dkr, cos, -sin))
    dqkv = jnp.concatenate([dq0.reshape(GTOK, 128), dk0, dv], axis=-1).astype(BF)
    da1 = dot(dqkv, w_heads, ((1,), (1,)))
    gain_one_grad = jnp.sum(da1 * x_all * scale_all, axis=0)
    grad_gains = jnp.concatenate(
        [
            gain_one_grad,
            jnp.sum(gain_two_terms, axis=0),
            jnp.sum(gain_q_terms, axis=(0, 1)),
            jnp.sum(gain_k_terms, axis=0),
        ]
    )
    head_grad = jnp.concatenate(
        [
            dot(a_all, dqkv, ((0,), (0,))).reshape(128, 8, 256),
            grad_router.reshape(128, 8, EXPERTS),
            jnp.pad(grad_gains.reshape(128, 1, GAINS), ((0, 0), (0, 7), (0, 96 - GAINS))),
        ],
        axis=-1,
    ).astype(BF)
    da1, head_grad, out_grad = collect(
        da1.astype(BF).reshape(8, ROWS, DIM),
        head_grad,
        dot(db, ob, ((0,), (0,))).astype(BF).reshape(128, 8, HEADS * HEAD),
    )
    da1 = jnp.sum(da1.astype(F32), axis=0)
    dx_one, _ = norm_back(x_f32, rms(x_f32), gain_one, da1)
    grad_inputs = (dx1 + dx_one).astype(BF)
    grad_w_output = jnp.sum(out_grad.astype(F32), axis=0).T
    head_grad = jnp.sum(head_grad.astype(F32).reshape(8, 16, 8, 384), axis=1)
    rows = jnp.swapaxes(head_grad, 0, 1)
    shared = jnp.sum(head_grad, axis=0)
    return (
        output[None],
        grad_inputs[None],
        rows[..., :128].reshape(8, HEADS * HEAD),
        rows[..., 128:192].reshape(8, KV_HEADS * HEAD),
        rows[..., 192:256].reshape(8, KV_HEADS * HEAD),
        grad_w_output,
        shared[:, 256:288],
        shared[0, 288 : 288 + GAINS],
        grad_gate_up,
        grad_down,
    )


def solution(mesh):
    groups = ("yh", "co", "z")
    specs = (
        P(groups, CTX, None),
        P(groups, CTX, None),
        P(ALL, None),
        P(ALL, None),
        P(ALL, None),
        P(None, ALL),
        P(ALL, None),
        P(ALL),
        P(("yh", "co"), WT, None),
        P(("yh", "co"), None, WT),
        P(groups, None),
        P(groups, None),
        P(groups, CTX, None),
        P(groups, CTX, None),
    )
    return jax.shard_map(
        shards,
        mesh=Mesh(mesh.devices.reshape(SIZES), ALL),
        in_specs=specs,
        out_specs=specs[:10],
        check_vma=False,
    )
```

```python
import math

import jax
import jax.numpy as jnp
from jax import lax
from jax.experimental import pallas as pl
from jax.experimental.pallas import tpu as pltpu
from jax.sharding import Mesh
from jax.sharding import PartitionSpec as P

HEADS = 16
KV_HEADS = 8
DIM = 1024
HEAD = 64
FF = 512
EXPERTS = 32
TOPK = 8
ROWS = 128
GTOK = 1024
CAP = 40
GAINS = 17
BF = jnp.bfloat16
F32 = jnp.float32

ALL = ("yl", "x", "yh", "co", "z")
SIZES = (2, 4, 2, 2, 4)
CTX = ("yl", "x")
EP = ("yh", "co", "yl", "z")
WT = ("yl", "x", "z")


SPAN = dict(zip(ALL, SIZES))


def linear(axes):
    index = 0
    for axis in axes:
        index = index * SPAN[axis] + lax.axis_index(axis)
    return index


def device(axes, index):
    at = {}
    for axis in reversed(axes):
        at[axis] = lax.rem(index, SPAN[axis])
        index = index // SPAN[axis]
    return tuple(at[axis] if axis in at else lax.axis_index(axis) for axis in ALL)


def greet(axes):
    n = math.prod(SPAN[axis] for axis in axes)
    me = linear(axes)
    barrier = pltpu.get_barrier_semaphore()

    def signal(i, carry):
        pl.semaphore_signal(
            barrier,
            inc=1,
            device_id=device(axes, lax.rem(me + i, n)),
            device_id_type=pl.DeviceIdType.MESH,
        )
        return carry

    lax.fori_loop(1, n, signal, 0)
    pl.semaphore_wait(barrier, n - 1)


class Send:
    def __init__(self, axes, part, slot, sems):
        self.axes, self.part, self.slot, self.sems = axes, part, slot, sems
        self.n = math.prod(SPAN[axis] for axis in axes)
        self.me = linear(axes)

    def copy(self, i):
        to = lax.rem(self.me + i, self.n)
        return pltpu.make_async_remote_copy(
            src_ref=self.part(to),
            dst_ref=self.slot(self.me),
            send_sem=self.sems.at[0, i],
            recv_sem=self.sems.at[1, i],
            device_id=device(self.axes, to),
            device_id_type=pl.DeviceIdType.MESH,
        )

    def own(self):
        return pltpu.make_async_copy(self.part(self.me), self.slot(self.me), self.sems.at[0, 0])

    def start(self, own=True):
        def one(i, carry):
            self.copy(i).start()
            return carry

        if own:
            self.own().start()
        lax.fori_loop(1, self.n, one, 0)

    def wait(self, own=True):
        def one(i, carry):
            self.copy(i).wait()
            return carry

        if own:
            self.own().wait()
        lax.fori_loop(1, self.n, one, 0)


def sems(n):
    return pltpu.SemaphoreType.DMA((2, n))


def move(body, name, number, operands, results, scratch):
    hbm = pl.BlockSpec(memory_space=pl.ANY)
    return pl.pallas_call(
        body,
        out_shape=[jax.ShapeDtypeStruct(shape, kind) for shape, kind in results],
        in_specs=[hbm] * len(operands),
        out_specs=[hbm] * len(results),
        scratch_shapes=scratch,
        compiler_params=pltpu.CompilerParams(collective_id=number, has_side_effects=True),
        name=name,
    )(*operands)


def halves():
    lane = lax.broadcasted_iota(jnp.int32, (1, 128), 1)
    return lane < HEAD, lax.rem(lane, HEAD) < HEAD // 2


def head_rms(v, first):
    square = v * v
    low = jnp.sum(jnp.where(first, square, 0.0), axis=1, keepdims=True)
    high = jnp.sum(jnp.where(first, 0.0, square), axis=1, keepdims=True)
    return lax.rsqrt(jnp.where(first, low, high) * (1.0 / HEAD) + 1e-06)


def turn_pair(v, cos, sin, front):
    return v * cos + jnp.where(front, -pltpu.roll(v, 96, 1), pltpu.roll(v, 32, 1)) * sin


def starts(tokens, ends):
    first = jnp.zeros_like(tokens)
    for end in ends:
        first = jnp.maximum(first, jnp.where(tokens >= end, end, 0))
    return first


def sequence_ends(lengths):
    ends, total = [], 0
    for i in range(3):
        total = total + lengths[i]
        ends.append(total)
    return ends


def spread_gains(packed):
    column = lax.broadcasted_iota(jnp.int32, (128, 128 * GAINS), 1)
    owner = (column * 3856) >> 16
    picked = lax.broadcasted_iota(jnp.int32, (128, 128 * GAINS), 0) == owner
    rows = dot(packed, picked.astype(F32).astype(BF), ((0,), (0,)))
    wanted = EXPERTS + column - owner * GAINS
    row = lax.broadcasted_iota(jnp.int32, (128, 128 * GAINS), 0)
    return jnp.sum(jnp.where(row == wanted, rows, 0.0), axis=0, keepdims=True)


def gather_kernel(
    lengths,
    blocks,
    x,
    heads,
    picks,
    dz,
    wide,
    out,
    a_all,
    x_to,
    heads_to,
    pre,
    qr,
    kr,
    vv,
    mixed,
    log_sum,
    gains,
    ranks,
    o_to,
    dz_to,
    wide_to,
    out_to,
    picks_to,
    hot,
    dz_slots,
    weights,
    o_rows,
    s_picks,
    s_x,
    s_heads,
    s_heads_core,
    s_dz,
    s_wide,
    s_wide_x,
    s_out,
    s_out_z,
    s_out_core,
    s_o,
):
    greet(ALL)
    place = linear(CTX)
    spot, core, deep = lax.axis_index("x"), lax.axis_index("co"), lax.axis_index("z")
    chips = ("yl", "x", "yh", "z")
    send_picks = Send(CTX, lambda p: picks, lambda q: picks_to.at[q], s_picks)
    send_x = Send(CTX, lambda p: x, lambda q: x_to.at[q], s_x)
    send_heads = Send(
        chips,
        lambda p: heads.at[p // 8],
        lambda q: heads_to.at[q // 4, core, lax.rem(q, 4)],
        s_heads,
    )
    swap_heads = Send(
        ("co",), lambda p: heads_to.at[:, core], lambda q: heads_to.at[:, q], s_heads_core
    )
    send_dz = Send(EP, lambda p: dz_slots.at[p], lambda q: dz_to.at[q], s_dz)
    send_wide = Send(
        ("yl", "z"),
        lambda p: wide.at[p],
        lambda q: wide_to.at[q // 4, spot, lax.rem(q, 4)],
        s_wide,
    )
    pass_wide = Send(("x",), lambda p: wide_to.at[:, spot], lambda q: wide_to.at[:, q], s_wide_x)
    send_out = Send(
        ("yl", "x", "yh"), lambda p: out, lambda q: out_to.at[q, core, deep], s_out
    )
    pass_out = Send(
        ("z",), lambda p: out_to.at[:, core, deep], lambda q: out_to.at[:, core, q], s_out_z
    )
    swap_out = Send(
        ("co",), lambda p: out_to.at[:, core], lambda q: out_to.at[:, q], s_out_core
    )
    send_o = Send(CTX, lambda p: o_rows.at[p], lambda q: o_to.at[q], s_o)

    send_picks.start()
    send_x.start()
    send_wide.start()
    send_heads.start()
    send_out.start()

    send_picks.wait()
    mine = jnp.zeros((16, 128), jnp.int32)
    for p in range(8):
        mine = mine + picks_to[p] * (blocks[p] == place).astype(jnp.int32)
    expert = lax.broadcasted_iota(jnp.int32, (EXPERTS, ROWS), 0)
    named = jnp.zeros((EXPERTS, ROWS), jnp.bool_)
    for k in range(TOPK):
        named = named | (mine[k : k + 1] == expert)
    order = jnp.broadcast_to(mine[TOPK : TOPK + 1].astype(F32), (128, ROWS))
    before = (order.T < order).astype(F32).astype(BF)
    rank = dot(named.astype(F32).astype(BF), before).astype(jnp.int32)
    rank = jnp.where(named, rank, -1)
    ranks[...] = rank
    ranks_f = rank.astype(F32)
    seat = lax.broadcasted_iota(jnp.int32, (CAP, ROWS), 0).astype(F32)
    for e in range(EXPERTS):
        hot[pl.ds(e * CAP, CAP)] = (ranks_f[e : e + 1] == seat).astype(F32)

    def fill(i, carry):
        rows = hot[pl.ds(pl.multiple_of(i * 160, 160), 160)].astype(BF)
        dz_slots[pl.ds(i * 4, 4)] = dot(rows, dz[...]).reshape(4, CAP, DIM).astype(BF)
        return carry

    lax.fori_loop(0, 8, fill, 0)
    send_dz.start()
    send_wide.wait()
    pass_wide.start(own=False)
    send_heads.wait()
    swap_heads.start(own=False)
    send_out.wait()
    pass_out.start(own=False)
    swap_heads.wait(own=False)

    packed = heads_to[...].astype(F32).reshape(128, 8, 384)
    weights[...] = packed[:, :, :256].reshape(DIM, 256).astype(BF)
    row = spread_gains(packed[:, 0, 256:384].astype(BF))
    gains[...] = row
    gain_one = row[:, :DIM]
    first, front = halves()
    pair = row[:, 2 * DIM :]
    swapped = pltpu.roll(pair, HEAD, 1)
    gain_q, gain_k = jnp.where(first, pair, swapped), jnp.where(first, swapped, pair)
    ends = sequence_ends(lengths)
    lane = lax.broadcasted_iota(jnp.int32, (1, 128), 1)
    frequency = jnp.exp(
        lax.rem(lane, HEAD // 2).astype(F32) * (-2.0 * math.log(10000.0) / HEAD)
    )

    def project(j):
        v = x_to[j].astype(F32)
        low = (v * rms(v) * gain_one).astype(BF)
        at = pl.ds(pl.multiple_of(j * ROWS, ROWS), ROWS)
        a_all[at] = low
        qkv = dot(low, weights[...])
        pre[at] = qkv
        token = j * ROWS + lax.broadcasted_iota(jnp.int32, (ROWS, 1), 0)
        angle = (token - starts(token, ends)).astype(F32) * frequency
        cos, sin = jnp.cos(angle), jnp.sin(angle)
        q, kv = qkv[:, :128], qkv[:, 128:]
        other = pltpu.roll(kv, HEAD, 1)
        k, val = jnp.where(first, kv, other), jnp.where(first, other, kv)
        qr[at] = turn_pair(q * head_rms(q, first) * gain_q, cos, sin, front).astype(BF)
        kr[at] = turn_pair(k * head_rms(k, first) * gain_k, cos, sin, front).astype(BF)
        vv[at] = val.astype(BF)

    send_x.own().wait()
    project(place)

    def arrive(i, carry):
        send_x.copy(i).wait()
        project(lax.rem(place - i + 8, 8))
        return carry

    lax.fori_loop(1, 8, arrive, 0)

    for tile in range(4):
        wide_keys = 256 * (tile + 1)
        q = qr[pl.ds(tile * 256, 256)].astype(F32)
        q = jnp.concatenate([jnp.where(first, q, 0.0), jnp.where(first, 0.0, q)], axis=0)
        keys = pl.ds(0, wide_keys)
        scores = dot(q.astype(BF), kr[keys], ((1,), (1,))) * HEAD**-0.5
        token = tile * 256 + lax.rem(lax.broadcasted_iota(jnp.int32, (512, 1), 0), 256)
        key = lax.broadcasted_iota(jnp.int32, (512, wide_keys), 1)
        scores = jnp.where((key <= token) & (key >= starts(token, ends)), scores, -1e30)
        top = jnp.max(scores, axis=1, keepdims=True)
        weight = jnp.exp(scores - top)
        total = jnp.sum(weight, axis=1, keepdims=True)
        both = dot((weight * (1.0 / total)).astype(BF), vv[keys])
        result = jnp.where(first, both[:256], both[256:])
        mixed[pl.ds(tile * 256, 256)] = result
        o_rows[pl.ds(2 * tile, 2)] = result.astype(BF).reshape(2, ROWS, 128)
        level = jnp.broadcast_to(top + jnp.log(total), (512, 128))
        log_sum[pl.ds(tile * 256, 256)] = jnp.where(first, level[:256], level[256:])
    send_o.start()
    pass_out.wait(own=False)
    swap_out.start(own=False)
    send_o.wait()
    swap_out.wait(own=False)
    send_dz.wait()
    pass_wide.wait(own=False)


def gather(lengths, blocks, x, heads, picks, dz, wide, out):
    smem, vmem, hbm = (
        pl.BlockSpec(memory_space=space) for space in (pltpu.SMEM, pltpu.VMEM, pl.ANY)
    )
    results = [
        ((GTOK, DIM), BF, vmem),
        ((8, ROWS, DIM), BF, vmem),
        ((16, 2, 4, 8, 384), BF, vmem),
        ((GTOK, 256), F32, vmem),
        ((GTOK, 128), BF, vmem),
        ((GTOK, 128), BF, vmem),
        ((GTOK, 128), BF, vmem),
        ((GTOK, 128), F32, vmem),
        ((GTOK, 128), F32, vmem),
        ((1, 128 * GAINS), F32, vmem),
        ((EXPERTS, ROWS), jnp.int32, vmem),
        ((8, ROWS, 128), BF, vmem),
        ((EXPERTS, CAP, DIM), BF, hbm),
        ((2, 4, 4, 32, 3 * FF), BF, hbm),
        ((16, 2, 4, 8, DIM), BF, hbm),
    ]
    return pl.pallas_call(
        gather_kernel,
        out_shape=[jax.ShapeDtypeStruct(shape, kind) for shape, kind, _ in results],
        in_specs=[smem, smem, vmem, vmem, vmem, vmem, hbm, vmem],
        out_specs=[space for _, _, space in results],
        scratch_shapes=[
            pltpu.VMEM((8, 16, 128), jnp.int32),
            pltpu.VMEM((EXPERTS * CAP, ROWS), F32),
            pltpu.VMEM((EXPERTS, CAP, DIM), BF),
            pltpu.VMEM((DIM, 256), BF),
            pltpu.VMEM((8, ROWS, 128), BF),
            sems(8),
            sems(8),
            sems(64),
            sems(2),
            sems(32),
            sems(8),
            sems(4),
            sems(16),
            sems(4),
            sems(2),
            sems(8),
        ],
        compiler_params=pltpu.CompilerParams(
            collective_id=0, has_side_effects=True, vmem_limit_bytes=56 << 20
        ),
        name="gather",
    )(lengths, blocks, x, heads, picks, dz, wide, out)


def dispatch_kernel(rows, gates, rows_to, gates_to, s1, s2):
    greet(EP)
    sends = [
        Send(EP, lambda p: gates.at[p], lambda q: gates_to.at[q], s2),
        Send(EP, lambda p: rows.at[p], lambda q: rows_to.at[q], s1),
    ]
    for send in sends:
        send.start()
    for send in sends:
        send.wait()


def dispatch(rows, gates):
    return move(
        dispatch_kernel,
        "dispatch",
        1,
        (rows, gates),
        [(rows.shape, rows.dtype), (gates.shape, gates.dtype)],
        [sems(32), sems(32)],
    )


def give_back_kernel(y, da, grad, y_to, da_to, grad_to, s1, s2, s3):
    greet(("yl", "x", "yh", "co", "z"))
    sends = [
        Send(EP, lambda p: y.at[p], lambda q: y_to.at[q], s1),
        Send(("x",), lambda p: grad.at[:, p], lambda q: grad_to.at[q], s3),
        Send(EP, lambda p: da.at[p], lambda q: da_to.at[q], s2),
    ]
    for send in sends:
        send.start()
    for send in sends:
        send.wait()


def give_back(y, da, grad):
    return move(
        give_back_kernel,
        "give_back",
        2,
        (y, da, grad),
        [(y.shape, BF), (da.shape, BF), ((4, 2, 4, 32, 3 * FF), BF)],
        [sems(32), sems(32), sems(4)],
    )


def collect_kernel(da, heads, out, da_to, heads_to, out_to, s1, s2, s3):
    greet(ALL)
    sends = [
        Send(CTX, lambda p: da.at[p], lambda q: da_to.at[q], s1),
        Send(ALL, lambda p: heads.at[p], lambda q: heads_to.at[q], s2),
        Send(ALL, lambda p: out.at[p], lambda q: out_to.at[q], s3),
    ]
    for send in sends:
        send.start()
    for send in sends:
        send.wait()


def collect(da, heads, out):
    return move(
        collect_kernel,
        "collect",
        3,
        (da, heads, out),
        [(da.shape, BF), (heads.shape, BF), (out.shape, BF)],
        [sems(8), sems(128), sems(128)],
    )


def exchange(blocks, axes):
    return lax.all_to_all(blocks, axes, split_axis=0, concat_axis=0, tiled=True)


def dot(left, right, dims=((1,), (0,))):
    return lax.dot_general(left, right, (dims, ((), ())), preferred_element_type=F32)


def rms(v):
    return lax.rsqrt(jnp.mean(v * v, axis=-1, keepdims=True) + 1e-06)


def norm_back(v, scale, gain, upstream):
    weighted = upstream * gain
    inner = jnp.mean(weighted * v, axis=-1, keepdims=True)
    return scale * weighted - v * (scale * scale * scale) * inner, upstream * v * scale


def turn(v, cos, sin):
    a, b = v[..., : HEAD // 2], v[..., HEAD // 2 :]
    return jnp.concatenate([a * cos - b * sin, b * cos + a * sin], axis=-1)


def layout(tokens, lengths):
    ends = jnp.cumsum(lengths)
    passed = (tokens[:, None] >= ends[None, :]).astype(jnp.int32)
    return jnp.sum(passed, axis=1), tokens - jnp.sum(passed * lengths[None, :], axis=1)


def shards(
    inputs,
    cotangent,
    w_query,
    key_weight,
    value_weight,
    w_output,
    w_router,
    norm_gains,
    w_gate_up,
    w_down,
    seq_lengths,
    block_map,
    routes,
    priority,
):
    x_own = inputs[0]
    dz_low = cotangent[0]
    dz = dz_low.astype(F32)

    head_rows = jnp.concatenate(
        [
            w_query.reshape(8, 8, 128),
            key_weight.reshape(8, 8, 64),
            value_weight.reshape(8, 8, 64),
            jnp.broadcast_to(w_router[:, None], (8, 8, EXPERTS)),
            jnp.broadcast_to(
                jnp.pad(norm_gains[None, :], ((0, 7), (0, 96 - GAINS)))[:, None], (8, 8, 96)
            ),
        ],
        axis=-1,
    ).transpose(1, 0, 2)
    picks = jnp.concatenate(
        [routes[0].T, priority[0], jnp.zeros((16 - TOPK - 1, ROWS), jnp.int32)], axis=0
    )
    expert_rows = jnp.concatenate([w_gate_up, jnp.swapaxes(w_down, 1, 2)], axis=-1)
    (
        a_all,
        x_all,
        head_rows,
        pre,
        qr,
        kr,
        v,
        mixed,
        log_sum,
        gains,
        ranks,
        ob,
        dz_slots,
        expert_rows,
        w_out,
    ) = gather(
        seq_lengths[0], block_map[0], x_own, head_rows, picks, dz_low, expert_rows, w_output.T
    )
    head_rows = head_rows.reshape(128, 8, 384)
    w_heads = head_rows[:, :, :256].reshape(DIM, 256)
    router = head_rows[:, :, 256:288].reshape(DIM, EXPERTS)
    gains = gains[0]
    gain_one, gain_two = gains[:DIM], gains[DIM : 2 * DIM]
    gain_q, gain_k = gains[2 * DIM : 2 * DIM + HEAD], gains[2 * DIM + HEAD :]
    dz_slots = dz_slots.reshape(EXPERTS * CAP, DIM)
    expert_rows = expert_rows.reshape(DIM, 3 * FF)
    w_gu, w_dn = expert_rows[:, : 2 * FF], expert_rows[:, 2 * FF :]
    w_out = w_out.reshape(DIM, HEADS * HEAD)
    named = (ranks >= 0).T
    slots = ranks[:, None, :] == jnp.arange(CAP, dtype=jnp.int32)[None, :, None]
    spread = slots.astype(BF).reshape(EXPERTS * CAP, ROWS)
    x_all = x_all.reshape(GTOK, DIM).astype(F32)
    scale_all = rms(x_all)
    q0, k0 = pre[:, :128].reshape(GTOK, 2, HEAD), pre[:, 128:192]
    rq, rk = rms(q0), rms(k0)
    qr, kr, v = qr.reshape(GTOK, 2, HEAD), kr[:, :HEAD], v[:, :HEAD]
    mixed = mixed.reshape(GTOK, 2, HEAD)
    tokens = jnp.arange(GTOK, dtype=jnp.int32)
    sequence, position = layout(tokens, seq_lengths[0])
    frequency = jnp.exp(
        jnp.arange(HEAD // 2, dtype=F32) * (-2.0 * math.log(10000.0) / HEAD)
    )
    angles = position.astype(F32)[:, None] * frequency[None, :]
    cos, sin = jnp.cos(angles), jnp.sin(angles)
    allowed = (sequence[:, None] == sequence[None, :]) & (tokens[None, :] <= tokens[:, None])
    ob = ob.transpose(1, 0, 2).reshape(ROWS, HEADS * HEAD)

    x_f32 = x_own.astype(F32)
    x1 = x_f32 + dot(ob, w_out, ((1,), (1,)))
    r2 = rms(x1)
    a2 = (x1 * r2 * gain_two).astype(BF)
    probs = jax.nn.softmax(dot(a2, router), axis=-1)
    chosen = jnp.where(named, probs, 0.0)
    total = jnp.sum(chosen, axis=1, keepdims=True)
    gate = chosen / total

    slot_gate = jnp.sum(jnp.where(slots, gate.T[:, None, :], 0.0), axis=2)
    a2_slots, slot_gate = dispatch(
        dot(spread, a2).astype(BF).reshape(EXPERTS, CAP, DIM),
        jnp.pad(slot_gate, ((0, 0), (0, 128 - CAP)))[:, None],
    )
    a2_slots = a2_slots.reshape(EXPERTS * CAP, DIM)
    slot_gate = slot_gate[:, 0, :CAP].reshape(EXPERTS * CAP, 1)
    gu = dot(a2_slots, w_gu)
    g, up = gu[:, :FF], gu[:, FF:]
    s = jax.nn.sigmoid(g)
    hid = (g * s * up).astype(BF)
    y = dot(hid, w_dn, ((1,), (1,))).astype(BF)
    dy = (slot_gate * dz_slots.astype(F32)).astype(BF)
    dhid = dot(dy, w_dn)
    dgu = jnp.concatenate([dhid * up * s * (1.0 + g * (1.0 - s)), dhid * g * s], axis=-1)
    dgu = dgu.astype(BF)
    da = dot(dgu, w_gu, ((1,), (1,))).astype(BF)
    expert_grad = jnp.concatenate(
        [dot(a2_slots, dgu, ((0,), (0,))), dot(dy, hid, ((0,), (0,)))], axis=-1
    ).astype(BF)
    y, da, expert_grad = give_back(
        y.reshape(EXPERTS, CAP, DIM),
        da.reshape(EXPERTS, CAP, DIM),
        expert_grad.reshape(2, 4, 4, 32, 3 * FF),
    )
    y = y.reshape(EXPERTS * CAP, DIM)
    da = da.reshape(EXPERTS * CAP, DIM)
    expert_grad = jnp.sum(expert_grad.astype(F32), axis=0).astype(BF).reshape(8, 32, 3 * FF)
    expert_grad = exchange(expert_grad, ("yl", "z")).astype(F32)
    grad_gate_up = expert_grad[..., : 2 * FF]
    grad_down = jnp.swapaxes(expert_grad[..., 2 * FF :], 1, 2)

    weigh = jnp.where(slots, gate.T[:, None, :], 0.0).reshape(EXPERTS * CAP, ROWS)
    weigh_high = weigh.astype(BF)
    weigh_low = (weigh - weigh_high.astype(F32)).astype(BF)
    mixture = dot(weigh_high, y, ((0,), (0,))) + dot(weigh_low, y, ((0,), (0,)))
    output = (x1 + mixture).astype(BF)
    pair = dot(y, dz_low, ((1,), (1,))).reshape(EXPERTS, CAP, ROWS)
    dgate = jnp.sum(jnp.where(slots, pair, 0.0), axis=1).T
    dc = jnp.where(named, dgate - jnp.sum(gate * dgate, axis=1, keepdims=True), 0.0) / total
    dl = (probs * (dc - jnp.sum(probs * dc, axis=-1, keepdims=True))).astype(BF)
    da2 = dot(spread, da, ((0,), (0,))) + dot(dl, router, ((1,), (1,)))
    grad_router = dot(a2, dl, ((0,), (0,)))
    dx_two, gain_two_terms = norm_back(x1, r2, gain_two, da2)
    dx1 = dz + dx_two
    db = dx1.astype(BF)

    do_rows = dot(db, w_out).astype(BF)
    do_rows = exchange(do_rows.reshape(ROWS, 8, 128).transpose(1, 0, 2), CTX)
    do_rows = do_rows.reshape(GTOK, 2, HEAD)
    scores = jnp.einsum("thd,ud->htu", qr, kr, preferred_element_type=F32) * HEAD**-0.5
    level = log_sum.reshape(GTOK, 2, HEAD)[:, :, 0].T
    probs_at = jnp.where(allowed[None], jnp.exp(scores - level[..., None]), 0.0)
    probs_low = probs_at.astype(BF)
    dv = jnp.einsum("htu,thd->ud", probs_low, do_rows, preferred_element_type=F32)
    dp = jnp.einsum("thd,ud->htu", do_rows, v, preferred_element_type=F32)
    delta = jnp.sum(do_rows.astype(F32) * mixed, axis=-1).T
    ds = (probs_at * (dp - delta[..., None])).astype(BF)
    dqr = jnp.einsum("htu,ud->thd", ds, kr, preferred_element_type=F32) * HEAD**-0.5
    dkr = jnp.einsum("htu,thd->ud", ds, qr, preferred_element_type=F32) * HEAD**-0.5
    dq0, gain_q_terms = norm_back(q0, rq, gain_q, turn(dqr, cos[:, None], -sin[:, None]))
    dk0, gain_k_terms = norm_back(k0, rk, gain_k, turn(dkr, cos, -sin))
    dqkv = jnp.concatenate([dq0.reshape(GTOK, 128), dk0, dv], axis=-1).astype(BF)
    da1 = dot(dqkv, w_heads, ((1,), (1,)))
    gain_one_grad = jnp.sum(da1 * x_all * scale_all, axis=0)
    grad_gains = jnp.concatenate(
        [
            gain_one_grad,
            jnp.sum(gain_two_terms, axis=0),
            jnp.sum(gain_q_terms, axis=(0, 1)),
            jnp.sum(gain_k_terms, axis=0),
        ]
    )
    head_grad = jnp.concatenate(
        [
            dot(a_all, dqkv, ((0,), (0,))).reshape(128, 8, 256),
            grad_router.reshape(128, 8, EXPERTS),
            jnp.pad(grad_gains.reshape(128, 1, GAINS), ((0, 0), (0, 7), (0, 96 - GAINS))),
        ],
        axis=-1,
    ).astype(BF)
    da1, head_grad, out_grad = collect(
        da1.astype(BF).reshape(8, ROWS, DIM),
        head_grad,
        dot(db, ob, ((0,), (0,))).astype(BF).reshape(128, 8, HEADS * HEAD),
    )
    da1 = jnp.sum(da1.astype(F32), axis=0)
    dx_one, _ = norm_back(x_f32, rms(x_f32), gain_one, da1)
    grad_inputs = (dx1 + dx_one).astype(BF)
    grad_w_output = jnp.sum(out_grad.astype(F32), axis=0).T
    head_grad = jnp.sum(head_grad.astype(F32).reshape(8, 16, 8, 384), axis=1)
    rows = jnp.swapaxes(head_grad, 0, 1)
    shared = jnp.sum(head_grad, axis=0)
    return (
        output[None],
        grad_inputs[None],
        rows[..., :128].reshape(8, HEADS * HEAD),
        rows[..., 128:192].reshape(8, KV_HEADS * HEAD),
        rows[..., 192:256].reshape(8, KV_HEADS * HEAD),
        grad_w_output,
        shared[:, 256:288],
        shared[0, 288 : 288 + GAINS],
        grad_gate_up,
        grad_down,
    )


def solution(mesh):
    groups = ("yh", "co", "z")
    specs = (
        P(groups, CTX, None),
        P(groups, CTX, None),
        P(ALL, None),
        P(ALL, None),
        P(ALL, None),
        P(None, ALL),
        P(ALL, None),
        P(ALL),
        P(("yh", "co"), WT, None),
        P(("yh", "co"), None, WT),
        P(groups, None),
        P(groups, None),
        P(groups, CTX, None),
        P(groups, CTX, None),
    )
    return jax.shard_map(
        shards,
        mesh=Mesh(mesh.devices.reshape(SIZES), ALL),
        in_specs=specs,
        out_specs=specs[:10],
        check_vma=False,
    )
```

```python
import math
import types

import jax
import jax.numpy as jnp
from jax import lax
from jax.experimental import pallas as pl
from jax.experimental.pallas import tpu as pltpu
from jax.sharding import Mesh
from jax.sharding import PartitionSpec as P

HEADS = 16
KV_HEADS = 8
DIM = 1024
HEAD = 64
FF = 512
EXPERTS = 32
TOPK = 8
ROWS = 128
GTOK = 1024
CAP = 40
GAINS = 17
WIDE = 3 * FF
PART = 8 * CAP
BF = jnp.bfloat16
F32 = jnp.float32
I32 = jnp.int32

ALL = ("yl", "x", "yh", "co", "z")
SIZES = (2, 4, 2, 2, 4)
SPAN = dict(zip(ALL, SIZES))
CTX = ("yl", "x")
EP = ("yh", "co", "yl", "z")
WT = ("yl", "x", "z")
LONG = ("yl", "x", "yh")


def linear(axes):
    index = 0
    for axis in axes:
        index = index * SPAN[axis] + lax.axis_index(axis)
    return index


def device(axes, index):
    at = {}
    for axis in reversed(axes):
        at[axis] = lax.rem(index, SPAN[axis])
        index = index // SPAN[axis]
    return tuple(at[axis] if axis in at else lax.axis_index(axis) for axis in ALL)


def flip(a, b, bits):
    return sum(lax.rem(a // 2**n + b // 2**n, 2) * 2**n for n in range(bits))


def greet(axes):
    n = math.prod(SPAN[axis] for axis in axes)
    me = linear(axes)
    barrier = pltpu.get_barrier_semaphore()

    def signal(i, carry):
        pl.semaphore_signal(
            barrier,
            inc=1,
            device_id=device(axes, lax.rem(me + i, n)),
            device_id_type=pl.DeviceIdType.MESH,
        )
        return carry

    lax.fori_loop(1, n, signal, 0)
    pl.semaphore_wait(barrier, n - 1)


class Send:
    def __init__(self, axes, part, slot, sems):
        self.axes, self.part, self.slot, self.sems = axes, part, slot, sems
        self.n = math.prod(SPAN[axis] for axis in axes)
        self.bits = self.n.bit_length() - 1
        self.me = linear(axes)

    def partner(self, i):
        return flip(self.me, i, self.bits)

    def copy(self, i):
        to = self.partner(i)
        return pltpu.make_async_remote_copy(
            src_ref=self.part(to),
            dst_ref=self.slot(self.me),
            send_sem=self.sems.at[0, i],
            recv_sem=self.sems.at[1, i],
            device_id=device(self.axes, to),
            device_id_type=pl.DeviceIdType.MESH,
        )

    def own(self):
        return pltpu.make_async_copy(self.part(self.me), self.slot(self.me), self.sems.at[0, 0])

    def each(self, act, low=1, high=None):
        def one(i, carry):
            act(self.copy(i))
            return carry

        lax.fori_loop(low, self.n if high is None else high, one, 0)

    def start(self, own=True):
        if own:
            self.own().start()
        self.each(lambda copy: copy.start())

    def arrived(self, low=1, high=None):
        self.each(lambda copy: copy.wait_recv(), low, high)

    def sent(self):
        self.each(lambda copy: copy.wait_send())

    def wait(self, own=True):
        if own:
            self.own().wait()
        self.each(lambda copy: copy.wait())


def dot(left, right, dims=((1,), (0,))):
    return lax.dot_general(left, right, (dims, ((), ())), preferred_element_type=F32)


def rms(v):
    return lax.rsqrt(jnp.mean(v * v, axis=-1, keepdims=True) + 1e-06)


def norm_back(v, scale, gain, upstream):
    weighted = upstream * gain
    inner = jnp.mean(weighted * v, axis=-1, keepdims=True)
    return scale * weighted - v * (scale * scale * scale) * inner, upstream * v * scale


def halves():
    lane = lax.broadcasted_iota(I32, (1, 128), 1)
    return lane < HEAD, lax.rem(lane, HEAD) < HEAD // 2


def head_mean(v, first):
    low = jnp.sum(jnp.where(first, v, 0.0), axis=1, keepdims=True)
    high = jnp.sum(jnp.where(first, 0.0, v), axis=1, keepdims=True)
    return jnp.where(first, low, high) * (1.0 / HEAD)


def head_rms(v, first):
    return lax.rsqrt(head_mean(v * v, first) + 1e-06)


def head_norm_back(v, gain, upstream, first):
    scale = head_rms(v, first)
    weighted = upstream * gain
    inner = head_mean(weighted * v, first)
    terms = jnp.sum(upstream * v * scale, axis=0, keepdims=True)
    return scale * weighted - v * (scale * scale * scale) * inner, terms


def turn_pair(v, cos, sin, front):
    return v * cos + jnp.where(front, -pltpu.roll(v, 96, 1), pltpu.roll(v, 32, 1)) * sin


def starts(tokens, ends):
    first = jnp.zeros_like(tokens)
    for end in ends:
        first = jnp.maximum(first, jnp.where(tokens >= end, end, 0))
    return first


def sequence_ends(lengths):
    ends, total = [], 0
    for i in range(3):
        total = total + lengths[i]
        ends.append(total)
    return ends


def gain_places():
    column = lax.broadcasted_iota(I32, (128, 128 * GAINS), 1)
    row = lax.broadcasted_iota(I32, (128, 128 * GAINS), 0)
    owner = (column * 3856) >> 16
    return row == owner, row == EXPERTS + column - owner * GAINS


def spread_gains(packed):
    owner, lane = gain_places()
    rows = dot(packed, owner.astype(F32).astype(BF), ((0,), (0,)))
    return jnp.sum(jnp.where(lane, rows, 0.0), axis=0, keepdims=True)


def pack_gains(row):
    owner, lane = gain_places()
    return dot(
        owner.astype(F32).astype(BF), jnp.where(lane, row, 0.0).astype(BF), ((1,), (1,))
    )


def merge(v):
    shape = v.shape
    return v.astype(F32).reshape(math.prod(shape[:-1]), shape[-1]).astype(BF)


def rows_of(j):
    return pl.ds(j * ROWS if isinstance(j, int) else pl.multiple_of(j * ROWS, ROWS), ROWS)


def layer_kernel(r):
    greet(ALL)
    place, seat_me = linear(CTX), linear(EP)
    spot, core, deep = lax.axis_index("x"), lax.axis_index("co"), lax.axis_index("z")
    first, front = halves()

    def bring(source, target):
        copy = pltpu.make_async_copy(source, target, r.s_stage.at[0, 0])
        copy.start()
        return copy

    send_picks = Send(CTX, lambda p: r.picks, lambda q: r.picks_to.at[q], r.s_picks)
    send_x = Send(CTX, lambda p: r.x, lambda q: r.x_to.at[q], r.s_x)
    send_heads = Send(
        ("yl", "x", "yh", "z"),
        lambda p: r.heads.at[p // 8],
        lambda q: r.heads_to.at[q // 4, core, lax.rem(q, 4)],
        r.s_heads,
    )
    swap_heads = Send(
        ("co",), lambda p: r.heads_to.at[:, core], lambda q: r.heads_to.at[:, q], r.s_heads_co
    )
    send_dz = Send(EP, lambda p: r.slots.at[p], lambda q: r.dz_to.at[q], r.s_dz)
    send_wide = Send(
        ("yl", "z"),
        lambda p: r.wide.at[p],
        lambda q: r.wide_to.at[q // 4, spot, lax.rem(q, 4)],
        r.s_wide,
    )
    pass_wide = Send(
        ("x",), lambda p: r.wide_to.at[:, spot], lambda q: r.wide_to.at[:, q], r.s_wide_x
    )
    send_out = Send(LONG, lambda p: r.out, lambda q: r.out_to.at[q, core, deep], r.s_out)
    pass_out = Send(
        ("z",), lambda p: r.out_to.at[:, core, deep], lambda q: r.out_to.at[:, core, q], r.s_out_z
    )
    swap_out = Send(
        ("co",), lambda p: r.out_to.at[:, core], lambda q: r.out_to.at[:, q], r.s_out_co
    )
    send_o = Send(CTX, lambda p: r.o_rows.at[p], lambda q: r.o_to.at[q], r.s_o)
    send_a2 = Send(EP, lambda p: r.slots.at[p], lambda q: r.a2_to.at[q], r.s_a2)
    send_gate = Send(EP, lambda p: r.gates.at[p], lambda q: r.gates_to.at[q], r.s_gate)
    send_y = Send(EP, lambda p: r.y_rows.at[p], lambda q: r.y_to.at[q], r.s_y)
    send_da = Send(EP, lambda p: r.da_rows.at[p], lambda q: r.da_to.at[q], r.s_da)
    send_grad = Send(("x",), lambda p: r.grad.at[:, p], lambda q: r.grad_to.at[:, q], r.s_grad)
    last_grad = Send(
        ("yl", "z"), lambda p: r.grad_mid.at[p], lambda q: r.grad_last.at[q], r.s_grad_last
    )
    send_do = Send(CTX, lambda p: r.do_rows.at[p], lambda q: r.do_to.at[q], r.s_do)
    send_da1 = Send(CTX, lambda p: r.x_to.at[p], lambda q: r.a_rows.at[rows_of(q)], r.s_da1)

    send_picks.start()
    send_x.start()
    send_wide.start()
    send_heads.start()
    send_out.start()

    send_picks.wait()
    mine = jnp.zeros((16, 128), I32)
    for p in range(8):
        mine = mine + r.picks_to[p] * (r.blocks[p] == place).astype(I32)
    expert = lax.broadcasted_iota(I32, (EXPERTS, ROWS), 0)
    named = jnp.zeros((EXPERTS, ROWS), jnp.bool_)
    for k in range(TOPK):
        named = named | (mine[k : k + 1] == expert)
    order = jnp.broadcast_to(mine[TOPK : TOPK + 1].astype(F32), (128, ROWS))
    before = (order.T < order).astype(F32).astype(BF)
    rank = jnp.where(named, dot(named.astype(F32).astype(BF), before), -1.0)
    seat = lax.broadcasted_iota(I32, (CAP, ROWS), 0).astype(F32)
    for e in range(EXPERTS):
        r.hot[pl.ds(e * CAP, CAP)] = (rank[e : e + 1] == seat).astype(F32)

    def fill(source):
        def one(i, carry):
            rows = r.hot[pl.ds(pl.multiple_of(i * 160, 160), 160)].astype(BF)
            r.slots[pl.ds(i * 4, 4)] = dot(rows, source[...]).reshape(4, CAP, DIM).astype(BF)
            return carry

        lax.fori_loop(0, 8, one, 0)

    fill(r.dz)
    send_dz.start()
    send_wide.wait()
    pass_wide.start(own=False)
    send_heads.wait()
    swap_heads.start(own=False)
    send_out.wait()
    pass_out.start(own=False)
    swap_heads.wait(own=False)

    packed = r.heads_to[...].astype(F32).reshape(128, 8, 384)
    r.w_heads[...] = packed[:, :, :256].reshape(DIM, 256).astype(BF)
    r.router[...] = packed[:, :, 256:].reshape(DIM, 128).astype(BF)
    gains = spread_gains(packed[:, 0, 256:].astype(BF))
    gain_one, gain_two, pair = gains[:, :DIM], gains[:, DIM : 2 * DIM], gains[:, 2 * DIM :]
    swapped = pltpu.roll(pair, HEAD, 1)
    gain_q, gain_k = jnp.where(first, pair, swapped), jnp.where(first, swapped, pair)
    ends = sequence_ends(r.lengths)
    lane = lax.broadcasted_iota(I32, (1, 128), 1)
    frequency = jnp.exp(
        lax.rem(lane, HEAD // 2).astype(F32) * (-2.0 * math.log(10000.0) / HEAD)
    )

    def project(j):
        at = rows_of(j)
        v = r.x_to[j].astype(F32)
        low = (v * rms(v) * gain_one).astype(BF)
        r.a_all[at] = low
        qkv = dot(low, r.w_heads[...])
        r.pre[at] = qkv
        token = j * ROWS + lax.broadcasted_iota(I32, (ROWS, 1), 0)
        angle = (token - starts(token, ends)).astype(F32) * frequency
        cos, sin = jnp.cos(angle), jnp.sin(angle)
        r.cos[at] = cos
        r.sin[at] = sin
        q, kv = qkv[:, :128], qkv[:, 128:]
        other = pltpu.roll(kv, HEAD, 1)
        k, val = jnp.where(first, kv, other), jnp.where(first, other, kv)
        r.qr[at] = turn_pair(q * head_rms(q, first) * gain_q, cos, sin, front).astype(BF)
        r.kr[at] = turn_pair(k * head_rms(k, first) * gain_k, cos, sin, front).astype(BF)
        r.vv[at] = val.astype(BF)

    send_x.own().wait()
    project(place)

    def arrive(i, carry):
        send_x.copy(i).wait()
        project(send_x.partner(i))
        return carry

    lax.fori_loop(1, 8, arrive, 0)

    def stacked(v):
        v = v.astype(F32)
        return jnp.concatenate(
            [jnp.where(first, v, 0.0), jnp.where(first, 0.0, v)], axis=0
        ).astype(BF)

    def beside(v):
        return jnp.where(first, v[:ROWS], v[ROWS:])

    def masked_scores(tile, q, width):
        scores = dot(q, r.kr[pl.ds(0, width)], ((1,), (1,))) * HEAD**-0.5
        token = tile * ROWS + lax.rem(lax.broadcasted_iota(I32, (2 * ROWS, 1), 0), ROWS)
        key = lax.broadcasted_iota(I32, (2 * ROWS, width), 1)
        return jnp.where((key <= token) & (key >= starts(token, ends)), scores, -1e30)

    for tile in range(8):
        width, at = ROWS * (tile + 1), rows_of(tile)
        scores = masked_scores(tile, stacked(r.qr[at]), width)
        top = jnp.max(scores, axis=1, keepdims=True)
        weight = jnp.exp(scores - top)
        total = jnp.sum(weight, axis=1, keepdims=True)
        result = beside(dot((weight * (1.0 / total)).astype(BF), r.vv[pl.ds(0, width)]))
        r.mixed[at] = result
        r.o_rows[tile] = result.astype(BF)
        r.level[at] = beside(jnp.broadcast_to(top + jnp.log(total), (2 * ROWS, 128)))
    send_o.start()
    pass_out.wait(own=False)
    swap_out.start(own=False)
    send_dz.wait()
    swap_out.wait(own=False)

    def lay(i, carry):
        r.w_out[rows_of(i)] = merge(r.out_to[pl.ds(2 * i, 2)])
        return carry

    lax.fori_loop(0, 8, lay, 0)

    send_o.wait()
    for h in range(8):
        r.ob[:, h * 128 : (h + 1) * 128] = r.o_to[h]
    x_own = r.x[...].astype(F32)
    dz = r.dz[...].astype(F32)
    x1 = x_own + dot(r.ob[...], r.w_out[...], ((1,), (1,)))
    r.x1[...] = x1
    r2 = rms(x1)
    r.a2[...] = (x1 * r2 * gain_two).astype(BF)
    logits = dot(r.router[...], r.a2[...], ((0,), (1,)))[:EXPERTS]
    weight = jnp.exp(logits - jnp.max(logits, axis=0, keepdims=True))
    probs = weight / jnp.sum(weight, axis=0, keepdims=True)
    chosen = jnp.where(named, probs, 0.0)
    total = jnp.sum(chosen, axis=0, keepdims=True)
    gate = chosen / total
    r.gate[...] = gate
    r.gates[:, 0, :] = gate
    r.gates[:, 1, :] = rank
    fill(r.a2)
    send_gate.start()
    send_a2.start()
    pass_wide.wait(own=False)
    send_gate.wait()
    send_a2.own().wait()

    w_all = r.wide_to.reshape(DIM, WIDE)
    w_gu, w_dn = w_all.at[:, : 2 * FF], w_all.at[:, 2 * FF :]

    def part_of(c):
        return flip(seat_me // 8, c, 2)

    def work(c, carry):
        send_a2.arrived(8 * c + (c == 0).astype(I32), 8 * c + 8)
        k8 = part_of(c) * 8
        at = pl.ds(pl.multiple_of(c * PART, PART), PART)
        a = merge(r.a2_to[pl.ds(k8, 8)])
        r.a_rows[at] = a
        staged = bring(r.dz_to.at[pl.ds(k8, 8)], r.stage)
        gu = dot(a, w_gu[...])
        g, up = gu[:, :FF], gu[:, FF:]
        s = 1.0 / (1.0 + jnp.exp(-g))
        hid = (g * s * up).astype(BF)
        r.hid[at] = hid
        y = dot(hid, w_dn[...], ((1,), (1,)))
        r.y_rows[pl.ds(k8, 8)] = y.reshape(8, CAP, DIM).astype(BF)

        @pl.when(c == 0)
        def _():
            send_y.own().start()

        send_y.each(lambda copy: copy.start(), 8 * c + (c == 0).astype(I32), 8 * c + 8)
        note = r.gates_to[pl.ds(k8, 8)]
        column = jnp.sum(
            jnp.where(note[:, 1:2] == seat[None], note[:, 0:1], 0.0), axis=2, keepdims=True
        )
        staged.wait()
        dy = r.stage[...].astype(F32) * column
        dy = dy.reshape(PART, DIM).astype(BF)
        r.dy[at] = dy
        dhid = dot(dy, w_dn[...])
        dgu = jnp.concatenate([dhid * up * s * (1.0 + g * (1.0 - s)), dhid * g * s], axis=1)
        dgu = dgu.astype(BF)
        r.dgu[at] = dgu
        da = dot(dgu, w_gu[...], ((1,), (1,)))
        r.da_rows[pl.ds(k8, 8)] = da.reshape(8, CAP, DIM).astype(BF)

        @pl.when(c == 0)
        def _():
            send_da.own().start()

        send_da.each(lambda copy: copy.start(), 8 * c + (c == 0).astype(I32), 8 * c + 8)
        return carry

    lax.fori_loop(0, 4, work, 0)
    send_a2.sent()

    def weigh(i, carry):
        to = send_grad.partner(i)
        for yl in range(2):
            at = pl.ds(pl.multiple_of((yl * 4 + to) * ROWS, ROWS), ROWS)
            gu = dot(r.a_rows[:, at], r.dgu[...], ((0,), (0,)))
            r.grad[yl, to, :, :, : 2 * FF] = gu.astype(BF).reshape(4, 32, 2 * FF)
            dn = dot(r.dy[:, at], r.hid[...], ((0,), (0,)))
            r.grad[yl, to, :, :, 2 * FF :] = dn.astype(BF).reshape(4, 32, FF)

        @pl.when(i < 4)
        def _():
            send_grad.copy(i).start()

        return carry

    lax.fori_loop(1, 5, weigh, 0)
    send_grad.own().start()

    send_y.own().wait()
    r.sum[...] = jnp.zeros_like(r.sum)

    def mix(c, carry):
        send_y.arrived(8 * c + (c == 0).astype(I32), 8 * c + 8)
        k8 = pl.multiple_of(part_of(c) * 8, 8)
        bring(r.y_to.at[pl.ds(k8, 8)], r.stage).wait()
        y = merge(r.stage[...])
        hot = r.hot[pl.ds(pl.multiple_of(k8 * CAP, PART), PART)]
        weights = (hot.reshape(8, CAP, ROWS) * r.gate[pl.ds(k8, 8)][:, None]).reshape(PART, ROWS)
        high = weights.astype(BF)
        low = (weights - high.astype(F32)).astype(BF)
        r.sum[...] += dot(high, y, ((0,), (0,))) + dot(low, y, ((0,), (0,)))
        pairs = dot(y, r.dz[...], ((1,), (1,))) * hot
        r.dgate[pl.ds(k8, 8)] = jnp.sum(pairs.reshape(8, CAP, ROWS), axis=1)
        return carry

    lax.fori_loop(0, 4, mix, 0)
    r.output[...] = (r.x1[...] + r.sum[...]).astype(BF)
    dgate = r.dgate[...]
    dc = jnp.where(named, dgate - jnp.sum(gate * dgate, axis=0, keepdims=True), 0.0) / total
    dl = probs * (dc - jnp.sum(probs * dc, axis=0, keepdims=True))
    dl = jnp.concatenate([dl, jnp.zeros((128 - EXPERTS, ROWS), F32)], axis=0).astype(BF)
    r.dl[...] = dl
    r.sum[...] = dot(dl, r.router[...], ((0,), (1,)))
    send_da.own().wait()

    def unmix(c, carry):
        send_da.arrived(8 * c + (c == 0).astype(I32), 8 * c + 8)
        k8 = pl.multiple_of(part_of(c) * 8, 8)
        hot = r.hot[pl.ds(pl.multiple_of(k8 * CAP, PART), PART)].astype(BF)
        bring(r.da_to.at[pl.ds(k8, 8)], r.stage).wait()
        r.sum[...] += dot(hot, merge(r.stage[...]), ((0,), (0,)))
        return carry

    lax.fori_loop(0, 4, unmix, 0)
    dx_two, terms_two = norm_back(r.x1[...], rms(r.x1[...]), gain_two, r.sum[...])
    gain_two_grad = jnp.sum(terms_two, axis=0, keepdims=True)
    r.dx1[...] = dz + dx_two
    r.db[...] = r.dx1[...].astype(BF)
    do = dot(r.db[...], r.w_out[...]).astype(BF)
    for h in range(8):
        r.do_rows[h] = do[:, h * 128 : (h + 1) * 128]
    send_do.start()

    swap_gwo = Send(("co",), lambda p: r.out_to.at[:, p], lambda q: r.gwo_co, r.s_gwo_co)
    pass_gwo = Send(("z",), lambda p: r.gwo_mid.at[:, p], lambda q: r.gwo_z.at[:, q], r.s_gwo_z)
    last_gwo = Send(LONG, lambda p: r.gwo_sum.at[p], lambda q: r.gwo_last.at[q], r.s_gwo)

    def spread_out(i, carry):
        part = dot(r.db[:, rows_of(i)], r.ob[...], ((0,), (0,)))
        r.out_to[pl.ds(2 * i, 2)] = part.reshape(2, 2, 4, 8, DIM).astype(BF)
        return carry

    lax.fori_loop(0, 8, spread_out, 0)
    swap_gwo.start(own=False)

    def add_core(i, carry):
        both = r.out_to[i, core].astype(F32) + r.gwo_mid[i].astype(F32)
        r.gwo_mid[i] = both.astype(BF)
        return carry

    send_do.wait()
    r.dk[...] = jnp.zeros_like(r.dk)
    r.dv[...] = jnp.zeros_like(r.dv)
    for tile in range(8):
        width, at = ROWS * (tile + 1), rows_of(tile)
        keys = pl.ds(0, width)
        q = stacked(r.qr[at])
        level = r.level[at]
        level = jnp.concatenate([level[:, :1], level[:, HEAD : HEAD + 1]], axis=0)
        probs_at = jnp.exp(masked_scores(tile, q, width) - level)
        do = r.do_to[tile]
        inner = head_mean(do.astype(F32) * r.mixed[at], first) * HEAD
        inner = jnp.concatenate([inner[:, :1], inner[:, HEAD : HEAD + 1]], axis=0)
        do = stacked(do)
        dp = dot(do, r.vv[keys], ((1,), (1,)))
        ds = (probs_at * (dp - inner)).astype(BF)
        r.dq[at] = beside(dot(ds, r.kr[keys])) * HEAD**-0.5
        r.dk[keys] += dot(ds, q, ((0,), (0,)))
        r.dv[keys] += dot(probs_at.astype(BF), do, ((0,), (0,)))

    swap_gwo.wait(own=False)
    bring(r.gwo_co, r.gwo_mid).wait()
    lax.fori_loop(0, 16, add_core, 0)
    pass_gwo.start()
    r.gain_one_grad[...] = jnp.zeros_like(r.gain_one_grad)
    r.gain_q_grad[...] = jnp.zeros_like(r.gain_q_grad)
    r.gain_k_grad[...] = jnp.zeros_like(r.gain_k_grad)

    def back(i, carry):
        j = send_da1.partner(lax.rem(i, 8))
        at = rows_of(j)
        cos, sin = r.cos[at], -r.sin[at]
        qkv = r.pre[at]
        q, kv = qkv[:, :128], qkv[:, 128:]
        k = jnp.where(first, kv, pltpu.roll(kv, HEAD, 1))
        dk, dv = r.dk[at] * HEAD**-0.5, r.dv[at]
        dk, dv = dk + pltpu.roll(dk, HEAD, 1), dv + pltpu.roll(dv, HEAD, 1)
        dq, terms = head_norm_back(q, gain_q, turn_pair(r.dq[at], cos, sin, front), first)
        r.gain_q_grad[...] += terms
        dk, terms = head_norm_back(k, gain_k, turn_pair(dk, cos, sin, front), first)
        r.gain_k_grad[...] += terms
        dqkv = jnp.concatenate([dq, jnp.where(first, dk, dv)], axis=1).astype(BF)
        r.dqkv[at] = dqkv
        da1 = dot(dqkv, r.w_heads[...], ((1,), (1,)))
        v = r.x_to[j].astype(F32)
        r.gain_one_grad[...] += jnp.sum(da1 * (v * rms(v)), axis=0, keepdims=True)
        r.x_to[j] = da1.astype(BF)

        @pl.when(i < 8)
        def _():
            send_da1.copy(i).start()

        return carry

    lax.fori_loop(1, 9, back, 0)
    send_da1.own().start()

    pair = jnp.where(
        first,
        r.gain_q_grad[...] + pltpu.roll(r.gain_q_grad[...], HEAD, 1),
        r.gain_k_grad[...],
    )
    gain_grads = pack_gains(
        jnp.concatenate([r.gain_one_grad[...], gain_two_grad, pair], axis=1)
    )
    r.side[...] = jnp.where(
        lax.broadcasted_iota(I32, (128, 8, 128), 1) == 0, gain_grads[:, None], 0.0
    ).reshape(DIM, 128) + dot(r.a2[...], r.dl[...], ((0,), (1,)))

    def small(i, carry):
        at = rows_of(i)
        part = dot(r.a_all[:, at], r.dqkv[...], ((0,), (0,)))
        part = jnp.concatenate([part, r.side[at]], axis=1)
        r.heads_to[pl.ds(2 * i, 2)] = part.reshape(2, 2, 4, 8, 384).astype(BF)
        return carry

    lax.fori_loop(0, 8, small, 0)
    swap_hg = Send(("co",), lambda p: r.heads_to.at[:, p], lambda q: r.hg_co, r.s_hg_co)
    pass_hg = Send(("z",), lambda p: r.hg_mid.at[:, p], lambda q: r.hg_z.at[q], r.s_hg_z)
    last_hg = Send(LONG, lambda p: r.hg_sum.at[p], lambda q: r.hg_last.at[q], r.s_hg)
    swap_hg.start(own=False)

    pass_gwo.wait()
    bring(r.gwo_z, r.out_to.at[:, 0]).wait()

    def add_deep(i, carry):
        total = sum(r.out_to[i, 0, n].astype(F32) for n in range(4))
        r.gwo_sum[i] = total.astype(BF)
        return carry

    lax.fori_loop(0, 16, add_deep, 0)
    last_gwo.start()
    send_grad.wait()
    bring(r.grad_to, r.wide_to).wait()

    def add_grad(i, carry):
        total = sum(
            r.wide_to[i // 4, n, lax.rem(i, 4)].astype(F32) for n in range(4)
        )
        r.grad_mid[i] = total.astype(BF)
        return carry

    lax.fori_loop(0, 8, add_grad, 0)
    last_grad.start()
    swap_hg.wait(own=False)
    r.hg_mid[...] = (r.heads_to[:, core].astype(F32) + r.hg_co[...].astype(F32)).astype(BF)
    pass_hg.start()
    pass_hg.wait()
    r.hg_sum[...] = sum(r.hg_z[n].astype(F32) for n in range(4)).astype(BF)
    last_hg.start()

    send_da1.wait()
    da1 = sum(r.a_rows[rows_of(n)].astype(F32) for n in range(8))
    x_own = r.x[...].astype(F32)
    dx_one, _ = norm_back(x_own, rms(x_own), gain_one, da1)
    r.grad_inputs[...] = (r.dx1[...] + dx_one).astype(BF)
    last_gwo.wait()
    r.grad_out[...] = sum(r.gwo_last[n].astype(F32) for n in range(16))
    last_grad.wait()
    last_hg.wait()
    r.head_grad[...] = sum(
        r.hg_last[...].astype(F32).reshape(8, 2, 8, 384)[:, n] for n in range(2)
    )
    send_y.sent()
    send_da.sent()


INPUTS = (
    ("lengths", pltpu.SMEM),
    ("blocks", pltpu.SMEM),
    ("x", pltpu.VMEM),
    ("heads", pltpu.VMEM),
    ("picks", pltpu.VMEM),
    ("dz", pltpu.VMEM),
    ("wide", pl.ANY),
    ("out", pltpu.VMEM),
)
OUTPUTS = (
    ("output", (ROWS, DIM), BF),
    ("grad_inputs", (ROWS, DIM), BF),
    ("head_grad", (8, 8, 384), F32),
    ("grad_out", (8, DIM), F32),
)
ROW_SLOTS = (EXPERTS, CAP, DIM)
LANDING = (
    ("grad_last", (8, 32, WIDE), BF),
    ("dz_to", ROW_SLOTS, BF),
    ("y_to", ROW_SLOTS, BF),
    ("da_to", ROW_SLOTS, BF),
    ("grad_to", (2, 4, 4, 32, WIDE), BF),
    ("gwo_co", (16, 4, 8, DIM), BF),
    ("gwo_z", (16, 4, 8, DIM), BF),
)
SCRATCH = (
    ("picks_to", (8, 16, 128), I32),
    ("x_to", (8, ROWS, DIM), BF),
    ("heads_to", (16, 2, 4, 8, 384), BF),
    ("wide_to", (2, 4, 4, 32, WIDE), BF),
    ("out_to", (16, 2, 4, 8, DIM), BF),
    ("hot", (EXPERTS * CAP, ROWS), F32),
    ("slots", ROW_SLOTS, BF),
    ("w_heads", (DIM, 256), BF),
    ("router", (DIM, 128), BF),
    ("a_all", (GTOK, DIM), BF),
    ("pre", (GTOK, 256), F32),
    ("cos", (GTOK, 128), F32),
    ("sin", (GTOK, 128), F32),
    ("qr", (GTOK, 128), BF),
    ("kr", (GTOK, 128), BF),
    ("vv", (GTOK, 128), BF),
    ("mixed", (GTOK, 128), F32),
    ("level", (GTOK, 128), F32),
    ("o_rows", (8, ROWS, 128), BF),
    ("o_to", (8, ROWS, 128), BF),
    ("w_out", (DIM, DIM), BF),
    ("ob", (ROWS, DIM), BF),
    ("x1", (ROWS, DIM), F32),
    ("a2", (ROWS, DIM), BF),
    ("gate", (EXPERTS, ROWS), F32),
    ("gates", (EXPERTS, 8, 128), F32),
    ("gates_to", (EXPERTS, 8, 128), F32),
    ("a2_to", ROW_SLOTS, BF),
    ("a_rows", (EXPERTS * CAP, DIM), BF),
    ("hid", (EXPERTS * CAP, FF), BF),
    ("dy", (EXPERTS * CAP, DIM), BF),
    ("dgu", (EXPERTS * CAP, 2 * FF), BF),
    ("y_rows", ROW_SLOTS, BF),
    ("da_rows", ROW_SLOTS, BF),
    ("grad", (2, 4, 4, 32, WIDE), BF),
    ("grad_mid", (8, 32, WIDE), BF),
    ("stage", (8, CAP, DIM), BF),
    ("sum", (ROWS, DIM), F32),
    ("dgate", (EXPERTS, ROWS), F32),
    ("dl", (128, ROWS), BF),
    ("dx1", (ROWS, DIM), F32),
    ("db", (ROWS, DIM), BF),
    ("do_rows", (8, ROWS, 128), BF),
    ("do_to", (8, ROWS, 128), BF),
    ("gwo_mid", (16, 4, 8, DIM), BF),
    ("gwo_sum", (16, 8, DIM), BF),
    ("gwo_last", (16, 8, DIM), BF),
    ("dq", (GTOK, 128), F32),
    ("dk", (GTOK, 128), F32),
    ("dv", (GTOK, 128), F32),
    ("dqkv", (GTOK, 256), BF),
    ("gain_one_grad", (1, DIM), F32),
    ("gain_q_grad", (1, 128), F32),
    ("gain_k_grad", (1, 128), F32),
    ("side", (DIM, 128), F32),
    ("hg_co", (16, 4, 8, 384), BF),
    ("hg_mid", (16, 4, 8, 384), BF),
    ("hg_z", (4, 16, 8, 384), BF),
    ("hg_sum", (16, 8, 384), BF),
    ("hg_last", (16, 8, 384), BF),
)
SEMS = dict(
    s_stage=1,
    s_picks=8,
    s_x=8,
    s_heads=64,
    s_heads_co=2,
    s_dz=32,
    s_wide=8,
    s_wide_x=4,
    s_out=16,
    s_out_z=4,
    s_out_co=2,
    s_o=8,
    s_a2=32,
    s_gate=32,
    s_y=32,
    s_da=32,
    s_grad=4,
    s_grad_last=8,
    s_do=8,
    s_da1=8,
    s_gwo_co=2,
    s_gwo_z=4,
    s_gwo=16,
    s_hg_co=2,
    s_hg_z=4,
    s_hg=16,
)


def layer(*operands):
    names = [name for name, *_ in INPUTS + OUTPUTS + LANDING + SCRATCH] + list(SEMS)

    def body(*refs):
        layer_kernel(types.SimpleNamespace(**dict(zip(names, refs))))

    return pl.pallas_call(
        body,
        out_shape=[jax.ShapeDtypeStruct(shape, kind) for _, shape, kind in OUTPUTS + LANDING],
        in_specs=[pl.BlockSpec(memory_space=space) for _, space in INPUTS],
        out_specs=[pl.BlockSpec(memory_space=pltpu.VMEM)] * len(OUTPUTS)
        + [pl.BlockSpec(memory_space=pl.ANY)] * len(LANDING),
        scratch_shapes=[pltpu.VMEM(shape, kind) for _, shape, kind in SCRATCH]
        + [pltpu.SemaphoreType.DMA((2, n)) for n in SEMS.values()],
        compiler_params=pltpu.CompilerParams(
            collective_id=0, has_side_effects=True, vmem_limit_bytes=VMEM_LIMIT
        ),
        name="layer",
    )(*operands)


VMEM_LIMIT = 63 << 20


def shards(
    inputs,
    cotangent,
    w_query,
    key_weight,
    value_weight,
    w_output,
    w_router,
    norm_gains,
    w_gate_up,
    w_down,
    seq_lengths,
    block_map,
    routes,
    priority,
):
    heads = jnp.concatenate(
        [
            w_query.reshape(8, 8, 128),
            key_weight.reshape(8, 8, 64),
            value_weight.reshape(8, 8, 64),
            jnp.broadcast_to(w_router[:, None], (8, 8, EXPERTS)),
            jnp.broadcast_to(
                jnp.pad(norm_gains[None, :], ((0, 7), (0, 96 - GAINS)))[:, None], (8, 8, 96)
            ),
        ],
        axis=-1,
    ).transpose(1, 0, 2)
    picks = jnp.concatenate(
        [routes[0].T, priority[0], jnp.zeros((16 - TOPK - 1, ROWS), I32)], axis=0
    )
    wide = jnp.concatenate([w_gate_up, jnp.swapaxes(w_down, 1, 2)], axis=-1)
    output, grad_inputs, head_grad, grad_out, expert_grad, *_ = layer(
        seq_lengths[0], block_map[0], inputs[0], heads, picks, cotangent[0], wide, w_output.T
    )
    expert_grad = expert_grad.astype(F32)
    rows = jnp.swapaxes(head_grad, 0, 1)
    shared = jnp.sum(head_grad, axis=0)
    return (
        output[None],
        grad_inputs[None],
        rows[..., :128].reshape(8, HEADS * HEAD),
        rows[..., 128:192].reshape(8, KV_HEADS * HEAD),
        rows[..., 192:256].reshape(8, KV_HEADS * HEAD),
        grad_out.T,
        shared[:, 256:288],
        shared[0, 288 : 288 + GAINS],
        expert_grad[..., : 2 * FF],
        jnp.swapaxes(expert_grad[..., 2 * FF :], 1, 2),
    )


def solution(mesh):
    groups = ("yh", "co", "z")
    specs = (
        P(groups, CTX, None),
        P(groups, CTX, None),
        P(ALL, None),
        P(ALL, None),
        P(ALL, None),
        P(None, ALL),
        P(ALL, None),
        P(ALL),
        P(("yh", "co"), WT, None),
        P(("yh", "co"), None, WT),
        P(groups, None),
        P(groups, None),
        P(groups, CTX, None),
        P(groups, CTX, None),
    )
    return jax.shard_map(
        shards,
        mesh=Mesh(mesh.devices.reshape(SIZES), ALL),
        in_specs=specs,
        out_specs=specs[:10],
        check_vma=False,
    )
```

```python
import math
import types

import jax
import jax.numpy as jnp
from jax import lax
from jax.experimental import pallas as pl
from jax.experimental.pallas import tpu as pltpu
from jax.sharding import Mesh
from jax.sharding import PartitionSpec as P

HEADS = 16
KV_HEADS = 8
DIM = 1024
HEAD = 64
FF = 512
EXPERTS = 32
TOPK = 8
ROWS = 128
GTOK = 1024
CAP = 40
GAINS = 17
WIDE = 3 * FF
PART = 8 * CAP
BF = jnp.bfloat16
F32 = jnp.float32
I32 = jnp.int32

ALL = ("yl", "x", "yh", "co", "z")
SIZES = (2, 4, 2, 2, 4)
SPAN = dict(zip(ALL, SIZES))
CTX = ("yl", "x")
EP = ("yh", "co", "yl", "z")
WT = ("yl", "x", "z")
LONG = ("yl", "x", "yh")
FLAT = ("yl", "yh", "z")


def linear(axes):
    index = 0
    for axis in axes:
        index = index * SPAN[axis] + lax.axis_index(axis)
    return index


def spin(axis, step):
    at = lax.axis_index(axis)
    return at if isinstance(step, int) and step == 0 else lax.rem(at + step, SPAN[axis])


def partner(axes, i):
    steps, at, index = {}, {}, 0
    for axis in reversed(axes):
        if isinstance(i, int):
            steps[axis], i = i % SPAN[axis], i // SPAN[axis]
        else:
            steps[axis], i = lax.rem(i, SPAN[axis]), lax.div(i, SPAN[axis])
    for axis in axes:
        at[axis] = spin(axis, steps[axis])
        index = index * SPAN[axis] + at[axis]
    return index, tuple(at[axis] if axis in at else lax.axis_index(axis) for axis in ALL)


def count(axes):
    return math.prod(SPAN[axis] for axis in axes)


def greet(sets, meanwhile):
    barrier = pltpu.get_barrier_semaphore()
    for axes in sets:
        for i in range(1, count(axes)):
            pl.semaphore_signal(
                barrier,
                inc=1,
                device_id=partner(axes, i)[1],
                device_id_type=pl.DeviceIdType.MESH,
            )
    meanwhile()
    pl.semaphore_wait(barrier, sum(count(axes) - 1 for axes in sets))


def remote(source, target, send_sem, recv_sem, to):
    return pltpu.make_async_remote_copy(
        src_ref=source,
        dst_ref=target,
        send_sem=send_sem,
        recv_sem=recv_sem,
        device_id=to,
        device_id_type=pl.DeviceIdType.MESH,
    )


def drain(span, sem):
    pltpu.make_async_copy(span, span, sem).wait()


class Send:
    def __init__(self, axes, part, slot, slots, sems, own=True):
        self.axes, self.part, self.slot, self.slots = axes, part, slot, slots
        self.sems, self.own, self.n, self.me = sems, own, count(axes), linear(axes)

    def copy(self, i, arrival=1, departure=0):
        place, to = partner(self.axes, i)
        send_sem, recv_sem = self.sems.at[departure], self.sems.at[arrival]
        return remote(self.part(place), self.slot(self.me), send_sem, recv_sem, to)

    def start_own(self, arrival=1):
        pltpu.make_async_copy(
            self.part(self.me), self.slot(self.me), self.sems.at[arrival]
        ).start()

    def start(self):
        if self.own:
            self.start_own()
        for i in range(1, self.n):
            self.copy(i).start()

    def arrived(self):
        drain(self.slots(self.n if self.own else self.n - 1), self.sems.at[1])

    def sent(self):
        drain(self.slots(self.n - 1), self.sems.at[0])

    def wait(self):
        self.arrived()
        self.sent()


class Pairs:
    def __init__(self, blocks, landing, sems):
        self.blocks, self.landing, self.sems, self.me = blocks, landing, sems, linear(EP)

    def start(self, c):
        yh, co = spin("yh", lax.div(c, 2)), spin("co", lax.rem(c, 2))
        for j in range(8):
            yl, z = spin("yl", j // 4), spin("z", j % 4)
            place = ((yh * 2 + co) * 2 + yl) * 4 + z
            copy = remote(
                self.blocks.at[place],
                self.landing.at[self.me],
                self.sems.at[4 + c],
                self.sems.at[c],
                (yl, lax.axis_index("x"), yh, co, z),
            )
            if j > 0:
                copy.start()
                continue

            @pl.when(c > 0)
            def _(copy=copy):
                copy.start()

            @pl.when(c == 0)
            def _():
                pltpu.make_async_copy(
                    self.blocks.at[self.me], self.landing.at[self.me], self.sems.at[0]
                ).start()

    def start_all(self):
        def one(c, carry):
            self.start(c)
            return carry

        lax.fori_loop(0, 4, one, 0)

    def arrived(self, c):
        drain(self.landing.at[pl.ds(0, 8)], self.sems.at[c])

    def sent(self, c):
        @pl.when(c > 0)
        def _():
            drain(self.blocks.at[pl.ds(0, 8)], self.sems.at[4 + c])

        @pl.when(c == 0)
        def _():
            drain(self.blocks.at[pl.ds(0, 7)], self.sems.at[4])

    def all_sent(self):
        def one(c, carry):
            self.sent(c)
            return carry

        lax.fori_loop(0, 4, one, 0)


def dot(left, right, dims=((1,), (0,))):
    return lax.dot_general(left, right, (dims, ((), ())), preferred_element_type=F32)


def rms(v):
    return lax.rsqrt(jnp.mean(v * v, axis=-1, keepdims=True) + 1e-06)


def norm_back(v, scale, gain, upstream):
    weighted = upstream * gain
    inner = jnp.mean(weighted * v, axis=-1, keepdims=True)
    return scale * weighted - v * (scale * scale * scale) * inner, upstream * v * scale


def halves():
    lane = lax.broadcasted_iota(I32, (1, 128), 1)
    return lane < HEAD, lax.rem(lane, HEAD) < HEAD // 2


def head_mean(v, first):
    low = jnp.sum(jnp.where(first, v, 0.0), axis=1, keepdims=True)
    high = jnp.sum(jnp.where(first, 0.0, v), axis=1, keepdims=True)
    return jnp.where(first, low, high) * (1.0 / HEAD)


def head_rms(v, first):
    return lax.rsqrt(head_mean(v * v, first) + 1e-06)


def head_norm_back(v, gain, upstream, first):
    scale = head_rms(v, first)
    weighted = upstream * gain
    inner = head_mean(weighted * v, first)
    terms = jnp.sum(upstream * v * scale, axis=0, keepdims=True)
    return scale * weighted - v * (scale * scale * scale) * inner, terms


def turn_pair(v, cos, sin, front):
    return v * cos + jnp.where(front, -pltpu.roll(v, 96, 1), pltpu.roll(v, 32, 1)) * sin


def starts(tokens, ends):
    first = jnp.zeros_like(tokens)
    for end in ends:
        first = jnp.maximum(first, jnp.where(tokens >= end, end, 0))
    return first


def sequence_ends(lengths):
    ends, total = [], 0
    for i in range(3):
        total = total + lengths[i]
        ends.append(total)
    return ends


def gain_places():
    column = lax.broadcasted_iota(I32, (128, 128 * GAINS), 1)
    row = lax.broadcasted_iota(I32, (128, 128 * GAINS), 0)
    owner = (column * 3856) >> 16
    return row == owner, row == EXPERTS + column - owner * GAINS


def spread_gains(packed):
    owner, lane = gain_places()
    rows = dot(packed, owner.astype(F32).astype(BF), ((0,), (0,)))
    return jnp.sum(jnp.where(lane, rows, 0.0), axis=0, keepdims=True)


def pack_gains(row):
    owner, lane = gain_places()
    return dot(
        owner.astype(F32).astype(BF), jnp.where(lane, row, 0.0).astype(BF), ((1,), (1,))
    )


def merge(v):
    shape = v.shape
    return v.astype(F32).reshape(math.prod(shape[:-1]), shape[-1]).astype(BF)


def rows_of(j):
    return pl.ds(j * ROWS if isinstance(j, int) else pl.multiple_of(j * ROWS, ROWS), ROWS)


def layer_kernel(r):
    def pack():
        wq, wk, wv, wr, gains = (
            ref[...].astype(F32) for ref in (r.wq, r.wk, r.wv, r.wr, r.norm)
        )
        gains = jnp.concatenate([gains, jnp.zeros((7, GAINS), F32)], axis=0)
        side = jnp.concatenate([wr, gains, jnp.zeros((8, 96 - GAINS), F32)], axis=1)
        for h in range(8):
            at = slice(h * HEAD, (h + 1) * HEAD)
            row = [wq[:, h * 128 : (h + 1) * 128], wk[:, at], wv[:, at], side]
            row = jnp.concatenate(row, axis=1).astype(BF)
            r.heads[h] = row
            r.wall[:, h * 256 : (h + 1) * 256] = row[:, :256]
        r.picks[pl.ds(0, 8)] = r.routes[...]
        r.picks[pl.ds(8, 8)] = jnp.broadcast_to(r.priority[...], (8, ROWS))

    greet((EP, LONG), pack)
    place = linear(CTX)
    spot, core, deep = lax.axis_index("x"), lax.axis_index("co"), lax.axis_index("z")
    yl, yh = lax.axis_index("yl"), lax.axis_index("yh")
    first, front = halves()

    def bring(source, target):
        copy = pltpu.make_async_copy(source, target, r.s_stage.at[0])
        copy.start()
        return copy

    send_picks = Send(
        CTX, lambda p: r.picks, lambda q: r.picks_to.at[q], lambda n: r.picks_to.at[pl.ds(0, n)], r.s_picks
    )
    cross_x = Send(
        ("yl",), lambda p: r.x, lambda q: r.x_to.at[q * 4 + spot], lambda n: r.x, r.s_x, own=False
    )
    send_x = Send(
        ("x",), lambda p: r.x, lambda q: r.x_to.at[yl * 4 + q], lambda n: r.x_to.at[pl.ds(0, n)], r.s_x
    )
    pass_x = Send(
        ("x",),
        lambda p: r.x_to.at[(1 - yl) * 4 + spot],
        lambda q: r.x_to.at[(1 - yl) * 4 + q],
        lambda n: r.x_to.at[pl.ds(0, n)],
        r.s_x,
    )
    send_heads = Send(
        CTX,
        lambda p: r.heads.at[p],
        lambda q: r.heads_to.at[q, yh, core, deep],
        lambda n: r.heads_to.at[pl.ds(0, n), yh, core, deep],
        r.s_heads,
    )
    pass_heads = Send(
        ("yh", "z"),
        lambda p: r.heads_to.at[:, yh, core, deep],
        lambda q: r.heads_to.at[:, lax.div(q, 4), core, lax.rem(q, 4)],
        lambda n: r.heads_to.at[pl.ds(0, n), :, :, pl.ds(0, 2)],
        r.s_heads_pass,
        own=False,
    )
    swap_heads = Send(
        ("co",),
        lambda p: r.heads_to.at[:, :, core],
        lambda q: r.heads_to.at[:, :, q],
        lambda n: r.heads_to.at[:, :, 0],
        r.s_heads_co,
        own=False,
    )
    send_gu = Send(
        ("yl", "z"),
        lambda p: r.w_gu.at[p],
        lambda q: r.wide_to.at[lax.div(q, 4), spot, lax.rem(q, 4), :, pl.ds(0, 2 * FF)],
        lambda n: r.w_gu.at[pl.ds(0, n)],
        r.s_gu,
    )
    send_dn = Send(
        ("yl", "z"),
        lambda p: r.w_dn.at[p],
        lambda q: r.wide_to.at[lax.div(q, 4), spot, lax.rem(q, 4), :, pl.ds(2 * FF, FF)],
        lambda n: r.w_dn.at[pl.ds(0, n)],
        r.s_dn,
    )
    pass_wide = Send(
        ("x",),
        lambda p: r.wide_to.at[:, spot],
        lambda q: r.wide_to.at[:, q],
        lambda n: r.wide_to.at[:, pl.ds(0, n)],
        r.s_wide,
        own=False,
    )
    send_out = Send(
        LONG,
        lambda p: r.out,
        lambda q: r.out_to.at[q, core, deep],
        lambda n: r.out_to.at[pl.ds(0, n), core, deep],
        r.s_out,
    )
    pass_out = Send(
        ("z",),
        lambda p: r.out_to.at[:, core, deep],
        lambda q: r.out_to.at[:, core, q],
        lambda n: r.out_to.at[:, core, pl.ds(0, n)],
        r.s_out_z,
        own=False,
    )
    swap_out = Send(
        ("co",),
        lambda p: r.out_to.at[:, core],
        lambda q: r.out_to.at[:, q],
        lambda n: r.out_to.at[:, 0],
        r.s_out_co,
        own=False,
    )
    send_all = Send(
        FLAT,
        lambda p: r.wall,
        lambda q: r.wall_to.at[q, spot, core],
        lambda n: r.wall_to.at[pl.ds(0, n), 0, 0],
        r.s_all,
    )
    pass_all = Send(
        ("x",),
        lambda p: r.wall_to.at[:, spot, core],
        lambda q: r.wall_to.at[:, q, core],
        lambda n: r.wall_to.at[:, pl.ds(0, n), core],
        r.s_all_x,
        own=False,
    )
    swap_all = Send(
        ("co",),
        lambda p: r.wall_to.at[:, :, core],
        lambda q: r.wall_to.at[:, :, q],
        lambda n: r.wall_to.at[:, :, 0],
        r.s_all_co,
        own=False,
    )
    send_o = Send(
        CTX, lambda p: r.o_rows.at[p], lambda q: r.o_to.at[q], lambda n: r.o_to.at[pl.ds(0, n)], r.s_o
    )
    send_dz = Pairs(r.dz_rows, r.dz_to, r.s_dz)
    send_a2 = Pairs(r.a2_rows, r.a2_to, r.s_a2)
    send_gate = Pairs(r.gates, r.gates_to, r.s_gate)
    send_da = Pairs(r.a2_rows, r.da_to, r.s_da)
    send_dg = Pairs(r.dg_rows, r.dg_to, r.s_dg)
    send_y = Pairs(r.dz_rows, r.y_to, r.s_y)
    send_grad = Send(
        ("x",),
        lambda p: r.grad.at[:, p],
        lambda q: r.grad_to.at[:, q],
        lambda n: r.grad.at[:, pl.ds(0, n)],
        r.s_grad,
    )
    last_grad = Send(
        ("yl", "z"),
        lambda p: r.grad_mid.at[p],
        lambda q: r.grad_last.at[q],
        lambda n: r.grad_mid.at[pl.ds(0, n)],
        r.s_grad_last,
    )
    send_do = Send(
        CTX, lambda p: r.do_rows.at[p], lambda q: r.do_to.at[q], lambda n: r.do_to.at[pl.ds(0, n)], r.s_do
    )
    send_dq = Send(
        CTX,
        lambda p: r.dqkv.at[rows_of(p)],
        lambda q: r.dq_to.at[q],
        lambda n: r.dq_to.at[pl.ds(0, n)],
        r.s_dq,
    )
    swap_gwo = Send(
        ("co",), lambda p: r.out_to.at[:, p], lambda q: r.gwo_co, lambda n: r.gwo_co, r.s_gwo_co, own=False
    )
    pass_gwo = Send(
        ("x",),
        lambda p: r.gwo_mid.at[:, p],
        lambda q: r.gwo_x.at[:, q],
        lambda n: r.gwo_x.at[:, pl.ds(0, n)],
        r.s_gwo_x,
    )
    last_gwo = Send(
        FLAT,
        lambda p: r.gwo_sum.at[p],
        lambda q: r.gwo_last.at[q],
        lambda n: r.gwo_sum.at[pl.ds(0, n)],
        r.s_gwo,
    )
    swap_hg = Send(
        ("co",),
        lambda p: r.heads_to.at[:, :, p],
        lambda q: r.hg_co,
        lambda n: r.hg_co,
        r.s_hg_co,
        own=False,
    )
    pass_hg = Send(
        ("z",),
        lambda p: r.hg_mid.at[:, :, p],
        lambda q: r.hg_z.at[q],
        lambda n: r.hg_z.at[pl.ds(0, n)],
        r.s_hg_z,
    )
    last_hg = Send(
        LONG,
        lambda p: r.hg_sum.at[lax.div(p, 2), lax.rem(p, 2)],
        lambda q: r.hg_last.at[q],
        lambda n: r.hg_last.at[pl.ds(0, n)],
        r.s_hg,
    )

    send_picks.start()
    cross_x.copy(1, 4, 8).start()
    send_x.start_own(0)
    for i in range(1, 4):
        send_x.copy(i, i, 9).start()
    send_heads.start()
    send_out.start()
    send_gu.start()
    send_dn.start()

    send_picks.wait()
    mine = jnp.zeros((16, 128), I32)
    for p in range(8):
        mine = mine + r.picks_to[p] * (r.blocks[p] == place).astype(I32)
    expert = lax.broadcasted_iota(I32, (EXPERTS, ROWS), 0)
    named = jnp.zeros((EXPERTS, ROWS), jnp.bool_)
    for k in range(TOPK):
        named = named | (mine[k : k + 1] == expert)
    order = jnp.broadcast_to(mine[TOPK : TOPK + 1].astype(F32), (128, ROWS))
    before = (order.T < order).astype(F32).astype(BF)
    rank = jnp.where(named, dot(named.astype(F32).astype(BF), before), -1.0)
    seat = lax.broadcasted_iota(I32, (CAP, ROWS), 0).astype(F32)
    for e in range(EXPERTS):
        r.hot[pl.ds(e * CAP, CAP)] = (rank[e : e + 1] == seat).astype(F32)

    def part_of(c):
        return spin("yh", lax.div(c, 2)) * 2 + spin("co", lax.rem(c, 2))

    def fill(source, rows, c):
        for i in range(2):
            eight = part_of(c) * 8 + 4 * i
            at = pl.ds(pl.multiple_of(eight * CAP, 4 * CAP), 4 * CAP)
            part = dot(r.hot[at].astype(BF), source[...])
            rows[pl.ds(eight, 4)] = part.reshape(4, CAP, DIM).astype(BF)

    drain(r.x, r.s_x.at[4])
    for i in range(1, 4):
        pass_x.copy(i, 4 + i, 10).start()
    send_heads.wait()
    pass_heads.start()
    send_out.wait()
    pass_out.start()
    pass_heads.wait()
    swap_heads.start()

    def fill_dz(c, carry):
        fill(r.dz, r.dz_rows, c)
        send_dz.start(c)
        return carry

    lax.fori_loop(0, 4, fill_dz, 0)
    swap_heads.wait()

    packed = r.heads_to[...].astype(F32).reshape(128, 8, 384)
    r.w_heads[...] = packed[:, :, :256].reshape(DIM, 256).astype(BF)
    r.router[...] = packed[:, :, 256:].reshape(DIM, 128).astype(BF)
    gains = spread_gains(packed[:, 0, 256:].astype(BF))
    gain_one, gain_two, pair = gains[:, :DIM], gains[:, DIM : 2 * DIM], gains[:, 2 * DIM :]
    swapped = pltpu.roll(pair, HEAD, 1)
    gain_q, gain_k = jnp.where(first, pair, swapped), jnp.where(first, swapped, pair)
    ends = sequence_ends(r.lengths)
    lane = lax.broadcasted_iota(I32, (1, 128), 1)
    frequency = jnp.exp(
        lax.rem(lane, HEAD // 2).astype(F32) * (-2.0 * math.log(10000.0) / HEAD)
    )

    def project(j):
        at = rows_of(j)
        v = r.x_to[j].astype(F32)
        low = (v * rms(v) * gain_one).astype(BF)
        r.a_all[at] = low
        qkv = dot(low, r.w_heads[...])
        r.pre[at] = qkv
        token = j * ROWS + lax.broadcasted_iota(I32, (ROWS, 1), 0)
        angle = (token - starts(token, ends)).astype(F32) * frequency
        cos, sin = jnp.cos(angle), jnp.sin(angle)
        r.cos[at] = cos
        r.sin[at] = sin
        q, kv = qkv[:, :128], qkv[:, 128:]
        other = pltpu.roll(kv, HEAD, 1)
        k, val = jnp.where(first, kv, other), jnp.where(first, other, kv)
        r.qr[at] = turn_pair(q * head_rms(q, first) * gain_q, cos, sin, front).astype(BF)
        r.kr[at] = turn_pair(k * head_rms(k, first) * gain_k, cos, sin, front).astype(BF)
        r.vv[at] = val.astype(BF)

    def arrive(i, carry):
        @pl.when(i != 4)
        def _():
            drain(r.x, r.s_x.at[i])

        project(spin("yl", 2 - lax.div(i, 4)) * 4 + spin("x", 4 - lax.rem(i, 4)))
        return carry

    lax.fori_loop(0, 8, arrive, 0)
    drain(r.x, r.s_x.at[8])
    for n in (9, 10):
        drain(send_x.slots(3), r.s_x.at[n])
    send_gu.wait()
    send_dn.wait()
    pass_wide.start()
    send_all.start()

    def stacked(v):
        v = v.astype(F32)
        return jnp.concatenate(
            [jnp.where(first, v, 0.0), jnp.where(first, 0.0, v)], axis=0
        ).astype(BF)

    def beside(v):
        return jnp.where(first, v[:ROWS], v[ROWS:])

    def masked_scores(tile, q, width):
        scores = dot(q, r.kr[pl.ds(0, width)], ((1,), (1,))) * HEAD**-0.5
        token = tile * ROWS + lax.rem(lax.broadcasted_iota(I32, (2 * ROWS, 1), 0), ROWS)
        key = lax.broadcasted_iota(I32, (2 * ROWS, width), 1)
        return jnp.where((key <= token) & (key >= starts(token, ends)), scores, -1e30)

    for tile in range(8):
        width, at = ROWS * (tile + 1), rows_of(tile)
        scores = masked_scores(tile, stacked(r.qr[at]), width)
        top = jnp.max(scores, axis=1, keepdims=True)
        weight = jnp.exp(scores - top)
        total = jnp.sum(weight, axis=1, keepdims=True)
        result = beside(dot((weight * (1.0 / total)).astype(BF), r.vv[pl.ds(0, width)]))
        r.mixed[at] = result
        r.o_rows[tile] = result.astype(BF)
        r.level[at] = beside(jnp.broadcast_to(top + jnp.log(total), (2 * ROWS, 128)))
    send_o.start()
    pass_out.wait()
    swap_out.start()
    swap_out.wait()

    def lay(i, carry):
        r.w_out[rows_of(i)] = merge(r.out_to[pl.ds(2 * i, 2)])
        return carry

    lax.fori_loop(0, 8, lay, 0)

    send_o.wait()
    for h in range(8):
        r.ob[:, h * 128 : (h + 1) * 128] = r.o_to[h]
    x_own = r.x[...].astype(F32)
    dz = r.dz[...].astype(F32)
    x1 = x_own + dot(r.ob[...], r.w_out[...], ((1,), (1,)))
    r.x1[...] = x1
    r2 = rms(x1)
    r.a2[...] = (x1 * r2 * gain_two).astype(BF)
    logits = dot(r.router[...], r.a2[...], ((0,), (1,)))[:EXPERTS]
    weight = jnp.exp(logits - jnp.max(logits, axis=0, keepdims=True))
    probs = weight / jnp.sum(weight, axis=0, keepdims=True)
    chosen = jnp.where(named, probs, 0.0)
    total = jnp.sum(chosen, axis=0, keepdims=True)
    gate = chosen / total
    r.gate[...] = gate
    r.gates[:, 0, :] = gate
    r.gates[:, 1, :] = rank
    send_gate.start_all()

    def fill_a2(c, carry):
        fill(r.a2, r.a2_rows, c)
        send_a2.start(c)
        return carry

    lax.fori_loop(0, 4, fill_a2, 0)
    send_all.wait()
    pass_all.start()
    pass_wide.wait()

    send_dz.all_sent()
    w_all = r.wide_to.reshape(DIM, WIDE)
    w_gu, w_dn = w_all.at[:, : 2 * FF], w_all.at[:, 2 * FF :]

    def work(c, carry):
        send_gate.arrived(c)
        send_dz.arrived(c)
        k8 = part_of(c) * 8
        at = pl.ds(pl.multiple_of(c * PART, PART), PART)
        staged = bring(r.dz_to.at[pl.ds(k8, 8)], r.stage)
        send_a2.arrived(c)
        a = merge(r.a2_to[pl.ds(k8, 8)])
        r.a_rows[at] = a
        gu = dot(a, w_gu[...])
        g, up = gu[:, :FF], gu[:, FF:]
        s = 1.0 / (1.0 + jnp.exp(-g))
        hid = (g * s * up).astype(BF)
        r.hid[at] = hid
        note = r.gates_to[pl.ds(k8, 8)]
        kept = note[:, 1:2] == seat[None]
        column = jnp.sum(jnp.where(kept, note[:, 0:1], 0.0), axis=2, keepdims=True)
        staged.wait()
        dz_part = r.stage[...].astype(F32)
        dy = (dz_part * column).reshape(PART, DIM).astype(BF)
        r.dy[at] = dy
        dhid = dot(dy, w_dn[...])
        dgu = jnp.concatenate([dhid * up * s * (1.0 + g * (1.0 - s)), dhid * g * s], axis=1)
        dgu = dgu.astype(BF)
        r.dgu[at] = dgu
        da = dot(dgu, w_gu[...], ((1,), (1,)))
        send_a2.sent(c)
        r.a2_rows[pl.ds(k8, 8)] = da.reshape(8, CAP, DIM).astype(BF)
        send_da.start(c)
        y = dot(hid, w_dn[...], ((1,), (1,))).reshape(8, CAP, DIM).astype(BF)
        r.dz_rows[pl.ds(k8, 8)] = y
        inner = jnp.sum(y.astype(F32) * dz_part, axis=2, keepdims=True)
        inner = jnp.sum(jnp.where(kept, inner, 0.0), axis=1, keepdims=True)
        r.dg_rows[pl.ds(k8, 8)] = jnp.broadcast_to(inner, (8, 8, ROWS))
        send_dg.start(c)
        return carry

    lax.fori_loop(0, 4, work, 0)

    def weigh(i, carry):
        to = spin("x", i)
        for half in range(2):
            at = rows_of(half * 4 + to)
            gu = dot(r.a_rows[:, at], r.dgu[...], ((0,), (0,)))
            r.grad[half, to, :, :, : 2 * FF] = gu.astype(BF).reshape(4, 32, 2 * FF)
            dn = dot(r.dy[:, at], r.hid[...], ((0,), (0,)))
            r.grad[half, to, :, :, 2 * FF :] = dn.astype(BF).reshape(4, 32, FF)

        @pl.when(i < 4)
        def _():
            send_grad.copy(i).start()

        return carry

    lax.fori_loop(1, 5, weigh, 0)
    send_grad.start_own()

    pass_all.wait()
    swap_all.start()
    for c in range(4):
        send_dg.arrived(c)
    dgate = r.dg_to[:, 0, :]
    dc = jnp.where(named, dgate - jnp.sum(gate * dgate, axis=0, keepdims=True), 0.0) / total
    dl = probs * (dc - jnp.sum(probs * dc, axis=0, keepdims=True))
    dl = jnp.concatenate([dl, jnp.zeros((128 - EXPERTS, ROWS), F32)], axis=0).astype(BF)
    r.dl[...] = dl
    r.sum[...] = dot(dl, r.router[...], ((0,), (1,)))

    def hot_part(c):
        return r.hot[pl.ds(pl.multiple_of(part_of(c) * PART, PART), PART)]

    def unmix(c, carry):
        send_da.arrived(c)
        bring(r.da_to.at[pl.ds(part_of(c) * 8, 8)], r.stage).wait()
        r.sum[...] += dot(hot_part(c).astype(BF), merge(r.stage[...]), ((0,), (0,)))
        return carry

    lax.fori_loop(0, 4, unmix, 0)
    dx_two, terms_two = norm_back(r.x1[...], rms(r.x1[...]), gain_two, r.sum[...])
    gain_two_grad = jnp.sum(terms_two, axis=0, keepdims=True)
    r.dx1[...] = dz + dx_two
    r.db[...] = r.dx1[...].astype(BF)
    do = dot(r.db[...], r.w_out[...]).astype(BF)
    for h in range(8):
        r.do_rows[h] = do[:, h * 128 : (h + 1) * 128]
    send_do.start()

    send_y.start(0)
    send_y.start(1)

    def spread_out(i, carry):
        part = dot(r.db[:, rows_of(i)], r.ob[...], ((0,), (0,)))
        part = part.reshape(2, 2, 4, 8, DIM).astype(BF)
        for n in range(4):
            at = pl.ds((lax.div(i, 4) * 2 + n // 2) * 4, 4)
            r.out_to[at, n % 2, lax.rem(i, 4)] = part[n // 2, n % 2]
        return carry

    lax.fori_loop(0, 8, spread_out, 0)
    swap_gwo.start()

    def add_core(i, carry):
        both = r.gwo_mid[i].astype(F32) + r.out_to[i, core].astype(F32)
        r.gwo_mid[i] = both.astype(BF)
        return carry

    send_do.wait()
    r.dk[...] = jnp.zeros_like(r.dk)
    r.dv[...] = jnp.zeros_like(r.dv)
    for tile in range(8):
        width, at = ROWS * (tile + 1), rows_of(tile)
        keys = pl.ds(0, width)
        q = stacked(r.qr[at])
        level = r.level[at]
        level = jnp.concatenate([level[:, :1], level[:, HEAD : HEAD + 1]], axis=0)
        probs_at = jnp.exp(masked_scores(tile, q, width) - level)
        do = r.do_to[tile]
        inner = head_mean(do.astype(F32) * r.mixed[at], first) * HEAD
        inner = jnp.concatenate([inner[:, :1], inner[:, HEAD : HEAD + 1]], axis=0)
        do = stacked(do)
        dp = dot(do, r.vv[keys], ((1,), (1,)))
        ds = (probs_at * (dp - inner)).astype(BF)
        r.dq[at] = beside(dot(ds, r.kr[keys])) * HEAD**-0.5
        r.dk[keys] += dot(ds, q, ((0,), (0,)))
        r.dv[keys] += dot(probs_at.astype(BF), do, ((0,), (0,)))

    swap_gwo.wait()
    bring(r.gwo_co, r.gwo_mid).wait()
    lax.fori_loop(0, 16, add_core, 0)
    pass_gwo.start()
    r.gain_q_grad[...] = jnp.zeros_like(r.gain_q_grad)
    r.gain_k_grad[...] = jnp.zeros_like(r.gain_k_grad)

    def back(i, carry):
        j, _ = partner(CTX, lax.rem(i, 8))
        at = rows_of(j)
        cos, sin = r.cos[at], -r.sin[at]
        qkv = r.pre[at]
        q, kv = qkv[:, :128], qkv[:, 128:]
        k = jnp.where(first, kv, pltpu.roll(kv, HEAD, 1))
        dk, dv = r.dk[at] * HEAD**-0.5, r.dv[at]
        dk, dv = dk + pltpu.roll(dk, HEAD, 1), dv + pltpu.roll(dv, HEAD, 1)
        dq, terms = head_norm_back(q, gain_q, turn_pair(r.dq[at], cos, sin, front), first)
        r.gain_q_grad[...] += terms
        dk, terms = head_norm_back(k, gain_k, turn_pair(dk, cos, sin, front), first)
        r.gain_k_grad[...] += terms
        r.dqkv[at] = jnp.concatenate([dq, jnp.where(first, dk, dv)], axis=1).astype(BF)

        @pl.when(i < 8)
        def _():
            send_dq.copy(i).start()

        return carry

    lax.fori_loop(1, 9, back, 0)
    send_dq.start_own()

    diagonal = lax.broadcasted_iota(I32, (ROWS, 128), 0) == lax.broadcasted_iota(I32, (ROWS, 128), 1)

    def small(i, carry):
        at = rows_of(i)
        part = dot(r.a_all[:, at], r.dqkv[...], ((0,), (0,)))
        r.heads_to[i, :, :, :, :, pl.ds(0, 256)] = part.reshape(2, 2, 4, 8, 256).astype(BF)
        column = jnp.sum(part * r.w_heads[at].astype(F32), axis=1, keepdims=True)
        r.gain_one_grad[:, at] = jnp.sum(jnp.where(diagonal, column, 0.0), axis=0, keepdims=True)
        return carry

    lax.fori_loop(0, 8, small, 0)
    pair = jnp.where(
        first,
        r.gain_q_grad[...] + pltpu.roll(r.gain_q_grad[...], HEAD, 1),
        r.gain_k_grad[...],
    )
    gain_grads = pack_gains(
        jnp.concatenate([r.gain_one_grad[...] / gain_one, gain_two_grad, pair], axis=1)
    )
    side = jnp.where(
        lax.broadcasted_iota(I32, (128, 8, 128), 1) == 0, gain_grads[:, None], 0.0
    ).reshape(DIM, 128) + dot(r.a2[...], r.dl[...], ((0,), (1,)))
    r.heads_to[:, :, :, :, :, pl.ds(256, 128)] = side.reshape(8, 2, 2, 4, 8, 128).astype(BF)
    swap_hg.start()

    send_grad.wait()
    bring(r.grad_to, r.wide_to).wait()

    def add_grad(i, carry):
        total = sum(r.wide_to[lax.div(i, 4), n, lax.rem(i, 4)].astype(F32) for n in range(4))
        r.grad_mid[i] = total.astype(BF)
        return carry

    lax.fori_loop(0, 8, add_grad, 0)
    last_grad.start()
    swap_hg.wait()
    r.hg_mid[...] = (r.heads_to[:, :, core].astype(F32) + r.hg_co[...].astype(F32)).astype(BF)
    pass_hg.start()
    send_y.start(2)
    send_y.start(3)
    pass_gwo.wait()
    bring(r.gwo_x, r.out_to.at[:, 0]).wait()

    def add_spot(i, carry):
        total = sum(r.out_to[i, 0, n].astype(F32) for n in range(4))
        r.gwo_sum[i] = total.astype(BF)
        return carry

    lax.fori_loop(0, 16, add_spot, 0)
    last_gwo.start()
    pass_hg.wait()
    r.hg_sum[...] = sum(r.hg_z[n].astype(F32) for n in range(4)).astype(BF)
    last_hg.start()

    send_dq.wait()
    swap_all.wait()
    for h in range(8):
        r.dq_all[:, h * 256 : (h + 1) * 256] = r.dq_to[h]

    def fetch(i):
        for n in range(4):
            pltpu.make_async_copy(
                r.wall_to.at[pl.ds((lax.div(i, 4) * 2 + n // 2) * 4, 4), lax.rem(i, 4), n % 2],
                r.wall_rows.at[lax.rem(i, 2), pl.ds(4 * n, 4)],
                r.s_fetch.at[lax.rem(i, 2)],
            ).start()

    fetch(0)

    def unproject(i, carry):
        @pl.when(i < 7)
        def _():
            fetch(i + 1)

        now = lax.rem(i, 2)
        drain(r.wall_rows.at[now], r.s_fetch.at[now])
        r.sum[:, rows_of(i)] = dot(r.dq_all[...], merge(r.wall_rows[now]), ((1,), (1,)))
        return carry

    lax.fori_loop(0, 8, unproject, 0)
    x_own = r.x[...].astype(F32)
    dx_one, _ = norm_back(x_own, rms(x_own), gain_one, r.sum[...])
    r.grad_inputs[...] = (r.dx1[...] + dx_one).astype(BF)

    r.sum[...] = r.x1[...]

    def mix(c, carry):
        send_y.arrived(c)
        k8 = pl.multiple_of(part_of(c) * 8, 8)
        bring(r.y_to.at[pl.ds(k8, 8)], r.stage).wait()
        y = merge(r.stage[...])
        weights = hot_part(c).reshape(8, CAP, ROWS) * r.gate[pl.ds(k8, 8)][:, None]
        weights = weights.reshape(PART, ROWS)
        high = weights.astype(BF)
        low = (weights - high.astype(F32)).astype(BF)
        r.sum[...] += dot(high, y, ((0,), (0,))) + dot(low, y, ((0,), (0,)))
        return carry

    lax.fori_loop(0, 4, mix, 0)
    r.output[...] = r.sum[...].astype(BF)
    for send in (last_gwo, last_grad, last_hg):
        send.wait()
    for send in (send_gate, send_da, send_dg, send_y):
        send.all_sent()


INPUTS = (
    ("lengths", pltpu.SMEM),
    ("blocks", pltpu.SMEM),
    ("x", pltpu.VMEM),
    ("dz", pltpu.VMEM),
    ("wq", pltpu.VMEM),
    ("wk", pltpu.VMEM),
    ("wv", pltpu.VMEM),
    ("wr", pltpu.VMEM),
    ("norm", pltpu.VMEM),
    ("out", pltpu.VMEM),
    ("routes", pltpu.VMEM),
    ("priority", pltpu.VMEM),
    ("w_gu", pl.ANY),
    ("w_dn", pl.ANY),
)
OUTPUTS = (
    ("output", (ROWS, DIM), BF),
    ("grad_inputs", (ROWS, DIM), BF),
)
ROW_SLOTS = (EXPERTS, CAP, DIM)
LANDING = (
    ("hg_last", (16, 8, 384), BF),
    ("gwo_last", (16, 8, DIM), BF),
    ("grad_last", (8, 32, WIDE), BF),
    ("dz_to", ROW_SLOTS, BF),
    ("y_to", ROW_SLOTS, BF),
    ("da_to", ROW_SLOTS, BF),
    ("grad_to", (2, 4, 4, 32, WIDE), BF),
    ("gwo_co", (16, 4, 8, DIM), BF),
    ("gwo_x", (16, 4, 8, DIM), BF),
    ("wall_to", (16, 4, 2, 8, 2 * DIM), BF),
)
SCRATCH = (
    ("heads", (8, 8, 384), BF),
    ("picks", (16, 128), I32),
    ("picks_to", (8, 16, 128), I32),
    ("x_to", (8, ROWS, DIM), BF),
    ("heads_to", (8, 2, 2, 4, 8, 384), BF),
    ("wide_to", (2, 4, 4, 32, WIDE), BF),
    ("out_to", (16, 2, 4, 8, DIM), BF),
    ("hot", (EXPERTS * CAP, ROWS), F32),
    ("wall", (8, 2 * DIM), BF),
    ("dz_rows", ROW_SLOTS, BF),
    ("a2_rows", ROW_SLOTS, BF),
    ("w_heads", (DIM, 256), BF),
    ("router", (DIM, 128), BF),
    ("a_all", (GTOK, DIM), BF),
    ("pre", (GTOK, 256), F32),
    ("cos", (GTOK, 128), F32),
    ("sin", (GTOK, 128), F32),
    ("qr", (GTOK, 128), BF),
    ("kr", (GTOK, 128), BF),
    ("vv", (GTOK, 128), BF),
    ("mixed", (GTOK, 128), F32),
    ("level", (GTOK, 128), F32),
    ("o_rows", (8, ROWS, 128), BF),
    ("o_to", (8, ROWS, 128), BF),
    ("w_out", (DIM, DIM), BF),
    ("ob", (ROWS, DIM), BF),
    ("x1", (ROWS, DIM), F32),
    ("a2", (ROWS, DIM), BF),
    ("gate", (EXPERTS, ROWS), F32),
    ("gates", (EXPERTS, 8, 128), F32),
    ("gates_to", (EXPERTS, 8, 128), F32),
    ("a2_to", ROW_SLOTS, BF),
    ("a_rows", (EXPERTS * CAP, DIM), BF),
    ("hid", (EXPERTS * CAP, FF), BF),
    ("dy", (EXPERTS * CAP, DIM), BF),
    ("dgu", (EXPERTS * CAP, 2 * FF), BF),
    ("dg_rows", (EXPERTS, 8, ROWS), F32),
    ("dg_to", (EXPERTS, 8, ROWS), F32),
    ("grad", (2, 4, 4, 32, WIDE), BF),
    ("grad_mid", (8, 32, WIDE), BF),
    ("stage", (8, CAP, DIM), BF),
    ("sum", (ROWS, DIM), F32),
    ("dl", (128, ROWS), BF),
    ("dx1", (ROWS, DIM), F32),
    ("db", (ROWS, DIM), BF),
    ("do_rows", (8, ROWS, 128), BF),
    ("do_to", (8, ROWS, 128), BF),
    ("gwo_mid", (16, 4, 8, DIM), BF),
    ("gwo_sum", (16, 8, DIM), BF),
    ("dq", (GTOK, 128), F32),
    ("dk", (GTOK, 128), F32),
    ("dv", (GTOK, 128), F32),
    ("dqkv", (GTOK, 256), BF),
    ("dq_to", (8, ROWS, 256), BF),
    ("dq_all", (ROWS, 2 * DIM), BF),
    ("wall_rows", (2, 16, 8, 2 * DIM), BF),
    ("gain_one_grad", (1, DIM), F32),
    ("gain_q_grad", (1, 128), F32),
    ("gain_k_grad", (1, 128), F32),
    ("hg_co", (8, 2, 4, 8, 384), BF),
    ("hg_mid", (8, 2, 4, 8, 384), BF),
    ("hg_z", (4, 8, 2, 8, 384), BF),
    ("hg_sum", (8, 2, 8, 384), BF),
)
SEMS = dict(s_stage=1, s_fetch=2, s_x=11)
PAIR_SEMS = ("s_dz", "s_a2", "s_gate", "s_da", "s_dg", "s_y")
SEMS.update(dict.fromkeys(PAIR_SEMS, 8))
SEND_SEMS = """s_picks s_heads s_heads_pass s_heads_co s_gu s_dn s_wide s_out s_out_z s_out_co s_all s_all_x s_all_co
s_o s_grad s_grad_last s_do s_dq s_gwo_co s_gwo_x s_gwo s_hg_co s_hg_z s_hg"""
SEMS.update(dict.fromkeys(SEND_SEMS.split(), 2))


def layer(*operands):
    names = [name for name, *_ in INPUTS + OUTPUTS + LANDING + SCRATCH] + list(SEMS)

    def body(*refs):
        layer_kernel(types.SimpleNamespace(**dict(zip(names, refs))))

    return pl.pallas_call(
        body,
        out_shape=[jax.ShapeDtypeStruct(shape, kind) for _, shape, kind in OUTPUTS + LANDING],
        in_specs=[pl.BlockSpec(memory_space=space) for _, space in INPUTS],
        out_specs=[pl.BlockSpec(memory_space=pltpu.VMEM)] * len(OUTPUTS)
        + [pl.BlockSpec(memory_space=pl.ANY)] * len(LANDING),
        scratch_shapes=[pltpu.VMEM(shape, kind) for _, shape, kind in SCRATCH]
        + [pltpu.SemaphoreType.DMA((n,)) for n in SEMS.values()],
        compiler_params=pltpu.CompilerParams(
            collective_id=0, has_side_effects=True, vmem_limit_bytes=VMEM_LIMIT
        ),
        name="layer",
    )(*operands)


VMEM_LIMIT = 63 << 20


def finish_kernel(
    output, grad_inputs, hg, gwo, experts, o_output, o_inputs, o_q, o_k, o_v, o_out, o_router, o_gains, o_gu, o_dn
):
    o_output[...] = output[...]
    o_inputs[...] = grad_inputs[...]
    heads = [hg[2 * c].astype(F32) + hg[2 * c + 1].astype(F32) for c in range(8)]
    for c in range(8):
        o_q[:, c * 128 : (c + 1) * 128] = heads[c][:, :128]
    for c in range(4):
        at, two = slice(c * 128, (c + 1) * 128), heads[2 * c : 2 * c + 2]
        o_k[:, at] = jnp.concatenate([head[:, 128:192] for head in two], axis=1)
        o_v[:, at] = jnp.concatenate([head[:, 192:256] for head in two], axis=1)
    side = sum(head[:, 256:] for head in heads)
    o_router[...] = side[:, :EXPERTS]
    o_gains[...] = side[:1, EXPERTS : EXPERTS + GAINS]
    o_out[...] = sum(gwo[n].astype(F32) for n in range(16))
    o_gu[...] = experts[:, :, : 2 * FF].astype(F32)
    o_dn[...] = experts[:, :, 2 * FF :].astype(F32)


def finish(*operands):
    shapes = (
        ((ROWS, DIM), BF),
        ((ROWS, DIM), BF),
        ((8, HEADS * HEAD), F32),
        ((8, KV_HEADS * HEAD), F32),
        ((8, KV_HEADS * HEAD), F32),
        ((8, DIM), F32),
        ((8, EXPERTS), F32),
        ((1, GAINS), F32),
        ((8, 32, 2 * FF), F32),
        ((8, 32, FF), F32),
    )
    vmem = pl.BlockSpec(memory_space=pltpu.VMEM)
    return pl.pallas_call(
        finish_kernel,
        out_shape=[jax.ShapeDtypeStruct(shape, kind) for shape, kind in shapes],
        in_specs=[vmem] * len(operands),
        out_specs=[vmem] * len(shapes),
        compiler_params=pltpu.CompilerParams(vmem_limit_bytes=VMEM_LIMIT),
        name="finish",
    )(*operands)


def shards(
    inputs,
    cotangent,
    w_query,
    key_weight,
    value_weight,
    w_output,
    w_router,
    norm_gains,
    w_gate_up,
    w_down,
    seq_lengths,
    block_map,
    routes,
    priority,
):
    output, grad_inputs, hg, gwo, experts, *_ = layer(
        seq_lengths[0],
        block_map[0],
        inputs[0],
        cotangent[0],
        w_query,
        key_weight,
        value_weight,
        w_router,
        norm_gains[None],
        w_output.T,
        routes[0].T,
        priority[0],
        w_gate_up,
        jnp.swapaxes(w_down, 1, 2),
    )
    output, grad_inputs, q, k, v, out, router, gains, gate_up, down = finish(
        output, grad_inputs, hg, gwo, experts
    )
    return (
        output[None],
        grad_inputs[None],
        q,
        k,
        v,
        out.T,
        router,
        gains[0],
        gate_up,
        jnp.swapaxes(down, 1, 2),
    )


def solution(mesh):
    groups = ("yh", "co", "z")
    specs = (
        P(groups, CTX, None),
        P(groups, CTX, None),
        P(ALL, None),
        P(ALL, None),
        P(ALL, None),
        P(None, ALL),
        P(ALL, None),
        P(ALL),
        P(("yh", "co"), WT, None),
        P(("yh", "co"), None, WT),
        P(groups, None),
        P(groups, None),
        P(groups, CTX, None),
        P(groups, CTX, None),
    )
    return jax.shard_map(
        shards,
        mesh=Mesh(mesh.devices.reshape(SIZES), ALL),
        in_specs=specs,
        out_specs=specs[:10],
        check_vma=False,
    )
```

```python
import math
import types

import jax
import jax.numpy as jnp
from jax import lax
from jax.experimental import pallas as pl
from jax.experimental.pallas import tpu as pltpu
from jax.sharding import Mesh
from jax.sharding import PartitionSpec as P

HEADS = 16
KV_HEADS = 8
DIM = 1024
HEAD = 64
FF = 512
EXPERTS = 32
TOPK = 8
ROWS = 128
GTOK = 1024
CAP = 40
GAINS = 17
WIDE = 3 * FF
PART = 8 * CAP
BF = jnp.bfloat16
F32 = jnp.float32
I32 = jnp.int32

ALL = ("yl", "x", "yh", "co", "z")
SIZES = (2, 4, 2, 2, 4)
SPAN = dict(zip(ALL, SIZES))
CTX = ("yl", "x")
EP = ("yh", "co", "yl", "z")
WT = ("yl", "x", "z")
LONG = ("yl", "x", "yh")
FLAT = ("yl", "yh", "z")


def linear(axes):
    index = 0
    for axis in axes:
        index = index * SPAN[axis] + lax.axis_index(axis)
    return index


def spin(axis, step):
    at = lax.axis_index(axis)
    return at if isinstance(step, int) and step == 0 else lax.rem(at + step, SPAN[axis])


def partner(axes, i):
    steps, at, index = {}, {}, 0
    for axis in reversed(axes):
        if isinstance(i, int):
            steps[axis], i = i % SPAN[axis], i // SPAN[axis]
        else:
            steps[axis], i = lax.rem(i, SPAN[axis]), lax.div(i, SPAN[axis])
    for axis in axes:
        at[axis] = spin(axis, steps[axis])
        index = index * SPAN[axis] + at[axis]
    return index, tuple(at[axis] if axis in at else lax.axis_index(axis) for axis in ALL)


def count(axes):
    return math.prod(SPAN[axis] for axis in axes)


def greet(sets, meanwhile):
    barrier = pltpu.get_barrier_semaphore()
    for axes in sets:
        for i in range(1, count(axes)):
            pl.semaphore_signal(
                barrier,
                inc=1,
                device_id=partner(axes, i)[1],
                device_id_type=pl.DeviceIdType.MESH,
            )
    meanwhile()
    pl.semaphore_wait(barrier, sum(count(axes) - 1 for axes in sets))


def remote(source, target, send_sem, recv_sem, to):
    return pltpu.make_async_remote_copy(
        src_ref=source,
        dst_ref=target,
        send_sem=send_sem,
        recv_sem=recv_sem,
        device_id=to,
        device_id_type=pl.DeviceIdType.MESH,
    )


def drain(span, sem):
    pltpu.make_async_copy(span, span, sem).wait()


class Send:
    def __init__(self, axes, part, slot, slots, sems, own=True):
        self.axes, self.part, self.slot, self.slots = axes, part, slot, slots
        self.sems, self.own, self.n, self.me = sems, own, count(axes), linear(axes)

    def copy(self, i, arrival=1, departure=0):
        place, to = partner(self.axes, i)
        send_sem, recv_sem = self.sems.at[departure], self.sems.at[arrival]
        return remote(self.part(place), self.slot(self.me), send_sem, recv_sem, to)

    def start_own(self, arrival=1):
        pltpu.make_async_copy(
            self.part(self.me), self.slot(self.me), self.sems.at[arrival]
        ).start()

    def start(self):
        if self.own:
            self.start_own()
        for i in range(1, self.n):
            self.copy(i).start()

    def arrived(self):
        drain(self.slots(self.n if self.own else self.n - 1), self.sems.at[1])

    def sent(self):
        drain(self.slots(self.n - 1), self.sems.at[0])

    def wait(self):
        self.arrived()
        self.sent()


class Pairs:
    def __init__(self, blocks, landing, sems):
        self.blocks, self.landing, self.sems, self.me = blocks, landing, sems, linear(EP)

    def start(self, c):
        yl, co = spin("yl", lax.div(c, 2)), spin("co", lax.rem(c, 2))
        for j in range(8):
            yh, z = spin("yh", j // 4), spin("z", j % 4)
            place = ((yh * 2 + co) * 2 + yl) * 4 + z
            copy = remote(
                self.blocks.at[place],
                self.landing.at[self.me],
                self.sems.at[4 + c],
                self.sems.at[c],
                (yl, lax.axis_index("x"), yh, co, z),
            )
            if j > 0:
                copy.start()
                continue

            @pl.when(c > 0)
            def _(copy=copy):
                copy.start()

            @pl.when(c == 0)
            def _():
                pltpu.make_async_copy(
                    self.blocks.at[self.me], self.landing.at[self.me], self.sems.at[0]
                ).start()

    def start_all(self):
        def one(c, carry):
            self.start(c)
            return carry

        lax.fori_loop(0, 4, one, 0)

    def arrived(self, c):
        drain(self.landing.at[pl.ds(0, 8)], self.sems.at[c])

    def sent(self, c):
        @pl.when(c > 0)
        def _():
            drain(self.blocks.at[pl.ds(0, 8)], self.sems.at[4 + c])

        @pl.when(c == 0)
        def _():
            drain(self.blocks.at[pl.ds(0, 7)], self.sems.at[4])

    def all_sent(self):
        def one(c, carry):
            self.sent(c)
            return carry

        lax.fori_loop(0, 4, one, 0)


def dot(left, right, dims=((1,), (0,))):
    return lax.dot_general(left, right, (dims, ((), ())), preferred_element_type=F32)


def rms(v):
    return lax.rsqrt(jnp.mean(v * v, axis=-1, keepdims=True) + 1e-06)


def norm_back(v, scale, gain, upstream):
    weighted = upstream * gain
    inner = jnp.mean(weighted * v, axis=-1, keepdims=True)
    return scale * weighted - v * (scale * scale * scale) * inner, upstream * v * scale


def halves():
    lane = lax.broadcasted_iota(I32, (1, 128), 1)
    return lane < HEAD, lax.rem(lane, HEAD) < HEAD // 2


def head_mean(v, first):
    low = jnp.sum(jnp.where(first, v, 0.0), axis=1, keepdims=True)
    high = jnp.sum(jnp.where(first, 0.0, v), axis=1, keepdims=True)
    return jnp.where(first, low, high) * (1.0 / HEAD)


def head_rms(v, first):
    return lax.rsqrt(head_mean(v * v, first) + 1e-06)


def head_norm_back(v, gain, upstream, first):
    scale = head_rms(v, first)
    weighted = upstream * gain
    inner = head_mean(weighted * v, first)
    terms = jnp.sum(upstream * v * scale, axis=0, keepdims=True)
    return scale * weighted - v * (scale * scale * scale) * inner, terms


def turn_pair(v, cos, sin, front):
    return v * cos + jnp.where(front, -pltpu.roll(v, 96, 1), pltpu.roll(v, 32, 1)) * sin


def starts(tokens, ends):
    first = jnp.zeros_like(tokens)
    for end in ends:
        first = jnp.maximum(first, jnp.where(tokens >= end, end, 0))
    return first


def sequence_ends(lengths):
    ends, total = [], 0
    for i in range(3):
        total = total + lengths[i]
        ends.append(total)
    return ends


def gain_places():
    column = lax.broadcasted_iota(I32, (128, 128 * GAINS), 1)
    row = lax.broadcasted_iota(I32, (128, 128 * GAINS), 0)
    owner = (column * 3856) >> 16
    return row == owner, row == EXPERTS + column - owner * GAINS


def spread_gains(packed):
    owner, lane = gain_places()
    rows = dot(packed, owner.astype(F32).astype(BF), ((0,), (0,)))
    return jnp.sum(jnp.where(lane, rows, 0.0), axis=0, keepdims=True)


def pack_gains(row):
    owner, lane = gain_places()
    return dot(
        owner.astype(F32).astype(BF), jnp.where(lane, row, 0.0).astype(BF), ((1,), (1,))
    )


def merge(v):
    shape = v.shape
    return v.astype(F32).reshape(math.prod(shape[:-1]), shape[-1]).astype(BF)


def rows_of(j):
    return pl.ds(j * ROWS if isinstance(j, int) else pl.multiple_of(j * ROWS, ROWS), ROWS)


def layer_kernel(r):
    def pack():
        wq, wk, wv, wr, gains = (
            ref[...].astype(F32) for ref in (r.wq, r.wk, r.wv, r.wr, r.norm)
        )
        gains = jnp.concatenate([gains, jnp.zeros((7, GAINS), F32)], axis=0)
        side = jnp.concatenate([wr, gains, jnp.zeros((8, 96 - GAINS), F32)], axis=1)
        for h in range(8):
            at = slice(h * HEAD, (h + 1) * HEAD)
            row = [wq[:, h * 128 : (h + 1) * 128], wk[:, at], wv[:, at], side]
            row = jnp.concatenate(row, axis=1).astype(BF)
            r.heads[h] = row
            r.wall[:, h * 256 : (h + 1) * 256] = row[:, :256]
        r.picks[pl.ds(0, 8)] = r.routes[...]
        r.picks[pl.ds(8, 8)] = jnp.broadcast_to(r.priority[...], (8, ROWS))

    greet((EP, LONG), pack)
    place = linear(CTX)
    spot, core, deep = lax.axis_index("x"), lax.axis_index("co"), lax.axis_index("z")
    yl, yh = lax.axis_index("yl"), lax.axis_index("yh")
    first, front = halves()

    def bring(source, target):
        copy = pltpu.make_async_copy(source, target, r.s_stage.at[0])
        copy.start()
        return copy

    send_picks = Send(
        CTX, lambda p: r.picks, lambda q: r.picks_to.at[q], lambda n: r.picks_to.at[pl.ds(0, n)], r.s_picks
    )
    cross_x = Send(
        ("yl",), lambda p: r.x, lambda q: r.x_to.at[q * 4 + spot], lambda n: r.x, r.s_x, own=False
    )
    send_x = Send(
        ("x",), lambda p: r.x, lambda q: r.x_to.at[yl * 4 + q], lambda n: r.x_to.at[pl.ds(0, n)], r.s_x
    )
    pass_x = Send(
        ("x",),
        lambda p: r.x_to.at[(1 - yl) * 4 + spot],
        lambda q: r.x_to.at[(1 - yl) * 4 + q],
        lambda n: r.x_to.at[pl.ds(0, n)],
        r.s_x,
    )
    send_heads = Send(
        CTX,
        lambda p: r.heads.at[p],
        lambda q: r.heads_to.at[q, yh, core, deep],
        lambda n: r.heads_to.at[pl.ds(0, n), yh, core, deep],
        r.s_heads,
    )
    pass_heads = Send(
        ("yh", "z"),
        lambda p: r.heads_to.at[:, yh, core, deep],
        lambda q: r.heads_to.at[:, lax.div(q, 4), core, lax.rem(q, 4)],
        lambda n: r.heads_to.at[pl.ds(0, n), :, :, pl.ds(0, 2)],
        r.s_heads_pass,
        own=False,
    )
    swap_heads = Send(
        ("co",),
        lambda p: r.heads_to.at[:, :, core],
        lambda q: r.heads_to.at[:, :, q],
        lambda n: r.heads_to.at[:, :, 0],
        r.s_heads_co,
        own=False,
    )
    send_gu = Send(
        ("yl", "z"),
        lambda p: r.w_gu.at[p],
        lambda q: r.wide_to.at[lax.div(q, 4), spot, lax.rem(q, 4), :, pl.ds(0, 2 * FF)],
        lambda n: r.w_gu.at[pl.ds(0, n)],
        r.s_gu,
    )
    send_dn = Send(
        ("yl", "z"),
        lambda p: r.w_dn.at[p],
        lambda q: r.wide_to.at[lax.div(q, 4), spot, lax.rem(q, 4), :, pl.ds(2 * FF, FF)],
        lambda n: r.w_dn.at[pl.ds(0, n)],
        r.s_dn,
    )
    pass_wide = Send(
        ("x",),
        lambda p: r.wide_to.at[:, spot],
        lambda q: r.wide_to.at[:, q],
        lambda n: r.wide_to.at[:, pl.ds(0, n)],
        r.s_wide,
        own=False,
    )
    send_out = Send(
        FLAT,
        lambda p: r.out,
        lambda q: r.out_to.at[q, core, spot],
        lambda n: r.out_to.at[pl.ds(0, n), core, spot],
        r.s_out,
    )
    pass_out = Send(
        ("x",),
        lambda p: r.out_to.at[:, core, spot],
        lambda q: r.out_to.at[:, core, q],
        lambda n: r.out_to.at[:, core, pl.ds(0, n)],
        r.s_out_x,
        own=False,
    )
    swap_out = Send(
        ("co",),
        lambda p: r.out_to.at[:, core],
        lambda q: r.out_to.at[:, q],
        lambda n: r.out_to.at[:, 0],
        r.s_out_co,
        own=False,
    )
    send_all = Send(
        FLAT,
        lambda p: r.wall,
        lambda q: r.wall_to.at[q, spot, core],
        lambda n: r.wall_to.at[pl.ds(0, n), 0, 0],
        r.s_all,
    )
    pass_all = Send(
        ("x",),
        lambda p: r.wall_to.at[:, spot, core],
        lambda q: r.wall_to.at[:, q, core],
        lambda n: r.wall_to.at[:, pl.ds(0, n), core],
        r.s_all_x,
        own=False,
    )
    swap_all = Send(
        ("co",),
        lambda p: r.wall_to.at[:, :, core],
        lambda q: r.wall_to.at[:, :, q],
        lambda n: r.wall_to.at[:, :, 0],
        r.s_all_co,
        own=False,
    )
    send_o = Send(
        CTX, lambda p: r.o_rows.at[p], lambda q: r.o_to.at[q], lambda n: r.o_to.at[pl.ds(0, n)], r.s_o
    )
    send_dz = Pairs(r.dz_rows, r.dz_to, r.s_dz)
    send_a2 = Pairs(r.a2_rows, r.a2_to, r.s_a2)
    send_gate = Pairs(r.gates, r.gates_to, r.s_gate)
    send_da = Pairs(r.a2_rows, r.da_to, r.s_da)
    send_dg = Pairs(r.dg_rows, r.dg_to, r.s_dg)
    send_y = Pairs(r.dz_rows, r.y_to, r.s_y)
    send_grad = Send(
        ("x",),
        lambda p: r.grad.at[:, p],
        lambda q: r.grad_to.at[:, q],
        lambda n: r.grad.at[:, pl.ds(0, n)],
        r.s_grad,
    )
    last_grad = Send(
        ("yl", "z"),
        lambda p: r.grad_mid.at[p],
        lambda q: r.grad_last.at[q],
        lambda n: r.grad_mid.at[pl.ds(0, n)],
        r.s_grad_last,
    )
    send_do = Send(
        CTX, lambda p: r.do_rows.at[p], lambda q: r.do_to.at[q], lambda n: r.do_to.at[pl.ds(0, n)], r.s_do
    )
    send_dq = Send(
        CTX,
        lambda p: r.dqkv.at[rows_of(p)],
        lambda q: r.dq_to.at[q],
        lambda n: r.dq_to.at[pl.ds(0, n)],
        r.s_dq,
    )
    swap_gwo = Send(
        ("co",), lambda p: r.out_to.at[:, p], lambda q: r.gwo_co, lambda n: r.gwo_co, r.s_gwo_co, own=False
    )
    pass_gwo = Send(
        ("x",),
        lambda p: r.gwo_mid.at[:, p],
        lambda q: r.gwo_x.at[:, q],
        lambda n: r.gwo_x.at[:, pl.ds(0, n)],
        r.s_gwo_x,
    )
    last_gwo = Send(
        FLAT,
        lambda p: r.gwo_sum.at[p],
        lambda q: r.gwo_last.at[q],
        lambda n: r.gwo_sum.at[pl.ds(0, n)],
        r.s_gwo,
    )
    swap_hg = Send(
        ("co",),
        lambda p: r.heads_to.at[:, :, p],
        lambda q: r.hg_co,
        lambda n: r.hg_co,
        r.s_hg_co,
        own=False,
    )
    pass_hg = Send(
        ("z",),
        lambda p: r.hg_mid.at[:, :, p],
        lambda q: r.hg_z.at[q],
        lambda n: r.hg_z.at[pl.ds(0, n)],
        r.s_hg_z,
    )
    last_hg = Send(
        LONG,
        lambda p: r.hg_sum.at[lax.div(p, 2), lax.rem(p, 2)],
        lambda q: r.hg_last.at[q],
        lambda n: r.hg_last.at[pl.ds(0, n)],
        r.s_hg,
    )

    send_picks.start()
    cross_x.copy(1, 4, 8).start()
    send_x.start_own(0)
    for i in range(1, 4):
        send_x.copy(i, i, 9).start()
    send_heads.start()
    send_out.start()
    send_gu.start()
    send_dn.start()

    send_picks.wait()
    drain(r.x, r.s_x.at[4])
    for i in range(1, 4):
        pass_x.copy(i, 4 + i, 10).start()
    mine = jnp.zeros((16, 128), I32)
    for p in range(8):
        mine = mine + r.picks_to[p] * (r.blocks[p] == place).astype(I32)
    expert = lax.broadcasted_iota(I32, (EXPERTS, ROWS), 0)
    named = jnp.zeros((EXPERTS, ROWS), jnp.bool_)
    for k in range(TOPK):
        named = named | (mine[k : k + 1] == expert)
    order = jnp.broadcast_to(mine[TOPK : TOPK + 1].astype(F32), (128, ROWS))
    before = (order.T < order).astype(F32).astype(BF)
    rank = jnp.where(named, dot(named.astype(F32).astype(BF), before), -1.0)
    seat = lax.broadcasted_iota(I32, (CAP, ROWS), 0).astype(F32)
    for e in range(EXPERTS):
        r.hot[pl.ds(e * CAP, CAP)] = (rank[e : e + 1] == seat).astype(F32)

    def runs(c):
        four = spin("co", lax.rem(c, 2)) * 8 + spin("yl", lax.div(c, 2)) * 4
        return four, four + 16

    def take(ref, c):
        return jnp.concatenate([ref[pl.ds(four, 4)] for four in runs(c)], axis=0)

    def put(ref, c, v):
        for n, four in enumerate(runs(c)):
            ref[pl.ds(four, 4)] = v[4 * n : 4 * n + 4]

    def stage(ref, c):
        for n, four in enumerate(runs(c)):
            pltpu.make_async_copy(
                ref.at[pl.ds(four, 4)], r.stage.at[pl.ds(4 * n, 4)], r.s_stage.at[0]
            ).start()

    def staged():
        drain(r.stage, r.s_stage.at[0])

    def hot_part(c):
        return jnp.concatenate(
            [r.hot[pl.ds(pl.multiple_of(four * CAP, 4 * CAP), 4 * CAP)] for four in runs(c)], axis=0
        )

    def fill(source, rows, c):
        part = dot(hot_part(c).astype(BF), source[...])
        put(rows, c, part.reshape(8, CAP, DIM).astype(BF))

    send_heads.wait()
    pass_heads.start()

    def fill_dz(c, carry):
        fill(r.dz, r.dz_rows, c)
        send_dz.start(c)
        return carry

    lax.fori_loop(0, 4, fill_dz, 0)
    send_all.start()
    pass_heads.wait()
    swap_heads.start()
    send_out.wait()
    pass_out.start()
    swap_heads.wait()

    packed = r.heads_to[...].astype(F32).reshape(128, 8, 384)
    r.w_heads[...] = packed[:, :, :256].reshape(DIM, 256).astype(BF)
    r.router[...] = packed[:, :, 256:].reshape(DIM, 128).astype(BF)
    gains = spread_gains(packed[:, 0, 256:].astype(BF))
    gain_one, gain_two, pair = gains[:, :DIM], gains[:, DIM : 2 * DIM], gains[:, 2 * DIM :]
    swapped = pltpu.roll(pair, HEAD, 1)
    gain_q, gain_k = jnp.where(first, pair, swapped), jnp.where(first, swapped, pair)
    ends = sequence_ends(r.lengths)
    lane = lax.broadcasted_iota(I32, (1, 128), 1)
    frequency = jnp.exp(
        lax.rem(lane, HEAD // 2).astype(F32) * (-2.0 * math.log(10000.0) / HEAD)
    )

    def project(j):
        at = rows_of(j)
        v = r.x_to[j].astype(F32)
        low = (v * rms(v) * gain_one).astype(BF)
        r.a_all[at] = low
        qkv = dot(low, r.w_heads[...])
        r.pre[at] = qkv
        token = j * ROWS + lax.broadcasted_iota(I32, (ROWS, 1), 0)
        angle = (token - starts(token, ends)).astype(F32) * frequency
        cos, sin = jnp.cos(angle), jnp.sin(angle)
        r.cos[at] = cos
        r.sin[at] = sin
        q, kv = qkv[:, :128], qkv[:, 128:]
        other = pltpu.roll(kv, HEAD, 1)
        k, val = jnp.where(first, kv, other), jnp.where(first, other, kv)
        r.qr[at] = turn_pair(q * head_rms(q, first) * gain_q, cos, sin, front).astype(BF)
        r.kr[at] = turn_pair(k * head_rms(k, first) * gain_k, cos, sin, front).astype(BF)
        r.vv[at] = val.astype(BF)

    def arrive(i, carry):
        @pl.when(i != 4)
        def _():
            drain(r.x, r.s_x.at[i])

        project(spin("yl", 2 - lax.div(i, 4)) * 4 + spin("x", 4 - lax.rem(i, 4)))
        return carry

    lax.fori_loop(0, 8, arrive, 0)
    drain(r.x, r.s_x.at[8])
    for n in (9, 10):
        drain(send_x.slots(3), r.s_x.at[n])

    def stacked(v):
        v = v.astype(F32)
        return jnp.concatenate(
            [jnp.where(first, v, 0.0), jnp.where(first, 0.0, v)], axis=0
        ).astype(BF)

    def beside(v):
        return jnp.where(first, v[:ROWS], v[ROWS:])

    def masked_scores(tile, q, width):
        scores = dot(q, r.kr[pl.ds(0, width)], ((1,), (1,))) * HEAD**-0.5
        token = tile * ROWS + lax.rem(lax.broadcasted_iota(I32, (2 * ROWS, 1), 0), ROWS)
        key = lax.broadcasted_iota(I32, (2 * ROWS, width), 1)
        return jnp.where((key <= token) & (key >= starts(token, ends)), scores, -1e30)

    for tile in range(8):
        width, at = ROWS * (tile + 1), rows_of(tile)
        scores = masked_scores(tile, stacked(r.qr[at]), width)
        top = jnp.max(scores, axis=1, keepdims=True)
        weight = jnp.exp(scores - top)
        total = jnp.sum(weight, axis=1, keepdims=True)
        result = beside(dot((weight * (1.0 / total)).astype(BF), r.vv[pl.ds(0, width)]))
        r.mixed[at] = result
        r.o_rows[tile] = result.astype(BF)
        r.level[at] = beside(jnp.broadcast_to(top + jnp.log(total), (2 * ROWS, 128)))
    send_o.start()
    send_gu.wait()
    send_dn.wait()
    pass_wide.start()
    pass_out.wait()
    swap_out.start()
    swap_out.wait()

    def lay(i, carry):
        rows = [
            r.out_to[pl.ds((lax.div(i, 4) * 2 + n // 2) * 4, 4), n % 2, lax.rem(i, 4)]
            for n in range(4)
        ]
        r.w_out[rows_of(i)] = merge(jnp.concatenate(rows, axis=0))
        return carry

    lax.fori_loop(0, 8, lay, 0)

    send_o.wait()
    for h in range(8):
        r.ob[:, h * 128 : (h + 1) * 128] = r.o_to[h]
    x_own = r.x[...].astype(F32)
    dz = r.dz[...].astype(F32)
    x1 = x_own + dot(r.ob[...], r.w_out[...], ((1,), (1,)))
    r.x1[...] = x1
    r2 = rms(x1)
    r.a2[...] = (x1 * r2 * gain_two).astype(BF)
    logits = dot(r.router[...], r.a2[...], ((0,), (1,)))[:EXPERTS]
    weight = jnp.exp(logits - jnp.max(logits, axis=0, keepdims=True))
    probs = weight / jnp.sum(weight, axis=0, keepdims=True)
    chosen = jnp.where(named, probs, 0.0)
    total = jnp.sum(chosen, axis=0, keepdims=True)
    gate = chosen / total
    for n in range(8):
        r.gate[n] = gate[4 * n : 4 * n + 4]
    r.gates[:, 0, :] = gate
    r.gates[:, 1, :] = rank
    send_gate.start_all()

    def fill_a2(c, carry):
        fill(r.a2, r.a2_rows, c)
        send_a2.start(c)
        return carry

    lax.fori_loop(0, 4, fill_a2, 0)
    send_all.wait()
    pass_all.start()
    pass_wide.wait()

    send_dz.all_sent()
    w_all = r.wide_to.reshape(DIM, WIDE)
    w_gu, w_dn = w_all.at[:, : 2 * FF], w_all.at[:, 2 * FF :]

    def work(c, carry):
        send_gate.arrived(c)
        send_dz.arrived(c)
        at = pl.ds(pl.multiple_of(c * PART, PART), PART)
        stage(r.dz_to, c)
        send_a2.arrived(c)
        a = merge(take(r.a2_to, c))
        r.a_rows[at] = a
        gu = dot(a, w_gu[...])
        g, up = gu[:, :FF], gu[:, FF:]
        s = 1.0 / (1.0 + jnp.exp(-g))
        hid = (g * s * up).astype(BF)
        r.hid[at] = hid
        note = take(r.gates_to, c)
        kept = note[:, 1:2] == seat[None]
        column = jnp.sum(jnp.where(kept, note[:, 0:1], 0.0), axis=2, keepdims=True)
        staged()
        dz_part = r.stage[...].astype(F32)
        dy = (dz_part * column).reshape(PART, DIM).astype(BF)
        r.dy[at] = dy
        dhid = dot(dy, w_dn[...])
        dgu = jnp.concatenate([dhid * up * s * (1.0 + g * (1.0 - s)), dhid * g * s], axis=1)
        dgu = dgu.astype(BF)
        r.dgu[at] = dgu
        da = dot(dgu, w_gu[...], ((1,), (1,)))
        send_a2.sent(c)
        put(r.a2_rows, c, da.reshape(8, CAP, DIM).astype(BF))
        send_da.start(c)
        y = dot(hid, w_dn[...], ((1,), (1,))).reshape(8, CAP, DIM).astype(BF)
        put(r.dz_rows, c, y)
        inner = jnp.sum(y.astype(F32) * dz_part, axis=2, keepdims=True)
        inner = jnp.sum(jnp.where(kept, inner, 0.0), axis=1, keepdims=True)
        put(r.dg_rows, c, jnp.broadcast_to(inner, (8, 8, ROWS)))
        send_dg.start(c)
        return carry

    lax.fori_loop(0, 4, work, 0)

    def weigh(i, carry):
        to = spin("x", i)
        for half in range(2):
            at = rows_of(half * 4 + to)
            gu = dot(r.a_rows[:, at], r.dgu[...], ((0,), (0,)))
            r.grad[half, to, :, :, : 2 * FF] = gu.astype(BF).reshape(4, 32, 2 * FF)
            dn = dot(r.dy[:, at], r.hid[...], ((0,), (0,)))
            r.grad[half, to, :, :, 2 * FF :] = dn.astype(BF).reshape(4, 32, FF)

        @pl.when(i < 4)
        def _():
            send_grad.copy(i).start()

        return carry

    lax.fori_loop(1, 5, weigh, 0)
    send_grad.start_own()

    pass_all.wait()
    swap_all.start()
    for c in range(4):
        send_dg.arrived(c)
    dgate = r.dg_to[:, 0, :]
    dc = jnp.where(named, dgate - jnp.sum(gate * dgate, axis=0, keepdims=True), 0.0) / total
    dl = probs * (dc - jnp.sum(probs * dc, axis=0, keepdims=True))
    dl = jnp.concatenate([dl, jnp.zeros((128 - EXPERTS, ROWS), F32)], axis=0).astype(BF)
    r.dl[...] = dl
    r.sum[...] = dot(dl, r.router[...], ((0,), (1,)))

    def unmix(c, carry):
        send_da.arrived(c)
        stage(r.da_to, c)
        staged()
        r.sum[...] += dot(hot_part(c).astype(BF), merge(r.stage[...]), ((0,), (0,)))
        return carry

    lax.fori_loop(0, 4, unmix, 0)
    send_y.start(0)
    send_y.start(1)
    dx_two, terms_two = norm_back(r.x1[...], rms(r.x1[...]), gain_two, r.sum[...])
    gain_two_grad = jnp.sum(terms_two, axis=0, keepdims=True)
    r.dx1[...] = dz + dx_two
    r.db[...] = r.dx1[...].astype(BF)
    do = dot(r.db[...], r.w_out[...]).astype(BF)
    for h in range(8):
        r.do_rows[h] = do[:, h * 128 : (h + 1) * 128]
    send_do.start()
    send_y.start(2)
    send_y.start(3)

    def spread_out(i, carry):
        part = dot(r.db[:, rows_of(i)], r.ob[...], ((0,), (0,)))
        part = part.reshape(2, 2, 4, 8, DIM).astype(BF)
        for n in range(4):
            at = pl.ds((lax.div(i, 4) * 2 + n // 2) * 4, 4)
            r.out_to[at, n % 2, lax.rem(i, 4)] = part[n // 2, n % 2]
        return carry

    lax.fori_loop(0, 8, spread_out, 0)
    swap_gwo.start()

    def add_core(i, carry):
        both = r.gwo_mid[i].astype(F32) + r.out_to[i, core].astype(F32)
        r.gwo_mid[i] = both.astype(BF)
        return carry

    send_do.wait()
    r.dk[...] = jnp.zeros_like(r.dk)
    r.dv[...] = jnp.zeros_like(r.dv)
    for tile in range(8):
        width, at = ROWS * (tile + 1), rows_of(tile)
        keys = pl.ds(0, width)
        q = stacked(r.qr[at])
        level = r.level[at]
        level = jnp.concatenate([level[:, :1], level[:, HEAD : HEAD + 1]], axis=0)
        probs_at = jnp.exp(masked_scores(tile, q, width) - level)
        do = r.do_to[tile]
        inner = head_mean(do.astype(F32) * r.mixed[at], first) * HEAD
        inner = jnp.concatenate([inner[:, :1], inner[:, HEAD : HEAD + 1]], axis=0)
        do = stacked(do)
        dp = dot(do, r.vv[keys], ((1,), (1,)))
        ds = (probs_at * (dp - inner)).astype(BF)
        r.dq[at] = beside(dot(ds, r.kr[keys])) * HEAD**-0.5
        r.dk[keys] += dot(ds, q, ((0,), (0,)))
        r.dv[keys] += dot(probs_at.astype(BF), do, ((0,), (0,)))

    swap_gwo.wait()
    bring(r.gwo_co, r.gwo_mid).wait()
    lax.fori_loop(0, 16, add_core, 0)
    r.gain_q_grad[...] = jnp.zeros_like(r.gain_q_grad)
    r.gain_k_grad[...] = jnp.zeros_like(r.gain_k_grad)

    def back(i, carry):
        j, _ = partner(CTX, lax.rem(i, 8))
        at = rows_of(j)
        cos, sin = r.cos[at], -r.sin[at]
        qkv = r.pre[at]
        q, kv = qkv[:, :128], qkv[:, 128:]
        k = jnp.where(first, kv, pltpu.roll(kv, HEAD, 1))
        dk, dv = r.dk[at] * HEAD**-0.5, r.dv[at]
        dk, dv = dk + pltpu.roll(dk, HEAD, 1), dv + pltpu.roll(dv, HEAD, 1)
        dq, terms = head_norm_back(q, gain_q, turn_pair(r.dq[at], cos, sin, front), first)
        r.gain_q_grad[...] += terms
        dk, terms = head_norm_back(k, gain_k, turn_pair(dk, cos, sin, front), first)
        r.gain_k_grad[...] += terms
        r.dqkv[at] = jnp.concatenate([dq, jnp.where(first, dk, dv)], axis=1).astype(BF)

        @pl.when(i < 8)
        def _():
            send_dq.copy(i).start()

        return carry

    lax.fori_loop(1, 9, back, 0)
    send_dq.start_own()
    send_grad.wait()
    bring(r.grad_to, r.wide_to).wait()

    def add_grad(i, carry):
        total = sum(r.wide_to[lax.div(i, 4), n, lax.rem(i, 4)].astype(F32) for n in range(4))
        r.grad_mid[i] = total.astype(BF)
        return carry

    lax.fori_loop(0, 8, add_grad, 0)
    last_grad.start()
    pass_gwo.start()

    diagonal = lax.broadcasted_iota(I32, (ROWS, 128), 0) == lax.broadcasted_iota(I32, (ROWS, 128), 1)

    def small(i, carry):
        at = rows_of(i)
        part = dot(r.a_all[:, at], r.dqkv[...], ((0,), (0,)))
        r.heads_to[i, :, :, :, :, pl.ds(0, 256)] = part.reshape(2, 2, 4, 8, 256).astype(BF)
        column = jnp.sum(part * r.w_heads[at].astype(F32), axis=1, keepdims=True)
        r.gain_one_grad[:, at] = jnp.sum(jnp.where(diagonal, column, 0.0), axis=0, keepdims=True)
        return carry

    lax.fori_loop(0, 8, small, 0)
    pair = jnp.where(
        first,
        r.gain_q_grad[...] + pltpu.roll(r.gain_q_grad[...], HEAD, 1),
        r.gain_k_grad[...],
    )
    gain_grads = pack_gains(
        jnp.concatenate([r.gain_one_grad[...] / gain_one, gain_two_grad, pair], axis=1)
    )
    side = jnp.where(
        lax.broadcasted_iota(I32, (128, 8, 128), 1) == 0, gain_grads[:, None], 0.0
    ).reshape(DIM, 128) + dot(r.a2[...], r.dl[...], ((0,), (1,)))
    r.heads_to[:, :, :, :, :, pl.ds(256, 128)] = side.reshape(8, 2, 2, 4, 8, 128).astype(BF)
    swap_hg.start()
    swap_hg.wait()
    r.hg_mid[...] = (r.heads_to[:, :, core].astype(F32) + r.hg_co[...].astype(F32)).astype(BF)
    pass_hg.start()

    send_dq.wait()
    swap_all.wait()
    for h in range(8):
        r.dq_all[:, h * 256 : (h + 1) * 256] = r.dq_to[h]

    def fetch(i):
        for n in range(4):
            pltpu.make_async_copy(
                r.wall_to.at[pl.ds((lax.div(i, 4) * 2 + n // 2) * 4, 4), lax.rem(i, 4), n % 2],
                r.wall_rows.at[lax.rem(i, 2), pl.ds(4 * n, 4)],
                r.s_fetch.at[lax.rem(i, 2)],
            ).start()

    fetch(0)

    def unproject(i, carry):
        @pl.when(i < 7)
        def _():
            fetch(i + 1)

        now = lax.rem(i, 2)
        drain(r.wall_rows.at[now], r.s_fetch.at[now])
        r.sum[:, rows_of(i)] = dot(r.dq_all[...], merge(r.wall_rows[now]), ((1,), (1,)))
        return carry

    lax.fori_loop(0, 8, unproject, 0)
    x_own = r.x[...].astype(F32)
    dx_one, _ = norm_back(x_own, rms(x_own), gain_one, r.sum[...])
    r.grad_inputs[...] = (r.dx1[...] + dx_one).astype(BF)

    pass_hg.wait()
    r.hg_sum[...] = sum(r.hg_z[n].astype(F32) for n in range(4)).astype(BF)
    last_hg.start()
    pass_gwo.wait()
    bring(r.gwo_x, r.out_to.at[:, 0]).wait()

    def add_spot(i, carry):
        total = sum(r.out_to[i, 0, n].astype(F32) for n in range(4))
        r.gwo_sum[i] = total.astype(BF)
        return carry

    lax.fori_loop(0, 16, add_spot, 0)
    last_gwo.start()

    r.sum[...] = r.x1[...]

    def gates_of(c):
        return jnp.concatenate([r.gate[lax.div(four, 4)] for four in runs(c)], axis=0)

    def mix(c, carry):
        send_y.arrived(c)
        stage(r.y_to, c)
        staged()
        y = merge(r.stage[...])
        weights = hot_part(c).reshape(8, CAP, ROWS) * gates_of(c)[:, None]
        weights = weights.reshape(PART, ROWS)
        high = weights.astype(BF)
        low = (weights - high.astype(F32)).astype(BF)
        r.sum[...] += dot(high, y, ((0,), (0,))) + dot(low, y, ((0,), (0,)))
        return carry

    lax.fori_loop(0, 4, mix, 0)
    r.output[...] = r.sum[...].astype(BF)
    for send in (last_gwo, last_grad, last_hg):
        send.wait()
    for send in (send_gate, send_da, send_dg, send_y):
        send.all_sent()


INPUTS = (
    ("lengths", pltpu.SMEM),
    ("blocks", pltpu.SMEM),
    ("x", pltpu.VMEM),
    ("dz", pltpu.VMEM),
    ("wq", pltpu.VMEM),
    ("wk", pltpu.VMEM),
    ("wv", pltpu.VMEM),
    ("wr", pltpu.VMEM),
    ("norm", pltpu.VMEM),
    ("out", pltpu.VMEM),
    ("routes", pltpu.VMEM),
    ("priority", pltpu.VMEM),
    ("w_gu", pl.ANY),
    ("w_dn", pl.ANY),
)
OUTPUTS = (
    ("output", (ROWS, DIM), BF),
    ("grad_inputs", (ROWS, DIM), BF),
)
ROW_SLOTS = (EXPERTS, CAP, DIM)
LANDING = (
    ("hg_last", (16, 8, 384), BF),
    ("gwo_last", (16, 8, DIM), BF),
    ("grad_last", (8, 32, WIDE), BF),
    ("dz_to", ROW_SLOTS, BF),
    ("y_to", ROW_SLOTS, BF),
    ("da_to", ROW_SLOTS, BF),
    ("grad_to", (2, 4, 4, 32, WIDE), BF),
    ("gwo_co", (16, 4, 8, DIM), BF),
    ("gwo_x", (16, 4, 8, DIM), BF),
    ("wall_to", (16, 4, 2, 8, 2 * DIM), BF),
)
SCRATCH = (
    ("heads", (8, 8, 384), BF),
    ("picks", (16, 128), I32),
    ("picks_to", (8, 16, 128), I32),
    ("x_to", (8, ROWS, DIM), BF),
    ("heads_to", (8, 2, 2, 4, 8, 384), BF),
    ("wide_to", (2, 4, 4, 32, WIDE), BF),
    ("out_to", (16, 2, 4, 8, DIM), BF),
    ("hot", (EXPERTS * CAP, ROWS), F32),
    ("wall", (8, 2 * DIM), BF),
    ("dz_rows", ROW_SLOTS, BF),
    ("a2_rows", ROW_SLOTS, BF),
    ("w_heads", (DIM, 256), BF),
    ("router", (DIM, 128), BF),
    ("a_all", (GTOK, DIM), BF),
    ("pre", (GTOK, 256), F32),
    ("cos", (GTOK, 128), F32),
    ("sin", (GTOK, 128), F32),
    ("qr", (GTOK, 128), BF),
    ("kr", (GTOK, 128), BF),
    ("vv", (GTOK, 128), BF),
    ("mixed", (GTOK, 128), F32),
    ("level", (GTOK, 128), F32),
    ("o_rows", (8, ROWS, 128), BF),
    ("o_to", (8, ROWS, 128), BF),
    ("w_out", (DIM, DIM), BF),
    ("ob", (ROWS, DIM), BF),
    ("x1", (ROWS, DIM), F32),
    ("a2", (ROWS, DIM), BF),
    ("gate", (8, 4, ROWS), F32),
    ("gates", (EXPERTS, 8, 128), F32),
    ("gates_to", (EXPERTS, 8, 128), F32),
    ("a2_to", ROW_SLOTS, BF),
    ("a_rows", (EXPERTS * CAP, DIM), BF),
    ("hid", (EXPERTS * CAP, FF), BF),
    ("dy", (EXPERTS * CAP, DIM), BF),
    ("dgu", (EXPERTS * CAP, 2 * FF), BF),
    ("dg_rows", (EXPERTS, 8, ROWS), F32),
    ("dg_to", (EXPERTS, 8, ROWS), F32),
    ("grad", (2, 4, 4, 32, WIDE), BF),
    ("grad_mid", (8, 32, WIDE), BF),
    ("stage", (8, CAP, DIM), BF),
    ("sum", (ROWS, DIM), F32),
    ("dl", (128, ROWS), BF),
    ("dx1", (ROWS, DIM), F32),
    ("db", (ROWS, DIM), BF),
    ("do_rows", (8, ROWS, 128), BF),
    ("do_to", (8, ROWS, 128), BF),
    ("gwo_mid", (16, 4, 8, DIM), BF),
    ("gwo_sum", (16, 8, DIM), BF),
    ("dq", (GTOK, 128), F32),
    ("dk", (GTOK, 128), F32),
    ("dv", (GTOK, 128), F32),
    ("dqkv", (GTOK, 256), BF),
    ("dq_to", (8, ROWS, 256), BF),
    ("dq_all", (ROWS, 2 * DIM), BF),
    ("wall_rows", (2, 16, 8, 2 * DIM), BF),
    ("gain_one_grad", (1, DIM), F32),
    ("gain_q_grad", (1, 128), F32),
    ("gain_k_grad", (1, 128), F32),
    ("hg_co", (8, 2, 4, 8, 384), BF),
    ("hg_mid", (8, 2, 4, 8, 384), BF),
    ("hg_z", (4, 8, 2, 8, 384), BF),
    ("hg_sum", (8, 2, 8, 384), BF),
)
SEMS = dict(s_stage=1, s_fetch=2, s_x=11)
PAIR_SEMS = ("s_dz", "s_a2", "s_gate", "s_da", "s_dg", "s_y")
SEMS.update(dict.fromkeys(PAIR_SEMS, 8))
SEND_SEMS = """s_picks s_heads s_heads_pass s_heads_co s_gu s_dn s_wide s_out s_out_x s_out_co s_all s_all_x s_all_co
s_o s_grad s_grad_last s_do s_dq s_gwo_co s_gwo_x s_gwo s_hg_co s_hg_z s_hg"""
SEMS.update(dict.fromkeys(SEND_SEMS.split(), 2))


def layer(*operands):
    names = [name for name, *_ in INPUTS + OUTPUTS + LANDING + SCRATCH] + list(SEMS)

    def body(*refs):
        layer_kernel(types.SimpleNamespace(**dict(zip(names, refs))))

    return pl.pallas_call(
        body,
        out_shape=[jax.ShapeDtypeStruct(shape, kind) for _, shape, kind in OUTPUTS + LANDING],
        in_specs=[pl.BlockSpec(memory_space=space) for _, space in INPUTS],
        out_specs=[pl.BlockSpec(memory_space=pltpu.VMEM)] * len(OUTPUTS)
        + [pl.BlockSpec(memory_space=pl.ANY)] * len(LANDING),
        scratch_shapes=[pltpu.VMEM(shape, kind) for _, shape, kind in SCRATCH]
        + [pltpu.SemaphoreType.DMA((n,)) for n in SEMS.values()],
        compiler_params=pltpu.CompilerParams(
            collective_id=0, has_side_effects=True, vmem_limit_bytes=VMEM_LIMIT
        ),
        name="layer",
    )(*operands)


VMEM_LIMIT = 63 << 20


def finish_kernel(
    output, grad_inputs, hg, gwo, experts, o_output, o_inputs, o_q, o_k, o_v, o_out, o_router, o_gains, o_gu, o_dn
):
    o_output[...] = output[...]
    o_inputs[...] = grad_inputs[...]
    heads = [hg[2 * c].astype(F32) + hg[2 * c + 1].astype(F32) for c in range(8)]
    for c in range(8):
        o_q[:, c * 128 : (c + 1) * 128] = heads[c][:, :128]
    for c in range(4):
        at, two = slice(c * 128, (c + 1) * 128), heads[2 * c : 2 * c + 2]
        o_k[:, at] = jnp.concatenate([head[:, 128:192] for head in two], axis=1)
        o_v[:, at] = jnp.concatenate([head[:, 192:256] for head in two], axis=1)
    side = sum(head[:, 256:] for head in heads)
    o_router[...] = side[:, :EXPERTS]
    o_gains[...] = side[:1, EXPERTS : EXPERTS + GAINS]
    o_out[...] = sum(gwo[n].astype(F32) for n in range(16))
    o_gu[...] = experts[:, :, : 2 * FF].astype(F32)
    o_dn[...] = experts[:, :, 2 * FF :].astype(F32)


def finish(*operands):
    shapes = (
        ((ROWS, DIM), BF),
        ((ROWS, DIM), BF),
        ((8, HEADS * HEAD), F32),
        ((8, KV_HEADS * HEAD), F32),
        ((8, KV_HEADS * HEAD), F32),
        ((8, DIM), F32),
        ((8, EXPERTS), F32),
        ((1, GAINS), F32),
        ((8, 32, 2 * FF), F32),
        ((8, 32, FF), F32),
    )
    vmem = pl.BlockSpec(memory_space=pltpu.VMEM)
    return pl.pallas_call(
        finish_kernel,
        out_shape=[jax.ShapeDtypeStruct(shape, kind) for shape, kind in shapes],
        in_specs=[vmem] * len(operands),
        out_specs=[vmem] * len(shapes),
        compiler_params=pltpu.CompilerParams(vmem_limit_bytes=VMEM_LIMIT),
        name="finish",
    )(*operands)


def shards(
    inputs,
    cotangent,
    w_query,
    key_weight,
    value_weight,
    w_output,
    w_router,
    norm_gains,
    w_gate_up,
    w_down,
    seq_lengths,
    block_map,
    routes,
    priority,
):
    output, grad_inputs, hg, gwo, experts, *_ = layer(
        seq_lengths[0],
        block_map[0],
        inputs[0],
        cotangent[0],
        w_query,
        key_weight,
        value_weight,
        w_router,
        norm_gains[None],
        w_output.T,
        routes[0].T,
        priority[0],
        w_gate_up,
        jnp.swapaxes(w_down, 1, 2),
    )
    output, grad_inputs, q, k, v, out, router, gains, gate_up, down = finish(
        output, grad_inputs, hg, gwo, experts
    )
    return (
        output[None],
        grad_inputs[None],
        q,
        k,
        v,
        out.T,
        router,
        gains[0],
        gate_up,
        jnp.swapaxes(down, 1, 2),
    )


def solution(mesh):
    groups = ("yh", "co", "z")
    specs = (
        P(groups, CTX, None),
        P(groups, CTX, None),
        P(ALL, None),
        P(ALL, None),
        P(ALL, None),
        P(None, ALL),
        P(ALL, None),
        P(ALL),
        P(("yh", "co"), WT, None),
        P(("yh", "co"), None, WT),
        P(groups, None),
        P(groups, None),
        P(groups, CTX, None),
        P(groups, CTX, None),
    )
    return jax.shard_map(
        shards,
        mesh=Mesh(mesh.devices.reshape(SIZES), ALL),
        in_specs=specs,
        out_specs=specs[:10],
        check_vma=False,
    )
```

```python
import math
import types

import jax
import jax.numpy as jnp
from jax import lax
from jax.experimental import pallas as pl
from jax.experimental.pallas import tpu as pltpu
from jax.sharding import Mesh
from jax.sharding import PartitionSpec as P

HEADS = 16
KV_HEADS = 8
DIM = 1024
HEAD = 64
FF = 512
EXPERTS = 32
TOPK = 8
ROWS = 128
GTOK = 1024
CAP = 40
GAINS = 17
WIDE = 3 * FF
PART = 8 * CAP
BF = jnp.bfloat16
F32 = jnp.float32
I32 = jnp.int32

ALL = ("yl", "x", "yh", "co", "z")
SIZES = (2, 4, 2, 2, 4)
SPAN = dict(zip(ALL, SIZES))
CTX = ("yl", "x")
EP = ("yh", "co", "yl", "z")
WT = ("yl", "x", "z")
LONG = ("yl", "x", "yh")
FLAT = ("yl", "yh", "z")


def linear(axes):
    index = 0
    for axis in axes:
        index = index * SPAN[axis] + lax.axis_index(axis)
    return index


def spin(axis, step):
    at = lax.axis_index(axis)
    return at if isinstance(step, int) and step == 0 else lax.rem(at + step, SPAN[axis])


def partner(axes, i):
    steps, at, index = {}, {}, 0
    for axis in reversed(axes):
        if isinstance(i, int):
            steps[axis], i = i % SPAN[axis], i // SPAN[axis]
        else:
            steps[axis], i = lax.rem(i, SPAN[axis]), lax.div(i, SPAN[axis])
    for axis in axes:
        at[axis] = spin(axis, steps[axis])
        index = index * SPAN[axis] + at[axis]
    return index, tuple(at[axis] if axis in at else lax.axis_index(axis) for axis in ALL)


def count(axes):
    return math.prod(SPAN[axis] for axis in axes)


def greet(sets, meanwhile):
    barrier = pltpu.get_barrier_semaphore()
    for axes in sets:
        for i in range(1, count(axes)):
            pl.semaphore_signal(
                barrier,
                inc=1,
                device_id=partner(axes, i)[1],
                device_id_type=pl.DeviceIdType.MESH,
            )
    meanwhile()
    pl.semaphore_wait(barrier, sum(count(axes) - 1 for axes in sets))


def remote(source, target, send_sem, recv_sem, to):
    return pltpu.make_async_remote_copy(
        src_ref=source,
        dst_ref=target,
        send_sem=send_sem,
        recv_sem=recv_sem,
        device_id=to,
        device_id_type=pl.DeviceIdType.MESH,
    )


def drain(span, sem):
    pltpu.make_async_copy(span, span, sem).wait()


class Send:
    def __init__(self, axes, part, slot, slots, sems, own=True):
        self.axes, self.part, self.slot, self.slots = axes, part, slot, slots
        self.sems, self.own, self.n, self.me = sems, own, count(axes), linear(axes)

    def copy(self, i, arrival=1, departure=0):
        place, to = partner(self.axes, i)
        send_sem, recv_sem = self.sems.at[departure], self.sems.at[arrival]
        return remote(self.part(place), self.slot(self.me), send_sem, recv_sem, to)

    def start_own(self, arrival=1):
        pltpu.make_async_copy(
            self.part(self.me), self.slot(self.me), self.sems.at[arrival]
        ).start()

    def start(self):
        if self.own:
            self.start_own()
        for i in range(1, self.n):
            self.copy(i).start()

    def arrived(self):
        drain(self.slots(self.n if self.own else self.n - 1), self.sems.at[1])

    def sent(self):
        drain(self.slots(self.n - 1), self.sems.at[0])

    def wait(self):
        self.arrived()
        self.sent()


class Pairs:
    def __init__(self, blocks, landing, sems):
        self.blocks, self.landing, self.sems, self.me = blocks, landing, sems, linear(EP)

    def start(self, c):
        yl, co = spin("yl", lax.div(c, 2)), spin("co", lax.rem(c, 2))
        for j in range(8):
            yh, z = spin("yh", j // 4), spin("z", j % 4)
            place = ((yh * 2 + co) * 2 + yl) * 4 + z
            copy = remote(
                self.blocks.at[place],
                self.landing.at[self.me],
                self.sems.at[4 + c],
                self.sems.at[c],
                (yl, lax.axis_index("x"), yh, co, z),
            )
            if j > 0:
                copy.start()
                continue

            @pl.when(c > 0)
            def _(copy=copy):
                copy.start()

            @pl.when(c == 0)
            def _():
                pltpu.make_async_copy(
                    self.blocks.at[self.me], self.landing.at[self.me], self.sems.at[0]
                ).start()

    def start_all(self):
        def one(c, carry):
            self.start(c)
            return carry

        lax.fori_loop(0, 4, one, 0)

    def arrived(self, c):
        drain(self.landing.at[pl.ds(0, 8)], self.sems.at[c])

    def sent(self, c):
        @pl.when(c > 0)
        def _():
            drain(self.blocks.at[pl.ds(0, 8)], self.sems.at[4 + c])

        @pl.when(c == 0)
        def _():
            drain(self.blocks.at[pl.ds(0, 7)], self.sems.at[4])

    def all_sent(self):
        def one(c, carry):
            self.sent(c)
            return carry

        lax.fori_loop(0, 4, one, 0)


def dot(left, right, dims=((1,), (0,))):
    return lax.dot_general(left, right, (dims, ((), ())), preferred_element_type=F32)


def rms(v):
    return lax.rsqrt(jnp.mean(v * v, axis=-1, keepdims=True) + 1e-06)


def norm_back(v, scale, gain, upstream):
    weighted = upstream * gain
    inner = jnp.mean(weighted * v, axis=-1, keepdims=True)
    return scale * weighted - v * (scale * scale * scale) * inner, upstream * v * scale


def halves():
    lane = lax.broadcasted_iota(I32, (1, 128), 1)
    return lane < HEAD, lax.rem(lane, HEAD) < HEAD // 2


def head_mean(v, first):
    low = jnp.sum(jnp.where(first, v, 0.0), axis=1, keepdims=True)
    high = jnp.sum(jnp.where(first, 0.0, v), axis=1, keepdims=True)
    return jnp.where(first, low, high) * (1.0 / HEAD)


def head_rms(v, first):
    return lax.rsqrt(head_mean(v * v, first) + 1e-06)


def head_norm_back(v, gain, upstream, first):
    scale = head_rms(v, first)
    weighted = upstream * gain
    inner = head_mean(weighted * v, first)
    terms = jnp.sum(upstream * v * scale, axis=0, keepdims=True)
    return scale * weighted - v * (scale * scale * scale) * inner, terms


def turn_pair(v, cos, sin, front):
    return v * cos + jnp.where(front, -pltpu.roll(v, 96, 1), pltpu.roll(v, 32, 1)) * sin


def starts(tokens, ends):
    first = jnp.zeros_like(tokens)
    for end in ends:
        first = jnp.maximum(first, jnp.where(tokens >= end, end, 0))
    return first


def sequence_ends(lengths):
    ends, total = [], 0
    for i in range(3):
        total = total + lengths[i]
        ends.append(total)
    return ends


def gain_places():
    column = lax.broadcasted_iota(I32, (128, 128 * GAINS), 1)
    row = lax.broadcasted_iota(I32, (128, 128 * GAINS), 0)
    owner = (column * 3856) >> 16
    return row == owner, row == EXPERTS + column - owner * GAINS


def spread_gains(packed):
    owner, lane = gain_places()
    rows = dot(packed, owner.astype(F32).astype(BF), ((0,), (0,)))
    return jnp.sum(jnp.where(lane, rows, 0.0), axis=0, keepdims=True)


def pack_gains(row):
    owner, lane = gain_places()
    return dot(
        owner.astype(F32).astype(BF), jnp.where(lane, row, 0.0).astype(BF), ((1,), (1,))
    )


def merge(v):
    shape = v.shape
    return v.astype(F32).reshape(math.prod(shape[:-1]), shape[-1]).astype(BF)


def rows_of(j):
    return pl.ds(j * ROWS if isinstance(j, int) else pl.multiple_of(j * ROWS, ROWS), ROWS)


def layer_kernel(r):
    def pack():
        wq, wk, wv, wr, gains = (
            ref[...].astype(F32) for ref in (r.wq, r.wk, r.wv, r.wr, r.norm)
        )
        gains = jnp.concatenate([gains, jnp.zeros((7, GAINS), F32)], axis=0)
        side = jnp.concatenate([wr, gains, jnp.zeros((8, 96 - GAINS), F32)], axis=1)
        for h in range(8):
            at = slice(h * HEAD, (h + 1) * HEAD)
            row = [wq[:, h * 128 : (h + 1) * 128], wk[:, at], wv[:, at], side]
            row = jnp.concatenate(row, axis=1).astype(BF)
            r.heads[h] = row
            r.wall[:, h * 256 : (h + 1) * 256] = row[:, :256]
        r.picks[pl.ds(0, 8)] = r.routes[...]
        r.picks[pl.ds(8, 8)] = jnp.broadcast_to(r.priority[...], (8, ROWS))

    greet((EP, LONG), pack)
    place = linear(CTX)
    spot, core, deep = lax.axis_index("x"), lax.axis_index("co"), lax.axis_index("z")
    yl, yh = lax.axis_index("yl"), lax.axis_index("yh")
    first, front = halves()

    def bring(source, target):
        copy = pltpu.make_async_copy(source, target, r.s_stage.at[0])
        copy.start()
        return copy

    send_picks = Send(
        CTX, lambda p: r.picks, lambda q: r.picks_to.at[q], lambda n: r.picks_to.at[pl.ds(0, n)], r.s_picks
    )
    cross_x = Send(
        ("yl",), lambda p: r.x, lambda q: r.x_to.at[q * 4 + spot], lambda n: r.x, r.s_x, own=False
    )
    send_x = Send(
        ("x",), lambda p: r.x, lambda q: r.x_to.at[yl * 4 + q], lambda n: r.x_to.at[pl.ds(0, n)], r.s_x
    )
    pass_x = Send(
        ("x",),
        lambda p: r.x_to.at[(1 - yl) * 4 + spot],
        lambda q: r.x_to.at[(1 - yl) * 4 + q],
        lambda n: r.x_to.at[pl.ds(0, n)],
        r.s_x,
    )
    send_heads = Send(
        CTX,
        lambda p: r.heads.at[p],
        lambda q: r.heads_to.at[q, yh, core, deep],
        lambda n: r.heads_to.at[pl.ds(0, n), yh, core, deep],
        r.s_heads,
    )
    pass_heads = Send(
        ("yh", "z"),
        lambda p: r.heads_to.at[:, yh, core, deep],
        lambda q: r.heads_to.at[:, lax.div(q, 4), core, lax.rem(q, 4)],
        lambda n: r.heads_to.at[pl.ds(0, n), :, :, pl.ds(0, 2)],
        r.s_heads_pass,
        own=False,
    )
    swap_heads = Send(
        ("co",),
        lambda p: r.heads_to.at[:, :, core],
        lambda q: r.heads_to.at[:, :, q],
        lambda n: r.heads_to.at[:, :, 0],
        r.s_heads_co,
        own=False,
    )
    send_gu = Send(
        ("yl", "z"),
        lambda p: r.w_gu.at[p],
        lambda q: r.wide_to.at[lax.div(q, 4), spot, lax.rem(q, 4), :, pl.ds(0, 2 * FF)],
        lambda n: r.w_gu.at[pl.ds(0, n)],
        r.s_gu,
    )
    send_dn = Send(
        ("yl", "z"),
        lambda p: r.w_dn.at[p],
        lambda q: r.wide_to.at[lax.div(q, 4), spot, lax.rem(q, 4), :, pl.ds(2 * FF, FF)],
        lambda n: r.w_dn.at[pl.ds(0, n)],
        r.s_dn,
    )
    pass_wide = Send(
        ("x",),
        lambda p: r.wide_to.at[:, spot],
        lambda q: r.wide_to.at[:, q],
        lambda n: r.wide_to.at[:, pl.ds(0, n)],
        r.s_wide,
        own=False,
    )
    send_out = Send(
        FLAT,
        lambda p: r.out,
        lambda q: r.out_to.at[q, core, spot],
        lambda n: r.out_to.at[pl.ds(0, n), core, spot],
        r.s_out,
    )
    pass_out = Send(
        ("x",),
        lambda p: r.out_to.at[:, core, spot],
        lambda q: r.out_to.at[:, core, q],
        lambda n: r.out_to.at[:, core, pl.ds(0, n)],
        r.s_out_x,
        own=False,
    )
    swap_out = Send(
        ("co",),
        lambda p: r.out_to.at[:, core],
        lambda q: r.out_to.at[:, q],
        lambda n: r.out_to.at[:, 0],
        r.s_out_co,
        own=False,
    )
    send_all = Send(
        FLAT,
        lambda p: r.wall,
        lambda q: r.wall_to.at[q, spot, core],
        lambda n: r.wall_to.at[pl.ds(0, n), 0, 0],
        r.s_all,
    )
    pass_all = Send(
        ("x",),
        lambda p: r.wall_to.at[:, spot, core],
        lambda q: r.wall_to.at[:, q, core],
        lambda n: r.wall_to.at[:, pl.ds(0, n), core],
        r.s_all_x,
        own=False,
    )
    swap_all = Send(
        ("co",),
        lambda p: r.wall_to.at[:, :, core],
        lambda q: r.wall_to.at[:, :, q],
        lambda n: r.wall_to.at[:, :, 0],
        r.s_all_co,
        own=False,
    )
    send_o = Send(
        CTX, lambda p: r.o_rows.at[p], lambda q: r.o_to.at[q], lambda n: r.o_to.at[pl.ds(0, n)], r.s_o
    )
    send_dz = Pairs(r.dz_rows, r.dz_to, r.s_dz)
    send_a2 = Pairs(r.a2_rows, r.a2_to, r.s_a2)
    send_gate = Pairs(r.gates, r.gates_to, r.s_gate)
    send_da = Pairs(r.a2_rows, r.da_to, r.s_da)
    send_dg = Pairs(r.dg_rows, r.dg_to, r.s_dg)
    send_y = Pairs(r.dz_rows, r.y_to, r.s_y)
    send_grad = Send(
        ("x",),
        lambda p: r.grad.at[:, p],
        lambda q: r.grad_to.at[:, q],
        lambda n: r.grad.at[:, pl.ds(0, n)],
        r.s_grad,
    )
    last_grad = Send(
        ("yl", "z"),
        lambda p: r.grad_mid.at[p],
        lambda q: r.grad_last.at[q],
        lambda n: r.grad_mid.at[pl.ds(0, n)],
        r.s_grad_last,
    )
    send_do = Send(
        CTX, lambda p: r.do_rows.at[p], lambda q: r.do_to.at[q], lambda n: r.do_to.at[pl.ds(0, n)], r.s_do
    )
    send_dq = Send(
        CTX,
        lambda p: r.dqkv.at[rows_of(p)],
        lambda q: r.dq_to.at[q],
        lambda n: r.dq_to.at[pl.ds(0, n)],
        r.s_dq,
    )
    swap_gwo = Send(
        ("co",), lambda p: r.out_to.at[:, p], lambda q: r.gwo_co, lambda n: r.gwo_co, r.s_gwo_co, own=False
    )
    pass_gwo = Send(
        ("x",),
        lambda p: r.gwo_mid.at[:, p],
        lambda q: r.gwo_x.at[:, q],
        lambda n: r.gwo_x.at[:, pl.ds(0, n)],
        r.s_gwo_x,
    )
    last_gwo = Send(
        FLAT,
        lambda p: r.gwo_sum.at[p],
        lambda q: r.gwo_last.at[q],
        lambda n: r.gwo_sum.at[pl.ds(0, n)],
        r.s_gwo,
    )
    swap_hg = Send(
        ("co",),
        lambda p: r.heads_to.at[:, :, p],
        lambda q: r.hg_co,
        lambda n: r.hg_co,
        r.s_hg_co,
        own=False,
    )
    pass_hg = Send(
        ("z",),
        lambda p: r.hg_mid.at[:, :, p],
        lambda q: r.hg_z.at[q],
        lambda n: r.hg_z.at[pl.ds(0, n)],
        r.s_hg_z,
    )
    last_hg = Send(
        LONG,
        lambda p: r.hg_sum.at[lax.div(p, 2), lax.rem(p, 2)],
        lambda q: r.hg_last.at[q],
        lambda n: r.hg_last.at[pl.ds(0, n)],
        r.s_hg,
    )

    send_picks.start()
    cross_x.copy(1, 4, 8).start()
    send_x.start_own(0)
    for i in range(1, 4):
        send_x.copy(i, i, 9).start()
    send_heads.start()
    send_out.start()
    send_gu.start()
    send_dn.start()

    send_picks.wait()
    drain(r.x, r.s_x.at[4])
    for i in range(1, 4):
        pass_x.copy(i, 4 + i, 10).start()
    mine = jnp.zeros((16, 128), I32)
    for p in range(8):
        mine = mine + r.picks_to[p] * (r.blocks[p] == place).astype(I32)
    expert = lax.broadcasted_iota(I32, (EXPERTS, ROWS), 0)
    named = jnp.zeros((EXPERTS, ROWS), jnp.bool_)
    for k in range(TOPK):
        named = named | (mine[k : k + 1] == expert)
    order = jnp.broadcast_to(mine[TOPK : TOPK + 1].astype(F32), (128, ROWS))
    before = (order.T < order).astype(F32).astype(BF)
    rank = jnp.where(named, dot(named.astype(F32).astype(BF), before), -1.0)
    seat = lax.broadcasted_iota(I32, (CAP, ROWS), 0).astype(F32)
    for e in range(EXPERTS):
        r.hot[pl.ds(e * CAP, CAP)] = (rank[e : e + 1] == seat).astype(F32)

    def runs(c):
        four = spin("co", lax.rem(c, 2)) * 8 + spin("yl", lax.div(c, 2)) * 4
        return four, four + 16

    def take(ref, c):
        return jnp.concatenate([ref[pl.ds(four, 4)] for four in runs(c)], axis=0)

    def put(ref, c, v):
        for n, four in enumerate(runs(c)):
            ref[pl.ds(four, 4)] = v[4 * n : 4 * n + 4]

    def stage(ref, c):
        for n, four in enumerate(runs(c)):
            pltpu.make_async_copy(
                ref.at[pl.ds(four, 4)], r.stage.at[pl.ds(4 * n, 4)], r.s_stage.at[0]
            ).start()

    def staged():
        drain(r.stage, r.s_stage.at[0])

    def hot_part(c):
        return jnp.concatenate(
            [r.hot[pl.ds(pl.multiple_of(four * CAP, 4 * CAP), 4 * CAP)] for four in runs(c)], axis=0
        )

    def fill(source, rows, c):
        part = dot(hot_part(c).astype(BF), source[...])
        put(rows, c, part.reshape(8, CAP, DIM).astype(BF))

    send_heads.wait()
    pass_heads.start()

    def fill_dz(c, carry):
        fill(r.dz, r.dz_rows, c)
        send_dz.start(c)
        return carry

    lax.fori_loop(0, 4, fill_dz, 0)
    send_all.start()
    pass_heads.wait()
    swap_heads.start()
    send_out.wait()
    pass_out.start()
    swap_heads.wait()

    packed = r.heads_to[...].astype(F32).reshape(128, 8, 384)
    r.w_heads[...] = packed[:, :, :256].reshape(DIM, 256).astype(BF)
    r.router[...] = packed[:, :, 256:].reshape(DIM, 128).astype(BF)
    gains = spread_gains(packed[:, 0, 256:].astype(BF))
    gain_one, gain_two, pair = gains[:, :DIM], gains[:, DIM : 2 * DIM], gains[:, 2 * DIM :]
    swapped = pltpu.roll(pair, HEAD, 1)
    gain_q, gain_k = jnp.where(first, pair, swapped), jnp.where(first, swapped, pair)
    ends = sequence_ends(r.lengths)
    lane = lax.broadcasted_iota(I32, (1, 128), 1)
    frequency = jnp.exp(
        lax.rem(lane, HEAD // 2).astype(F32) * (-2.0 * math.log(10000.0) / HEAD)
    )

    def project(j):
        at = rows_of(j)
        v = r.x_to[j].astype(F32)
        low = (v * rms(v) * gain_one).astype(BF)
        r.a_all[at] = low
        qkv = dot(low, r.w_heads[...])
        r.pre[at] = qkv
        token = j * ROWS + lax.broadcasted_iota(I32, (ROWS, 1), 0)
        angle = (token - starts(token, ends)).astype(F32) * frequency
        cos, sin = jnp.cos(angle), jnp.sin(angle)
        r.cos[at] = cos
        r.sin[at] = sin
        q, kv = qkv[:, :128], qkv[:, 128:]
        other = pltpu.roll(kv, HEAD, 1)
        k, val = jnp.where(first, kv, other), jnp.where(first, other, kv)
        r.qr[at] = turn_pair(q * head_rms(q, first) * gain_q, cos, sin, front).astype(BF)
        r.kr[at] = turn_pair(k * head_rms(k, first) * gain_k, cos, sin, front).astype(BF)
        r.vv[at] = val.astype(BF)

    def arrive(i, carry):
        @pl.when(i != 4)
        def _():
            drain(r.x, r.s_x.at[i])

        project(spin("yl", 2 - lax.div(i, 4)) * 4 + spin("x", 4 - lax.rem(i, 4)))
        return carry

    lax.fori_loop(0, 8, arrive, 0)
    drain(r.x, r.s_x.at[8])
    for n in (9, 10):
        drain(send_x.slots(3), r.s_x.at[n])

    def stacked(v):
        v = v.astype(F32)
        return jnp.concatenate(
            [jnp.where(first, v, 0.0), jnp.where(first, 0.0, v)], axis=0
        ).astype(BF)

    def beside(v):
        return jnp.where(first, v[:ROWS], v[ROWS:])

    def masked_scores(tile, q, width):
        scores = dot(q, r.kr[pl.ds(0, width)], ((1,), (1,))) * HEAD**-0.5
        token = tile * ROWS + lax.rem(lax.broadcasted_iota(I32, (2 * ROWS, 1), 0), ROWS)
        key = lax.broadcasted_iota(I32, (2 * ROWS, width), 1)
        return jnp.where((key <= token) & (key >= starts(token, ends)), scores, -1e30)

    for tile in range(8):
        width, at = ROWS * (tile + 1), rows_of(tile)
        scores = masked_scores(tile, stacked(r.qr[at]), width)
        top = jnp.max(scores, axis=1, keepdims=True)
        weight = jnp.exp(scores - top)
        total = jnp.sum(weight, axis=1, keepdims=True)
        result = beside(dot((weight * (1.0 / total)).astype(BF), r.vv[pl.ds(0, width)]))
        r.mixed[at] = result
        r.o_rows[tile] = result.astype(BF)
        r.level[at] = beside(jnp.broadcast_to(top + jnp.log(total), (2 * ROWS, 128)))
    send_o.start()
    send_gu.wait()
    send_dn.wait()
    pass_wide.start()
    pass_out.wait()
    swap_out.start()
    swap_out.wait()

    def lay(i, carry):
        rows = [
            r.out_to[pl.ds((lax.div(i, 4) * 2 + n // 2) * 4, 4), n % 2, lax.rem(i, 4)]
            for n in range(4)
        ]
        r.w_out[rows_of(i)] = merge(jnp.concatenate(rows, axis=0))
        return carry

    lax.fori_loop(0, 8, lay, 0)

    send_o.wait()
    for h in range(8):
        r.ob[:, h * 128 : (h + 1) * 128] = r.o_to[h]
    x_own = r.x[...].astype(F32)
    dz = r.dz[...].astype(F32)
    x1 = x_own + dot(r.ob[...], r.w_out[...], ((1,), (1,)))
    r.x1[...] = x1
    r2 = rms(x1)
    r.a2[...] = (x1 * r2 * gain_two).astype(BF)
    logits = dot(r.router[...], r.a2[...], ((0,), (1,)))[:EXPERTS]
    weight = jnp.exp(logits - jnp.max(logits, axis=0, keepdims=True))
    probs = weight / jnp.sum(weight, axis=0, keepdims=True)
    chosen = jnp.where(named, probs, 0.0)
    total = jnp.sum(chosen, axis=0, keepdims=True)
    gate = chosen / total
    for n in range(8):
        r.gate[n] = gate[4 * n : 4 * n + 4]
    r.gates[:, 0, :] = gate
    r.gates[:, 1, :] = rank
    send_gate.start_all()

    def fill_a2(c, carry):
        fill(r.a2, r.a2_rows, c)
        send_a2.start(c)
        return carry

    lax.fori_loop(0, 4, fill_a2, 0)
    send_all.wait()
    pass_all.start()
    pass_wide.wait()

    send_dz.all_sent()
    w_all = r.wide_to.reshape(DIM, WIDE)
    w_gu, w_dn = w_all.at[:, : 2 * FF], w_all.at[:, 2 * FF :]

    def work(c, carry):
        send_gate.arrived(c)
        send_dz.arrived(c)
        at = pl.ds(pl.multiple_of(c * PART, PART), PART)
        stage(r.dz_to, c)
        send_a2.arrived(c)
        a = merge(take(r.a2_to, c))
        r.a_rows[at] = a
        gu = dot(a, w_gu[...])
        g, up = gu[:, :FF], gu[:, FF:]
        s = 1.0 / (1.0 + jnp.exp(-g))
        hid = (g * s * up).astype(BF)
        r.hid[at] = hid
        note = take(r.gates_to, c)
        kept = note[:, 1:2] == seat[None]
        column = jnp.sum(jnp.where(kept, note[:, 0:1], 0.0), axis=2, keepdims=True)
        staged()
        dz_part = r.stage[...].astype(F32)
        dy = (dz_part * column).reshape(PART, DIM).astype(BF)
        r.dy[at] = dy
        dhid = dot(dy, w_dn[...])
        dgu = jnp.concatenate([dhid * up * s * (1.0 + g * (1.0 - s)), dhid * g * s], axis=1)
        dgu = dgu.astype(BF)
        r.dgu[at] = dgu
        da = dot(dgu, w_gu[...], ((1,), (1,)))
        send_a2.sent(c)
        put(r.a2_rows, c, da.reshape(8, CAP, DIM).astype(BF))
        send_da.start(c)
        y = dot(hid, w_dn[...], ((1,), (1,))).reshape(8, CAP, DIM).astype(BF)
        put(r.dz_rows, c, y)
        inner = jnp.sum(y.astype(F32) * dz_part, axis=2, keepdims=True)
        inner = jnp.sum(jnp.where(kept, inner, 0.0), axis=1, keepdims=True)
        put(r.dg_rows, c, jnp.broadcast_to(inner, (8, 8, ROWS)))
        send_dg.start(c)
        return carry

    lax.fori_loop(0, 4, work, 0)

    def weigh(i, carry):
        to = spin("x", i)
        for half in range(2):
            at = rows_of(half * 4 + to)
            gu = dot(r.a_rows[:, at], r.dgu[...], ((0,), (0,)))
            r.grad[half, to, :, :, : 2 * FF] = gu.astype(BF).reshape(4, 32, 2 * FF)
            dn = dot(r.dy[:, at], r.hid[...], ((0,), (0,)))
            r.grad[half, to, :, :, 2 * FF :] = dn.astype(BF).reshape(4, 32, FF)

        @pl.when(i < 4)
        def _():
            send_grad.copy(i).start()

        return carry

    lax.fori_loop(1, 5, weigh, 0)
    send_grad.start_own()

    pass_all.wait()
    swap_all.start()
    for c in range(4):
        send_dg.arrived(c)
    dgate = r.dg_to[:, 0, :]
    dc = jnp.where(named, dgate - jnp.sum(gate * dgate, axis=0, keepdims=True), 0.0) / total
    dl = probs * (dc - jnp.sum(probs * dc, axis=0, keepdims=True))
    dl = jnp.concatenate([dl, jnp.zeros((128 - EXPERTS, ROWS), F32)], axis=0).astype(BF)
    r.dl[...] = dl
    r.sum[...] = dot(dl, r.router[...], ((0,), (1,)))

    def unmix(c, carry):
        send_da.arrived(c)
        stage(r.da_to, c)
        staged()
        r.sum[...] += dot(hot_part(c).astype(BF), merge(r.stage[...]), ((0,), (0,)))
        return carry

    lax.fori_loop(0, 4, unmix, 0)
    send_y.start(0)
    send_y.start(1)
    dx_two, terms_two = norm_back(r.x1[...], rms(r.x1[...]), gain_two, r.sum[...])
    gain_two_grad = jnp.sum(terms_two, axis=0, keepdims=True)
    r.dx1[...] = dz + dx_two
    r.db[...] = r.dx1[...].astype(BF)
    do = dot(r.db[...], r.w_out[...]).astype(BF)
    for h in range(8):
        r.do_rows[h] = do[:, h * 128 : (h + 1) * 128]
    send_do.start()
    send_y.start(2)
    send_y.start(3)

    def spread_out(i, carry):
        part = dot(r.db[:, rows_of(i)], r.ob[...], ((0,), (0,)))
        part = part.reshape(2, 2, 4, 8, DIM).astype(BF)
        for n in range(4):
            at = pl.ds((lax.div(i, 4) * 2 + n // 2) * 4, 4)
            r.out_to[at, n % 2, lax.rem(i, 4)] = part[n // 2, n % 2]
        return carry

    lax.fori_loop(0, 8, spread_out, 0)
    swap_gwo.start()

    def add_core(i, carry):
        both = r.gwo_mid[i].astype(F32) + r.out_to[i, core].astype(F32)
        r.gwo_mid[i] = both.astype(BF)
        return carry

    send_do.wait()
    r.dk[...] = jnp.zeros_like(r.dk)
    r.dv[...] = jnp.zeros_like(r.dv)
    for tile in range(8):
        width, at = ROWS * (tile + 1), rows_of(tile)
        keys = pl.ds(0, width)
        q = stacked(r.qr[at])
        level = r.level[at]
        level = jnp.concatenate([level[:, :1], level[:, HEAD : HEAD + 1]], axis=0)
        probs_at = jnp.exp(masked_scores(tile, q, width) - level)
        do = r.do_to[tile]
        inner = head_mean(do.astype(F32) * r.mixed[at], first) * HEAD
        inner = jnp.concatenate([inner[:, :1], inner[:, HEAD : HEAD + 1]], axis=0)
        do = stacked(do)
        dp = dot(do, r.vv[keys], ((1,), (1,)))
        ds = (probs_at * (dp - inner)).astype(BF)
        r.dq[at] = beside(dot(ds, r.kr[keys])) * HEAD**-0.5
        r.dk[keys] += dot(ds, q, ((0,), (0,)))
        r.dv[keys] += dot(probs_at.astype(BF), do, ((0,), (0,)))

    swap_gwo.wait()
    bring(r.gwo_co, r.gwo_mid).wait()
    lax.fori_loop(0, 16, add_core, 0)
    r.gain_q_grad[...] = jnp.zeros_like(r.gain_q_grad)
    r.gain_k_grad[...] = jnp.zeros_like(r.gain_k_grad)

    def back(i, carry):
        j, _ = partner(CTX, lax.rem(i, 8))
        at = rows_of(j)
        cos, sin = r.cos[at], -r.sin[at]
        qkv = r.pre[at]
        q, kv = qkv[:, :128], qkv[:, 128:]
        k = jnp.where(first, kv, pltpu.roll(kv, HEAD, 1))
        dk, dv = r.dk[at] * HEAD**-0.5, r.dv[at]
        dk, dv = dk + pltpu.roll(dk, HEAD, 1), dv + pltpu.roll(dv, HEAD, 1)
        dq, terms = head_norm_back(q, gain_q, turn_pair(r.dq[at], cos, sin, front), first)
        r.gain_q_grad[...] += terms
        dk, terms = head_norm_back(k, gain_k, turn_pair(dk, cos, sin, front), first)
        r.gain_k_grad[...] += terms
        r.dqkv[at] = jnp.concatenate([dq, jnp.where(first, dk, dv)], axis=1).astype(BF)

        @pl.when(i < 8)
        def _():
            send_dq.copy(i).start()

        return carry

    lax.fori_loop(1, 9, back, 0)
    send_dq.start_own()
    send_grad.wait()
    bring(r.grad_to, r.wide_to).wait()

    def add_grad(i, carry):
        total = sum(r.wide_to[lax.div(i, 4), n, lax.rem(i, 4)].astype(F32) for n in range(4))
        r.grad_mid[i] = total.astype(BF)
        return carry

    lax.fori_loop(0, 8, add_grad, 0)
    last_grad.start()
    pass_gwo.start()

    diagonal = lax.broadcasted_iota(I32, (ROWS, 128), 0) == lax.broadcasted_iota(I32, (ROWS, 128), 1)

    def small(i, carry):
        at = rows_of(i)
        part = dot(r.a_all[:, at], r.dqkv[...], ((0,), (0,)))
        r.heads_to[i, :, :, :, :, pl.ds(0, 256)] = part.reshape(2, 2, 4, 8, 256).astype(BF)
        column = jnp.sum(part * r.w_heads[at].astype(F32), axis=1, keepdims=True)
        r.gain_one_grad[:, at] = jnp.sum(jnp.where(diagonal, column, 0.0), axis=0, keepdims=True)
        return carry

    lax.fori_loop(0, 8, small, 0)
    pair = jnp.where(
        first,
        r.gain_q_grad[...] + pltpu.roll(r.gain_q_grad[...], HEAD, 1),
        r.gain_k_grad[...],
    )
    gain_grads = pack_gains(
        jnp.concatenate([r.gain_one_grad[...] / gain_one, gain_two_grad, pair], axis=1)
    )
    side = jnp.where(
        lax.broadcasted_iota(I32, (128, 8, 128), 1) == 0, gain_grads[:, None], 0.0
    ).reshape(DIM, 128) + dot(r.a2[...], r.dl[...], ((0,), (1,)))
    r.heads_to[:, :, :, :, :, pl.ds(256, 128)] = side.reshape(8, 2, 2, 4, 8, 128).astype(BF)
    swap_hg.start()
    swap_hg.wait()
    r.hg_mid[...] = (r.heads_to[:, :, core].astype(F32) + r.hg_co[...].astype(F32)).astype(BF)
    pass_hg.start()

    send_dq.wait()
    swap_all.wait()
    for h in range(8):
        r.dq_all[:, h * 256 : (h + 1) * 256] = r.dq_to[h]

    def fetch(i):
        for n in range(4):
            pltpu.make_async_copy(
                r.wall_to.at[pl.ds((lax.div(i, 4) * 2 + n // 2) * 4, 4), lax.rem(i, 4), n % 2],
                r.wall_rows.at[lax.rem(i, 2), pl.ds(4 * n, 4)],
                r.s_fetch.at[lax.rem(i, 2)],
            ).start()

    fetch(0)

    def unproject(i, carry):
        @pl.when(i < 7)
        def _():
            fetch(i + 1)

        now = lax.rem(i, 2)
        drain(r.wall_rows.at[now], r.s_fetch.at[now])
        r.sum[:, rows_of(i)] = dot(r.dq_all[...], merge(r.wall_rows[now]), ((1,), (1,)))
        return carry

    lax.fori_loop(0, 8, unproject, 0)
    x_own = r.x[...].astype(F32)
    dx_one, _ = norm_back(x_own, rms(x_own), gain_one, r.sum[...])
    r.grad_inputs[...] = (r.dx1[...] + dx_one).astype(BF)

    pass_hg.wait()
    r.hg_sum[...] = sum(r.hg_z[n].astype(F32) for n in range(4)).astype(BF)
    last_hg.start()
    pass_gwo.wait()
    bring(r.gwo_x, r.out_to.at[:, 0]).wait()

    def add_spot(i, carry):
        total = sum(r.out_to[i, 0, n].astype(F32) for n in range(4))
        r.gwo_sum[i] = total.astype(BF)
        return carry

    lax.fori_loop(0, 16, add_spot, 0)
    last_gwo.start()

    r.sum[...] = r.x1[...]

    def gates_of(c):
        return jnp.concatenate([r.gate[lax.div(four, 4)] for four in runs(c)], axis=0)

    def mix(c, carry):
        send_y.arrived(c)
        stage(r.y_to, c)
        staged()
        y = merge(r.stage[...])
        weights = hot_part(c).reshape(8, CAP, ROWS) * gates_of(c)[:, None]
        weights = weights.reshape(PART, ROWS)
        high = weights.astype(BF)
        low = (weights - high.astype(F32)).astype(BF)
        r.sum[...] += dot(high, y, ((0,), (0,))) + dot(low, y, ((0,), (0,)))
        return carry

    lax.fori_loop(0, 4, mix, 0)
    r.output[...] = r.sum[...].astype(BF)
    for send in (last_gwo, last_grad, last_hg):
        send.wait()
    for send in (send_gate, send_da, send_dg, send_y):
        send.all_sent()


INPUTS = (
    ("lengths", pltpu.SMEM),
    ("blocks", pltpu.SMEM),
    ("x", pltpu.VMEM),
    ("dz", pltpu.VMEM),
    ("wq", pltpu.VMEM),
    ("wk", pltpu.VMEM),
    ("wv", pltpu.VMEM),
    ("wr", pltpu.VMEM),
    ("norm", pltpu.VMEM),
    ("out", pltpu.VMEM),
    ("routes", pltpu.VMEM),
    ("priority", pltpu.VMEM),
    ("w_gu", pl.ANY),
    ("w_dn", pl.ANY),
)
OUTPUTS = (
    ("output", (ROWS, DIM), BF),
    ("grad_inputs", (ROWS, DIM), BF),
)
ROW_SLOTS = (EXPERTS, CAP, DIM)
LANDING = (
    ("hg_last", (16, 8, 384), BF),
    ("gwo_last", (16, 8, DIM), BF),
    ("grad_last", (8, 32, WIDE), BF),
    ("dz_to", ROW_SLOTS, BF),
    ("y_to", ROW_SLOTS, BF),
    ("da_to", ROW_SLOTS, BF),
    ("grad_to", (2, 4, 4, 32, WIDE), BF),
    ("gwo_co", (16, 4, 8, DIM), BF),
    ("gwo_x", (16, 4, 8, DIM), BF),
    ("wall_to", (16, 4, 2, 8, 2 * DIM), BF),
)
SCRATCH = (
    ("heads", (8, 8, 384), BF),
    ("picks", (16, 128), I32),
    ("picks_to", (8, 16, 128), I32),
    ("x_to", (8, ROWS, DIM), BF),
    ("heads_to", (8, 2, 2, 4, 8, 384), BF),
    ("wide_to", (2, 4, 4, 32, WIDE), BF),
    ("out_to", (16, 2, 4, 8, DIM), BF),
    ("hot", (EXPERTS * CAP, ROWS), F32),
    ("wall", (8, 2 * DIM), BF),
    ("dz_rows", ROW_SLOTS, BF),
    ("a2_rows", ROW_SLOTS, BF),
    ("w_heads", (DIM, 256), BF),
    ("router", (DIM, 128), BF),
    ("a_all", (GTOK, DIM), BF),
    ("pre", (GTOK, 256), F32),
    ("cos", (GTOK, 128), F32),
    ("sin", (GTOK, 128), F32),
    ("qr", (GTOK, 128), BF),
    ("kr", (GTOK, 128), BF),
    ("vv", (GTOK, 128), BF),
    ("mixed", (GTOK, 128), F32),
    ("level", (GTOK, 128), F32),
    ("o_rows", (8, ROWS, 128), BF),
    ("o_to", (8, ROWS, 128), BF),
    ("w_out", (DIM, DIM), BF),
    ("ob", (ROWS, DIM), BF),
    ("x1", (ROWS, DIM), F32),
    ("a2", (ROWS, DIM), BF),
    ("gate", (8, 4, ROWS), F32),
    ("gates", (EXPERTS, 8, 128), F32),
    ("gates_to", (EXPERTS, 8, 128), F32),
    ("a2_to", ROW_SLOTS, BF),
    ("a_rows", (EXPERTS * CAP, DIM), BF),
    ("hid", (EXPERTS * CAP, FF), BF),
    ("dy", (EXPERTS * CAP, DIM), BF),
    ("dgu", (EXPERTS * CAP, 2 * FF), BF),
    ("dg_rows", (EXPERTS, 8, ROWS), F32),
    ("dg_to", (EXPERTS, 8, ROWS), F32),
    ("grad", (2, 4, 4, 32, WIDE), BF),
    ("grad_mid", (8, 32, WIDE), BF),
    ("stage", (8, CAP, DIM), BF),
    ("sum", (ROWS, DIM), F32),
    ("dl", (128, ROWS), BF),
    ("dx1", (ROWS, DIM), F32),
    ("db", (ROWS, DIM), BF),
    ("do_rows", (8, ROWS, 128), BF),
    ("do_to", (8, ROWS, 128), BF),
    ("gwo_mid", (16, 4, 8, DIM), BF),
    ("gwo_sum", (16, 8, DIM), BF),
    ("dq", (GTOK, 128), F32),
    ("dk", (GTOK, 128), F32),
    ("dv", (GTOK, 128), F32),
    ("dqkv", (GTOK, 256), BF),
    ("dq_to", (8, ROWS, 256), BF),
    ("dq_all", (ROWS, 2 * DIM), BF),
    ("wall_rows", (2, 16, 8, 2 * DIM), BF),
    ("gain_one_grad", (1, DIM), F32),
    ("gain_q_grad", (1, 128), F32),
    ("gain_k_grad", (1, 128), F32),
    ("hg_co", (8, 2, 4, 8, 384), BF),
    ("hg_mid", (8, 2, 4, 8, 384), BF),
    ("hg_z", (4, 8, 2, 8, 384), BF),
    ("hg_sum", (8, 2, 8, 384), BF),
)
SEMS = dict(s_stage=1, s_fetch=2, s_x=11)
PAIR_SEMS = ("s_dz", "s_a2", "s_gate", "s_da", "s_dg", "s_y")
SEMS.update(dict.fromkeys(PAIR_SEMS, 8))
SEND_SEMS = (
    "s_picks",
    "s_heads",
    "s_heads_pass",
    "s_heads_co",
    "s_gu",
    "s_dn",
    "s_wide",
    "s_out",
    "s_out_x",
    "s_out_co",
    "s_all",
    "s_all_x",
    "s_all_co",
    "s_o",
    "s_grad",
    "s_grad_last",
    "s_do",
    "s_dq",
    "s_gwo_co",
    "s_gwo_x",
    "s_gwo",
    "s_hg_co",
    "s_hg_z",
    "s_hg",
)
SEMS.update(dict.fromkeys(SEND_SEMS, 2))


def layer(*operands):
    names = [name for name, *_ in INPUTS + OUTPUTS + LANDING + SCRATCH] + list(SEMS)

    def body(*refs):
        layer_kernel(types.SimpleNamespace(**dict(zip(names, refs))))

    return pl.pallas_call(
        body,
        out_shape=[jax.ShapeDtypeStruct(shape, kind) for _, shape, kind in OUTPUTS + LANDING],
        in_specs=[pl.BlockSpec(memory_space=space) for _, space in INPUTS],
        out_specs=[pl.BlockSpec(memory_space=pltpu.VMEM)] * len(OUTPUTS)
        + [pl.BlockSpec(memory_space=pl.ANY)] * len(LANDING),
        scratch_shapes=[pltpu.VMEM(shape, kind) for _, shape, kind in SCRATCH]
        + [pltpu.SemaphoreType.DMA((n,)) for n in SEMS.values()],
        compiler_params=pltpu.CompilerParams(
            collective_id=0, has_side_effects=True, vmem_limit_bytes=VMEM_LIMIT
        ),
        name="layer",
    )(*operands)


VMEM_LIMIT = 63 << 20


def finish_kernel(
    output, grad_inputs, hg, gwo, experts, o_output, o_inputs, o_q, o_k, o_v, o_out, o_router, o_gains, o_gu, o_dn
):
    o_output[...] = output[...]
    o_inputs[...] = grad_inputs[...]
    heads = [hg[2 * c].astype(F32) + hg[2 * c + 1].astype(F32) for c in range(8)]
    for c in range(8):
        o_q[:, c * 128 : (c + 1) * 128] = heads[c][:, :128]
    for c in range(4):
        at, two = slice(c * 128, (c + 1) * 128), heads[2 * c : 2 * c + 2]
        o_k[:, at] = jnp.concatenate([head[:, 128:192] for head in two], axis=1)
        o_v[:, at] = jnp.concatenate([head[:, 192:256] for head in two], axis=1)
    side = sum(head[:, 256:] for head in heads)
    o_router[...] = side[:, :EXPERTS]
    o_gains[...] = side[:1, EXPERTS : EXPERTS + GAINS]
    o_out[...] = sum(gwo[n].astype(F32) for n in range(16))
    o_gu[...] = experts[:, :, : 2 * FF].astype(F32)
    o_dn[...] = experts[:, :, 2 * FF :].astype(F32)


def finish(*operands):
    shapes = (
        ((ROWS, DIM), BF),
        ((ROWS, DIM), BF),
        ((8, HEADS * HEAD), F32),
        ((8, KV_HEADS * HEAD), F32),
        ((8, KV_HEADS * HEAD), F32),
        ((8, DIM), F32),
        ((8, EXPERTS), F32),
        ((1, GAINS), F32),
        ((8, 32, 2 * FF), F32),
        ((8, 32, FF), F32),
    )
    vmem = pl.BlockSpec(memory_space=pltpu.VMEM)
    return pl.pallas_call(
        finish_kernel,
        out_shape=[jax.ShapeDtypeStruct(shape, kind) for shape, kind in shapes],
        in_specs=[vmem] * len(operands),
        out_specs=[vmem] * len(shapes),
        compiler_params=pltpu.CompilerParams(vmem_limit_bytes=VMEM_LIMIT),
        name="finish",
    )(*operands)


def shards(
    inputs,
    cotangent,
    w_query,
    key_weight,
    value_weight,
    w_output,
    w_router,
    norm_gains,
    w_gate_up,
    w_down,
    seq_lengths,
    block_map,
    routes,
    priority,
):
    output, grad_inputs, hg, gwo, experts, *_ = layer(
        seq_lengths[0],
        block_map[0],
        inputs[0],
        cotangent[0],
        w_query,
        key_weight,
        value_weight,
        w_router,
        norm_gains[None],
        w_output.T,
        routes[0].T,
        priority[0],
        w_gate_up,
        jnp.swapaxes(w_down, 1, 2),
    )
    output, grad_inputs, q, k, v, out, router, gains, gate_up, down = finish(
        output, grad_inputs, hg, gwo, experts
    )
    return (
        output[None],
        grad_inputs[None],
        q,
        k,
        v,
        out.T,
        router,
        gains[0],
        gate_up,
        jnp.swapaxes(down, 1, 2),
    )


def solution(mesh):
    groups = ("yh", "co", "z")
    specs = (
        P(groups, CTX, None),
        P(groups, CTX, None),
        P(ALL, None),
        P(ALL, None),
        P(ALL, None),
        P(None, ALL),
        P(ALL, None),
        P(ALL),
        P(("yh", "co"), WT, None),
        P(("yh", "co"), None, WT),
        P(groups, None),
        P(groups, None),
        P(groups, CTX, None),
        P(groups, CTX, None),
    )
    return jax.shard_map(
        shards,
        mesh=Mesh(mesh.devices.reshape(SIZES), ALL),
        in_specs=specs,
        out_specs=specs[:10],
        check_vma=False,
    )
```

```python
import math
import types

import jax
import jax.numpy as jnp
from jax import lax
from jax.experimental import pallas as pl
from jax.experimental.pallas import tpu as pltpu
from jax.sharding import Mesh
from jax.sharding import PartitionSpec as P

HEADS = 16
KV_HEADS = 8
DIM = 1024
HEAD = 64
FF = 512
EXPERTS = 32
TOPK = 8
ROWS = 128
GTOK = 1024
CAP = 40
GAINS = 17
WIDE = 3 * FF
PART = 8 * CAP
BF = jnp.bfloat16
F32 = jnp.float32
I32 = jnp.int32

ALL = ("yl", "x", "yh", "co", "z")
SIZES = (2, 4, 2, 2, 4)
SPAN = dict(zip(ALL, SIZES))
CTX = ("yl", "x")
EP = ("yh", "co", "yl", "z")
WT = ("yl", "x", "z")
LONG = ("yl", "x", "yh")
FLAT = ("yl", "yh", "z")


def linear(axes):
    index = 0
    for axis in axes:
        index = index * SPAN[axis] + lax.axis_index(axis)
    return index


def spin(axis, step):
    at = lax.axis_index(axis)
    return at if isinstance(step, int) and step == 0 else lax.rem(at + step, SPAN[axis])


def partner(axes, i):
    steps, at, index = {}, {}, 0
    for axis in reversed(axes):
        if isinstance(i, int):
            steps[axis], i = i % SPAN[axis], i // SPAN[axis]
        else:
            steps[axis], i = lax.rem(i, SPAN[axis]), lax.div(i, SPAN[axis])
    for axis in axes:
        at[axis] = spin(axis, steps[axis])
        index = index * SPAN[axis] + at[axis]
    return index, tuple(at[axis] if axis in at else lax.axis_index(axis) for axis in ALL)


def count(axes):
    return math.prod(SPAN[axis] for axis in axes)


def greet(sets, meanwhile):
    barrier = pltpu.get_barrier_semaphore()
    for axes in sets:
        for i in range(1, count(axes)):
            pl.semaphore_signal(
                barrier,
                inc=1,
                device_id=partner(axes, i)[1],
                device_id_type=pl.DeviceIdType.MESH,
            )
    meanwhile()
    pl.semaphore_wait(barrier, sum(count(axes) - 1 for axes in sets))


def remote(source, target, send_sem, recv_sem, to):
    return pltpu.make_async_remote_copy(
        src_ref=source,
        dst_ref=target,
        send_sem=send_sem,
        recv_sem=recv_sem,
        device_id=to,
        device_id_type=pl.DeviceIdType.MESH,
    )


def drain(span, sem):
    pltpu.make_async_copy(span, span, sem).wait()


class Send:
    def __init__(self, axes, part, slot, slots, sems, own=True):
        self.axes, self.part, self.slot, self.slots = axes, part, slot, slots
        self.sems, self.own, self.n, self.me = sems, own, count(axes), linear(axes)

    def copy(self, i, arrival=1, departure=0):
        place, to = partner(self.axes, i)
        send_sem, recv_sem = self.sems.at[departure], self.sems.at[arrival]
        return remote(self.part(place), self.slot(self.me), send_sem, recv_sem, to)

    def start_own(self, arrival=1):
        pltpu.make_async_copy(
            self.part(self.me), self.slot(self.me), self.sems.at[arrival]
        ).start()

    def start(self):
        if self.own:
            self.start_own()
        for i in range(1, self.n):
            self.copy(i).start()

    def arrived(self):
        drain(self.slots(self.n if self.own else self.n - 1), self.sems.at[1])

    def sent(self):
        drain(self.slots(self.n - 1), self.sems.at[0])

    def wait(self):
        self.arrived()
        self.sent()


class Pairs:
    def __init__(self, blocks, landing, sems):
        self.blocks, self.landing, self.sems, self.me = blocks, landing, sems, linear(EP)

    def start(self, c):
        yl, co = spin("yl", lax.div(c, 2)), spin("co", lax.rem(c, 2))
        for j in range(8):
            yh, z = spin("yh", j // 4), spin("z", j % 4)
            place = ((yh * 2 + co) * 2 + yl) * 4 + z
            copy = remote(
                self.blocks.at[place],
                self.landing.at[self.me],
                self.sems.at[4 + c],
                self.sems.at[c],
                (yl, lax.axis_index("x"), yh, co, z),
            )
            if j > 0:
                copy.start()
                continue

            @pl.when(c > 0)
            def _(copy=copy):
                copy.start()

            @pl.when(c == 0)
            def _():
                pltpu.make_async_copy(
                    self.blocks.at[self.me], self.landing.at[self.me], self.sems.at[0]
                ).start()

    def start_all(self):
        def one(c, carry):
            self.start(c)
            return carry

        lax.fori_loop(0, 4, one, 0)

    def arrived(self, c):
        drain(self.landing.at[pl.ds(0, 8)], self.sems.at[c])

    def sent(self, c):
        @pl.when(c > 0)
        def _():
            drain(self.blocks.at[pl.ds(0, 8)], self.sems.at[4 + c])

        @pl.when(c == 0)
        def _():
            drain(self.blocks.at[pl.ds(0, 7)], self.sems.at[4])

    def all_sent(self):
        def one(c, carry):
            self.sent(c)
            return carry

        lax.fori_loop(0, 4, one, 0)


def dot(left, right, dims=((1,), (0,))):
    return lax.dot_general(left, right, (dims, ((), ())), preferred_element_type=F32)


def rms(v):
    return lax.rsqrt(jnp.mean(v * v, axis=-1, keepdims=True) + 1e-06)


def norm_back(v, scale, gain, upstream):
    weighted = upstream * gain
    inner = jnp.mean(weighted * v, axis=-1, keepdims=True)
    return scale * weighted - v * (scale * scale * scale) * inner, upstream * v * scale


def halves():
    lane = lax.broadcasted_iota(I32, (1, 128), 1)
    return lane < HEAD, lax.rem(lane, HEAD) < HEAD // 2


def head_mean(v, first):
    low = jnp.sum(jnp.where(first, v, 0.0), axis=1, keepdims=True)
    high = jnp.sum(jnp.where(first, 0.0, v), axis=1, keepdims=True)
    return jnp.where(first, low, high) * (1.0 / HEAD)


def head_rms(v, first):
    return lax.rsqrt(head_mean(v * v, first) + 1e-06)


def head_norm_back(v, gain, upstream, first):
    scale = head_rms(v, first)
    weighted = upstream * gain
    inner = head_mean(weighted * v, first)
    terms = jnp.sum(upstream * v * scale, axis=0, keepdims=True)
    return scale * weighted - v * (scale * scale * scale) * inner, terms


def turn_pair(v, cos, sin, front):
    return v * cos + jnp.where(front, -pltpu.roll(v, 96, 1), pltpu.roll(v, 32, 1)) * sin


def starts(tokens, ends):
    first = jnp.zeros_like(tokens)
    for end in ends:
        first = jnp.maximum(first, jnp.where(tokens >= end, end, 0))
    return first


def sequence_ends(lengths):
    ends, total = [], 0
    for i in range(3):
        total = total + lengths[i]
        ends.append(total)
    return ends


def gain_places():
    column = lax.broadcasted_iota(I32, (128, 128 * GAINS), 1)
    row = lax.broadcasted_iota(I32, (128, 128 * GAINS), 0)
    owner = (column * 3856) >> 16
    return row == owner, row == EXPERTS + column - owner * GAINS


def spread_gains(packed):
    owner, lane = gain_places()
    rows = dot(packed, owner.astype(F32).astype(BF), ((0,), (0,)))
    return jnp.sum(jnp.where(lane, rows, 0.0), axis=0, keepdims=True)


def pack_gains(row):
    owner, lane = gain_places()
    return dot(
        owner.astype(F32).astype(BF), jnp.where(lane, row, 0.0).astype(BF), ((1,), (1,))
    )


def merge(v):
    shape = v.shape
    return v.astype(F32).reshape(math.prod(shape[:-1]), shape[-1]).astype(BF)


def rows_of(j):
    return pl.ds(j * ROWS if isinstance(j, int) else pl.multiple_of(j * ROWS, ROWS), ROWS)


def layer_kernel(r):
    def pack():
        wq, wk, wv, wr, gains = (
            ref[...].astype(F32) for ref in (r.wq, r.wk, r.wv, r.wr, r.norm)
        )
        gains = jnp.concatenate([gains, jnp.zeros((7, GAINS), F32)], axis=0)
        side = jnp.concatenate([wr, gains, jnp.zeros((8, 96 - GAINS), F32)], axis=1)
        for h in range(8):
            at = slice(h * HEAD, (h + 1) * HEAD)
            row = [wq[:, h * 128 : (h + 1) * 128], wk[:, at], wv[:, at], side]
            row = jnp.concatenate(row, axis=1).astype(BF)
            r.heads[h] = row
            r.wall[:, h * 256 : (h + 1) * 256] = row[:, :256]
        r.picks[pl.ds(0, 8)] = r.routes[...]
        r.picks[pl.ds(8, 8)] = jnp.broadcast_to(r.priority[...], (8, ROWS))

    greet((EP, LONG), pack)
    place = linear(CTX)
    spot, core, deep = lax.axis_index("x"), lax.axis_index("co"), lax.axis_index("z")
    yl, yh = lax.axis_index("yl"), lax.axis_index("yh")
    first, front = halves()

    def bring(source, target):
        copy = pltpu.make_async_copy(source, target, r.s_stage.at[0])
        copy.start()
        return copy

    send_picks = Send(
        CTX, lambda p: r.picks, lambda q: r.picks_to.at[q], lambda n: r.picks_to.at[pl.ds(0, n)], r.s_picks
    )
    cross_x = Send(
        ("yl",), lambda p: r.x, lambda q: r.x_to.at[q * 4 + spot], lambda n: r.x, r.s_x, own=False
    )
    send_x = Send(
        ("x",), lambda p: r.x, lambda q: r.x_to.at[yl * 4 + q], lambda n: r.x_to.at[pl.ds(0, n)], r.s_x
    )
    pass_x = Send(
        ("x",),
        lambda p: r.x_to.at[(1 - yl) * 4 + spot],
        lambda q: r.x_to.at[(1 - yl) * 4 + q],
        lambda n: r.x_to.at[pl.ds(0, n)],
        r.s_x,
    )
    send_heads = Send(
        CTX,
        lambda p: r.heads.at[p],
        lambda q: r.heads_to.at[q, yh, core, deep],
        lambda n: r.heads_to.at[pl.ds(0, n), yh, core, deep],
        r.s_heads,
    )
    pass_heads = Send(
        ("yh", "z"),
        lambda p: r.heads_to.at[:, yh, core, deep],
        lambda q: r.heads_to.at[:, lax.div(q, 4), core, lax.rem(q, 4)],
        lambda n: r.heads_to.at[pl.ds(0, n), :, :, pl.ds(0, 2)],
        r.s_heads_pass,
        own=False,
    )
    swap_heads = Send(
        ("co",),
        lambda p: r.heads_to.at[:, :, core],
        lambda q: r.heads_to.at[:, :, q],
        lambda n: r.heads_to.at[:, :, 0],
        r.s_heads_co,
        own=False,
    )
    send_gu = Send(
        ("yl", "z"),
        lambda p: r.w_gu.at[p],
        lambda q: r.wide_to.at[lax.div(q, 4), spot, lax.rem(q, 4), :, pl.ds(0, 2 * FF)],
        lambda n: r.w_gu.at[pl.ds(0, n)],
        r.s_gu,
    )
    send_dn = Send(
        ("yl", "z"),
        lambda p: r.w_dn.at[p],
        lambda q: r.wide_to.at[lax.div(q, 4), spot, lax.rem(q, 4), :, pl.ds(2 * FF, FF)],
        lambda n: r.w_dn.at[pl.ds(0, n)],
        r.s_dn,
    )
    pass_wide = Send(
        ("x",),
        lambda p: r.wide_to.at[:, spot],
        lambda q: r.wide_to.at[:, q],
        lambda n: r.wide_to.at[:, pl.ds(0, n)],
        r.s_wide,
        own=False,
    )
    send_out = Send(
        FLAT,
        lambda p: r.out,
        lambda q: r.out_to.at[q, core, spot],
        lambda n: r.out_to.at[pl.ds(0, n), core, spot],
        r.s_out,
    )
    pass_out = Send(
        ("x",),
        lambda p: r.out_to.at[:, core, spot],
        lambda q: r.out_to.at[:, core, q],
        lambda n: r.out_to.at[:, core, pl.ds(0, n)],
        r.s_out_x,
        own=False,
    )
    swap_out = Send(
        ("co",),
        lambda p: r.out_to.at[:, core],
        lambda q: r.out_to.at[:, q],
        lambda n: r.out_to.at[:, 0],
        r.s_out_co,
        own=False,
    )
    send_all = Send(
        FLAT,
        lambda p: r.wall,
        lambda q: r.wall_to.at[q, spot, core],
        lambda n: r.wall_to.at[pl.ds(0, n), 0, 0],
        r.s_all,
    )
    pass_all = Send(
        ("x",),
        lambda p: r.wall_to.at[:, spot, core],
        lambda q: r.wall_to.at[:, q, core],
        lambda n: r.wall_to.at[:, pl.ds(0, n), core],
        r.s_all_x,
        own=False,
    )
    swap_all = Send(
        ("co",),
        lambda p: r.wall_to.at[:, :, core],
        lambda q: r.wall_to.at[:, :, q],
        lambda n: r.wall_to.at[:, :, 0],
        r.s_all_co,
        own=False,
    )
    send_o = Send(
        CTX, lambda p: r.o_rows.at[p], lambda q: r.o_to.at[q], lambda n: r.o_to.at[pl.ds(0, n)], r.s_o
    )
    send_dz = Pairs(r.dz_rows, r.dz_to, r.s_dz)
    send_a2 = Pairs(r.a2_rows, r.a2_to, r.s_a2)
    send_gate = Pairs(r.gates, r.gates_to, r.s_gate)
    send_da = Pairs(r.a2_rows, r.da_to, r.s_da)
    send_dg = Pairs(r.dg_rows, r.dg_to, r.s_dg)
    send_y = Pairs(r.dz_rows, r.y_to, r.s_y)
    send_grad = Send(
        ("x",),
        lambda p: r.grad.at[:, p],
        lambda q: r.grad_to.at[:, q],
        lambda n: r.grad.at[:, pl.ds(0, n)],
        r.s_grad,
    )
    last_grad = Send(
        ("yl", "z"),
        lambda p: r.grad_mid.at[p],
        lambda q: r.grad_last.at[q],
        lambda n: r.grad_mid.at[pl.ds(0, n)],
        r.s_grad_last,
    )
    send_do = Send(
        CTX, lambda p: r.do_rows.at[p], lambda q: r.do_to.at[q], lambda n: r.do_to.at[pl.ds(0, n)], r.s_do
    )
    send_dq = Send(
        CTX,
        lambda p: r.dqkv.at[rows_of(p)],
        lambda q: r.dq_to.at[q],
        lambda n: r.dq_to.at[pl.ds(0, n)],
        r.s_dq,
    )
    swap_gwo = Send(
        ("co",), lambda p: r.out_to.at[:, p], lambda q: r.gwo_co, lambda n: r.gwo_co, r.s_gwo_co, own=False
    )
    pass_gwo = Send(
        ("x",),
        lambda p: r.gwo_mid.at[:, p],
        lambda q: r.gwo_x.at[:, q],
        lambda n: r.gwo_x.at[:, pl.ds(0, n)],
        r.s_gwo_x,
    )
    last_gwo = Send(
        FLAT,
        lambda p: r.gwo_sum.at[p],
        lambda q: r.gwo_last.at[q],
        lambda n: r.gwo_sum.at[pl.ds(0, n)],
        r.s_gwo,
    )
    swap_hg = Send(
        ("co",),
        lambda p: r.heads_to.at[:, :, p],
        lambda q: r.hg_co,
        lambda n: r.hg_co,
        r.s_hg_co,
        own=False,
    )
    pass_hg = Send(
        ("z",),
        lambda p: r.hg_mid.at[:, :, p],
        lambda q: r.hg_z.at[q],
        lambda n: r.hg_z.at[pl.ds(0, n)],
        r.s_hg_z,
    )
    last_hg = Send(
        LONG,
        lambda p: r.hg_sum.at[lax.div(p, 2), lax.rem(p, 2)],
        lambda q: r.hg_last.at[q],
        lambda n: r.hg_last.at[pl.ds(0, n)],
        r.s_hg,
    )

    send_picks.start()
    cross_x.copy(1, 4, 8).start()
    send_x.start_own(0)
    for i in range(1, 4):
        send_x.copy(i, i, 9).start()
    send_heads.start()
    send_out.start()
    send_gu.start()
    send_dn.start()

    send_picks.wait()
    drain(r.x, r.s_x.at[4])
    for i in range(1, 4):
        pass_x.copy(i, 4 + i, 10).start()
    mine = jnp.zeros((16, 128), I32)
    for p in range(8):
        mine = mine + r.picks_to[p] * (r.blocks[p] == place).astype(I32)
    expert = lax.broadcasted_iota(I32, (EXPERTS, ROWS), 0)
    named = jnp.zeros((EXPERTS, ROWS), jnp.bool_)
    for k in range(TOPK):
        named = named | (mine[k : k + 1] == expert)
    order = jnp.broadcast_to(mine[TOPK : TOPK + 1].astype(F32), (128, ROWS))
    before = (order.T < order).astype(F32).astype(BF)
    rank = jnp.where(named, dot(named.astype(F32).astype(BF), before), -1.0)
    seat = lax.broadcasted_iota(I32, (CAP, ROWS), 0).astype(F32)
    for e in range(EXPERTS):
        r.hot[pl.ds(e * CAP, CAP)] = (rank[e : e + 1] == seat).astype(F32)

    def runs(c):
        four = spin("co", lax.rem(c, 2)) * 8 + spin("yl", lax.div(c, 2)) * 4
        return four, four + 16

    def take(ref, c):
        return jnp.concatenate([ref[pl.ds(four, 4)] for four in runs(c)], axis=0)

    def put(ref, c, v):
        for n, four in enumerate(runs(c)):
            ref[pl.ds(four, 4)] = v[4 * n : 4 * n + 4]

    def stage(ref, c):
        for n, four in enumerate(runs(c)):
            pltpu.make_async_copy(
                ref.at[pl.ds(four, 4)], r.stage.at[pl.ds(4 * n, 4)], r.s_stage.at[0]
            ).start()

    def staged():
        drain(r.stage, r.s_stage.at[0])

    def hot_part(c):
        return jnp.concatenate(
            [r.hot[pl.ds(pl.multiple_of(four * CAP, 4 * CAP), 4 * CAP)] for four in runs(c)], axis=0
        )

    def fill(source, rows, c):
        part = dot(hot_part(c).astype(BF), source[...])
        put(rows, c, part.reshape(8, CAP, DIM).astype(BF))

    send_heads.wait()
    pass_heads.start()

    def fill_dz(c, carry):
        fill(r.dz, r.dz_rows, c)

        @pl.when(c < 3)
        def _():
            send_dz.start(c)

        return carry

    lax.fori_loop(0, 4, fill_dz, 0)
    send_all.start()
    pass_heads.wait()
    swap_heads.start()
    send_out.wait()
    pass_out.start()
    swap_heads.wait()

    packed = r.heads_to[...].astype(F32).reshape(128, 8, 384)
    r.w_heads[...] = packed[:, :, :256].reshape(DIM, 256).astype(BF)
    r.router[...] = packed[:, :, 256:].reshape(DIM, 128).astype(BF)
    gains = spread_gains(packed[:, 0, 256:].astype(BF))
    gain_one, gain_two, pair = gains[:, :DIM], gains[:, DIM : 2 * DIM], gains[:, 2 * DIM :]
    swapped = pltpu.roll(pair, HEAD, 1)
    gain_q, gain_k = jnp.where(first, pair, swapped), jnp.where(first, swapped, pair)
    ends = sequence_ends(r.lengths)
    lane = lax.broadcasted_iota(I32, (1, 128), 1)
    frequency = jnp.exp(
        lax.rem(lane, HEAD // 2).astype(F32) * (-2.0 * math.log(10000.0) / HEAD)
    )

    def project(j):
        at = rows_of(j)
        v = r.x_to[j].astype(F32)
        low = (v * rms(v) * gain_one).astype(BF)
        r.a_all[at] = low
        qkv = dot(low, r.w_heads[...])
        r.pre[at] = qkv
        token = j * ROWS + lax.broadcasted_iota(I32, (ROWS, 1), 0)
        angle = (token - starts(token, ends)).astype(F32) * frequency
        cos, sin = jnp.cos(angle), jnp.sin(angle)
        r.cos[at] = cos
        r.sin[at] = sin
        q, kv = qkv[:, :128], qkv[:, 128:]
        other = pltpu.roll(kv, HEAD, 1)
        k, val = jnp.where(first, kv, other), jnp.where(first, other, kv)
        r.qr[at] = turn_pair(q * head_rms(q, first) * gain_q, cos, sin, front).astype(BF)
        r.kr[at] = turn_pair(k * head_rms(k, first) * gain_k, cos, sin, front).astype(BF)
        r.vv[at] = val.astype(BF)

    def arrive(i, carry):
        @pl.when(i != 4)
        def _():
            drain(r.x, r.s_x.at[i])

        project(spin("yl", 2 - lax.div(i, 4)) * 4 + spin("x", 4 - lax.rem(i, 4)))
        return carry

    lax.fori_loop(0, 8, arrive, 0)
    drain(r.x, r.s_x.at[8])
    for n in (9, 10):
        drain(send_x.slots(3), r.s_x.at[n])

    def stacked(v):
        v = v.astype(F32)
        return jnp.concatenate(
            [jnp.where(first, v, 0.0), jnp.where(first, 0.0, v)], axis=0
        ).astype(BF)

    def beside(v):
        return jnp.where(first, v[:ROWS], v[ROWS:])

    def masked_scores(tile, q, width):
        scores = dot(q, r.kr[pl.ds(0, width)], ((1,), (1,))) * HEAD**-0.5
        token = tile * ROWS + lax.rem(lax.broadcasted_iota(I32, (2 * ROWS, 1), 0), ROWS)
        key = lax.broadcasted_iota(I32, (2 * ROWS, width), 1)
        return jnp.where((key <= token) & (key >= starts(token, ends)), scores, -1e30)

    for tile in range(8):
        width, at = ROWS * (tile + 1), rows_of(tile)
        scores = masked_scores(tile, stacked(r.qr[at]), width)
        top = jnp.max(scores, axis=1, keepdims=True)
        weight = jnp.exp(scores - top)
        total = jnp.sum(weight, axis=1, keepdims=True)
        result = beside(dot((weight * (1.0 / total)).astype(BF), r.vv[pl.ds(0, width)]))
        r.mixed[at] = result
        r.o_rows[tile] = result.astype(BF)
        r.level[at] = beside(jnp.broadcast_to(top + jnp.log(total), (2 * ROWS, 128)))
    send_o.start()
    send_gu.wait()
    send_dn.wait()
    pass_wide.start()
    pass_out.wait()
    swap_out.start()
    swap_out.wait()

    def lay(i, carry):
        rows = [
            r.out_to[pl.ds((lax.div(i, 4) * 2 + n // 2) * 4, 4), n % 2, lax.rem(i, 4)]
            for n in range(4)
        ]
        r.w_out[rows_of(i)] = merge(jnp.concatenate(rows, axis=0))
        return carry

    lax.fori_loop(0, 8, lay, 0)

    send_o.wait()
    for h in range(8):
        r.ob[:, h * 128 : (h + 1) * 128] = r.o_to[h]
    x_own = r.x[...].astype(F32)
    dz = r.dz[...].astype(F32)
    x1 = x_own + dot(r.ob[...], r.w_out[...], ((1,), (1,)))
    r.x1[...] = x1
    r2 = rms(x1)
    r.a2[...] = (x1 * r2 * gain_two).astype(BF)
    logits = dot(r.router[...], r.a2[...], ((0,), (1,)))[:EXPERTS]
    weight = jnp.exp(logits - jnp.max(logits, axis=0, keepdims=True))
    probs = weight / jnp.sum(weight, axis=0, keepdims=True)
    chosen = jnp.where(named, probs, 0.0)
    total = jnp.sum(chosen, axis=0, keepdims=True)
    gate = chosen / total
    for n in range(8):
        r.gate[n] = gate[4 * n : 4 * n + 4]
    r.gates[:, 0, :] = gate
    r.gates[:, 1, :] = rank
    send_gate.start_all()

    def fill_a2(c, carry):
        fill(r.a2, r.a2_rows, c)
        send_a2.start(c)

        @pl.when(c == 2)
        def _():
            send_dz.start(3)

        return carry

    lax.fori_loop(0, 4, fill_a2, 0)
    send_all.wait()
    pass_all.start()
    pass_wide.wait()

    send_dz.all_sent()
    w_all = r.wide_to.reshape(DIM, WIDE)
    w_gu, w_dn = w_all.at[:, : 2 * FF], w_all.at[:, 2 * FF :]

    def work(c, carry):
        send_gate.arrived(c)
        send_dz.arrived(c)
        at = pl.ds(pl.multiple_of(c * PART, PART), PART)
        stage(r.dz_to, c)
        send_a2.arrived(c)
        a = merge(take(r.a2_to, c))
        r.a_rows[at] = a
        gu = dot(a, w_gu[...])
        g, up = gu[:, :FF], gu[:, FF:]
        s = 1.0 / (1.0 + jnp.exp(-g))
        hid = (g * s * up).astype(BF)
        r.hid[at] = hid
        note = take(r.gates_to, c)
        kept = note[:, 1:2] == seat[None]
        column = jnp.sum(jnp.where(kept, note[:, 0:1], 0.0), axis=2, keepdims=True)
        staged()
        dz_part = r.stage[...].astype(F32)
        dy = (dz_part * column).reshape(PART, DIM).astype(BF)
        r.dy[at] = dy
        dhid = dot(dy, w_dn[...])
        dgu = jnp.concatenate([dhid * up * s * (1.0 + g * (1.0 - s)), dhid * g * s], axis=1)
        dgu = dgu.astype(BF)
        r.dgu[at] = dgu
        da = dot(dgu, w_gu[...], ((1,), (1,)))
        send_a2.sent(c)
        put(r.a2_rows, c, da.reshape(8, CAP, DIM).astype(BF))
        send_da.start(c)
        y = dot(hid, w_dn[...], ((1,), (1,))).reshape(8, CAP, DIM).astype(BF)
        put(r.dz_rows, c, y)
        inner = jnp.sum(y.astype(F32) * dz_part, axis=2, keepdims=True)
        inner = jnp.sum(jnp.where(kept, inner, 0.0), axis=1, keepdims=True)
        put(r.dg_rows, c, jnp.broadcast_to(inner, (8, 8, ROWS)))
        send_dg.start(c)
        return carry

    lax.fori_loop(0, 4, work, 0)

    def weigh(i, carry):
        to = spin("x", i)
        for half in range(2):
            at = rows_of(half * 4 + to)
            gu = dot(r.a_rows[:, at], r.dgu[...], ((0,), (0,)))
            r.grad[half, to, :, :, : 2 * FF] = gu.astype(BF).reshape(4, 32, 2 * FF)
            dn = dot(r.dy[:, at], r.hid[...], ((0,), (0,)))
            r.grad[half, to, :, :, 2 * FF :] = dn.astype(BF).reshape(4, 32, FF)

        @pl.when(i < 4)
        def _():
            send_grad.copy(i).start()

        return carry

    lax.fori_loop(1, 5, weigh, 0)
    send_grad.start_own()

    pass_all.wait()
    swap_all.start()
    for c in range(4):
        send_dg.arrived(c)
    dgate = r.dg_to[:, 0, :]
    dc = jnp.where(named, dgate - jnp.sum(gate * dgate, axis=0, keepdims=True), 0.0) / total
    dl = probs * (dc - jnp.sum(probs * dc, axis=0, keepdims=True))
    dl = jnp.concatenate([dl, jnp.zeros((128 - EXPERTS, ROWS), F32)], axis=0).astype(BF)
    r.dl[...] = dl
    r.sum[...] = dot(dl, r.router[...], ((0,), (1,)))

    def unmix(c, carry):
        send_da.arrived(c)
        stage(r.da_to, c)
        staged()
        r.sum[...] += dot(hot_part(c).astype(BF), merge(r.stage[...]), ((0,), (0,)))
        return carry

    lax.fori_loop(0, 4, unmix, 0)
    send_y.start(0)
    send_y.start(1)
    dx_two, terms_two = norm_back(r.x1[...], rms(r.x1[...]), gain_two, r.sum[...])
    gain_two_grad = jnp.sum(terms_two, axis=0, keepdims=True)
    r.dx1[...] = dz + dx_two
    r.db[...] = r.dx1[...].astype(BF)
    do = dot(r.db[...], r.w_out[...]).astype(BF)
    for h in range(8):
        r.do_rows[h] = do[:, h * 128 : (h + 1) * 128]
    send_do.start()
    send_y.start(2)
    send_y.start(3)

    def spread_out(i, carry):
        part = dot(r.db[:, rows_of(i)], r.ob[...], ((0,), (0,)))
        part = part.reshape(2, 2, 4, 8, DIM).astype(BF)
        for n in range(4):
            at = pl.ds((lax.div(i, 4) * 2 + n // 2) * 4, 4)
            r.out_to[at, n % 2, lax.rem(i, 4)] = part[n // 2, n % 2]
        return carry

    lax.fori_loop(0, 8, spread_out, 0)
    swap_gwo.start()

    def add_core(i, carry):
        both = r.gwo_mid[i].astype(F32) + r.out_to[i, core].astype(F32)
        r.gwo_mid[i] = both.astype(BF)
        return carry

    send_do.wait()
    r.dk[...] = jnp.zeros_like(r.dk)
    r.dv[...] = jnp.zeros_like(r.dv)
    for tile in range(8):
        width, at = ROWS * (tile + 1), rows_of(tile)
        keys = pl.ds(0, width)
        q = stacked(r.qr[at])
        level = r.level[at]
        level = jnp.concatenate([level[:, :1], level[:, HEAD : HEAD + 1]], axis=0)
        probs_at = jnp.exp(masked_scores(tile, q, width) - level)
        do = r.do_to[tile]
        inner = head_mean(do.astype(F32) * r.mixed[at], first) * HEAD
        inner = jnp.concatenate([inner[:, :1], inner[:, HEAD : HEAD + 1]], axis=0)
        do = stacked(do)
        dp = dot(do, r.vv[keys], ((1,), (1,)))
        ds = (probs_at * (dp - inner)).astype(BF)
        r.dq[at] = beside(dot(ds, r.kr[keys])) * HEAD**-0.5
        r.dk[keys] += dot(ds, q, ((0,), (0,)))
        r.dv[keys] += dot(probs_at.astype(BF), do, ((0,), (0,)))

    swap_gwo.wait()
    bring(r.gwo_co, r.gwo_mid).wait()
    lax.fori_loop(0, 16, add_core, 0)
    r.gain_q_grad[...] = jnp.zeros_like(r.gain_q_grad)
    r.gain_k_grad[...] = jnp.zeros_like(r.gain_k_grad)

    def back(i, carry):
        j, _ = partner(CTX, lax.rem(i, 8))
        at = rows_of(j)
        cos, sin = r.cos[at], -r.sin[at]
        qkv = r.pre[at]
        q, kv = qkv[:, :128], qkv[:, 128:]
        k = jnp.where(first, kv, pltpu.roll(kv, HEAD, 1))
        dk, dv = r.dk[at] * HEAD**-0.5, r.dv[at]
        dk, dv = dk + pltpu.roll(dk, HEAD, 1), dv + pltpu.roll(dv, HEAD, 1)
        dq, terms = head_norm_back(q, gain_q, turn_pair(r.dq[at], cos, sin, front), first)
        r.gain_q_grad[...] += terms
        dk, terms = head_norm_back(k, gain_k, turn_pair(dk, cos, sin, front), first)
        r.gain_k_grad[...] += terms
        r.dqkv[at] = jnp.concatenate([dq, jnp.where(first, dk, dv)], axis=1).astype(BF)

        @pl.when(i < 8)
        def _():
            send_dq.copy(i).start()

        return carry

    lax.fori_loop(1, 9, back, 0)
    send_dq.start_own()
    send_grad.wait()
    bring(r.grad_to, r.wide_to).wait()

    def add_grad(i, carry):
        total = sum(r.wide_to[lax.div(i, 4), n, lax.rem(i, 4)].astype(F32) for n in range(4))
        r.grad_mid[i] = total.astype(BF)
        return carry

    lax.fori_loop(0, 8, add_grad, 0)
    last_grad.start()
    pass_gwo.start()

    diagonal = lax.broadcasted_iota(I32, (ROWS, 128), 0) == lax.broadcasted_iota(I32, (ROWS, 128), 1)

    def small(i, carry):
        at = rows_of(i)
        part = dot(r.a_all[:, at], r.dqkv[...], ((0,), (0,)))
        r.heads_to[i, :, :, :, :, pl.ds(0, 256)] = part.reshape(2, 2, 4, 8, 256).astype(BF)
        column = jnp.sum(part * r.w_heads[at].astype(F32), axis=1, keepdims=True)
        r.gain_one_grad[:, at] = jnp.sum(jnp.where(diagonal, column, 0.0), axis=0, keepdims=True)
        return carry

    lax.fori_loop(0, 8, small, 0)
    pair = jnp.where(
        first,
        r.gain_q_grad[...] + pltpu.roll(r.gain_q_grad[...], HEAD, 1),
        r.gain_k_grad[...],
    )
    gain_grads = pack_gains(
        jnp.concatenate([r.gain_one_grad[...] / gain_one, gain_two_grad, pair], axis=1)
    )
    side = jnp.where(
        lax.broadcasted_iota(I32, (128, 8, 128), 1) == 0, gain_grads[:, None], 0.0
    ).reshape(DIM, 128) + dot(r.a2[...], r.dl[...], ((0,), (1,)))
    r.heads_to[:, :, :, :, :, pl.ds(256, 128)] = side.reshape(8, 2, 2, 4, 8, 128).astype(BF)
    swap_hg.start()
    swap_hg.wait()
    r.hg_mid[...] = (r.heads_to[:, :, core].astype(F32) + r.hg_co[...].astype(F32)).astype(BF)
    pass_hg.start()

    send_dq.wait()
    swap_all.wait()
    for h in range(8):
        r.dq_all[:, h * 256 : (h + 1) * 256] = r.dq_to[h]

    def fetch(i):
        for n in range(4):
            pltpu.make_async_copy(
                r.wall_to.at[pl.ds((lax.div(i, 4) * 2 + n // 2) * 4, 4), lax.rem(i, 4), n % 2],
                r.wall_rows.at[lax.rem(i, 2), pl.ds(4 * n, 4)],
                r.s_fetch.at[lax.rem(i, 2)],
            ).start()

    fetch(0)

    def unproject(i, carry):
        @pl.when(i < 7)
        def _():
            fetch(i + 1)

        now = lax.rem(i, 2)
        drain(r.wall_rows.at[now], r.s_fetch.at[now])
        r.sum[:, rows_of(i)] = dot(r.dq_all[...], merge(r.wall_rows[now]), ((1,), (1,)))
        return carry

    lax.fori_loop(0, 8, unproject, 0)
    x_own = r.x[...].astype(F32)
    dx_one, _ = norm_back(x_own, rms(x_own), gain_one, r.sum[...])
    r.grad_inputs[...] = (r.dx1[...] + dx_one).astype(BF)

    pass_hg.wait()
    r.hg_sum[...] = sum(r.hg_z[n].astype(F32) for n in range(4)).astype(BF)
    last_hg.start()
    pass_gwo.wait()
    bring(r.gwo_x, r.out_to.at[:, 0]).wait()

    def add_spot(i, carry):
        total = sum(r.out_to[i, 0, n].astype(F32) for n in range(4))
        r.gwo_sum[i] = total.astype(BF)
        return carry

    lax.fori_loop(0, 16, add_spot, 0)
    last_gwo.start()

    r.sum[...] = r.x1[...]

    def gates_of(c):
        return jnp.concatenate([r.gate[lax.div(four, 4)] for four in runs(c)], axis=0)

    def mix(c, carry):
        send_y.arrived(c)
        stage(r.y_to, c)
        staged()
        y = merge(r.stage[...])
        weights = hot_part(c).reshape(8, CAP, ROWS) * gates_of(c)[:, None]
        weights = weights.reshape(PART, ROWS)
        high = weights.astype(BF)
        low = (weights - high.astype(F32)).astype(BF)
        r.sum[...] += dot(high, y, ((0,), (0,))) + dot(low, y, ((0,), (0,)))
        return carry

    lax.fori_loop(0, 4, mix, 0)
    r.output[...] = r.sum[...].astype(BF)
    for send in (last_gwo, last_grad, last_hg):
        send.wait()
    for send in (send_gate, send_da, send_dg, send_y):
        send.all_sent()


INPUTS = (
    ("lengths", pltpu.SMEM),
    ("blocks", pltpu.SMEM),
    ("x", pltpu.VMEM),
    ("dz", pltpu.VMEM),
    ("wq", pltpu.VMEM),
    ("wk", pltpu.VMEM),
    ("wv", pltpu.VMEM),
    ("wr", pltpu.VMEM),
    ("norm", pltpu.VMEM),
    ("out", pltpu.VMEM),
    ("routes", pltpu.VMEM),
    ("priority", pltpu.VMEM),
    ("w_gu", pl.ANY),
    ("w_dn", pl.ANY),
)
OUTPUTS = (
    ("output", (ROWS, DIM), BF),
    ("grad_inputs", (ROWS, DIM), BF),
)
ROW_SLOTS = (EXPERTS, CAP, DIM)
LANDING = (
    ("hg_last", (16, 8, 384), BF),
    ("gwo_last", (16, 8, DIM), BF),
    ("grad_last", (8, 32, WIDE), BF),
    ("dz_to", ROW_SLOTS, BF),
    ("y_to", ROW_SLOTS, BF),
    ("da_to", ROW_SLOTS, BF),
    ("grad_to", (2, 4, 4, 32, WIDE), BF),
    ("gwo_co", (16, 4, 8, DIM), BF),
    ("gwo_x", (16, 4, 8, DIM), BF),
    ("wall_to", (16, 4, 2, 8, 2 * DIM), BF),
)
SCRATCH = (
    ("heads", (8, 8, 384), BF),
    ("picks", (16, 128), I32),
    ("picks_to", (8, 16, 128), I32),
    ("x_to", (8, ROWS, DIM), BF),
    ("heads_to", (8, 2, 2, 4, 8, 384), BF),
    ("wide_to", (2, 4, 4, 32, WIDE), BF),
    ("out_to", (16, 2, 4, 8, DIM), BF),
    ("hot", (EXPERTS * CAP, ROWS), F32),
    ("wall", (8, 2 * DIM), BF),
    ("dz_rows", ROW_SLOTS, BF),
    ("a2_rows", ROW_SLOTS, BF),
    ("w_heads", (DIM, 256), BF),
    ("router", (DIM, 128), BF),
    ("a_all", (GTOK, DIM), BF),
    ("pre", (GTOK, 256), F32),
    ("cos", (GTOK, 128), F32),
    ("sin", (GTOK, 128), F32),
    ("qr", (GTOK, 128), BF),
    ("kr", (GTOK, 128), BF),
    ("vv", (GTOK, 128), BF),
    ("mixed", (GTOK, 128), F32),
    ("level", (GTOK, 128), F32),
    ("o_rows", (8, ROWS, 128), BF),
    ("o_to", (8, ROWS, 128), BF),
    ("w_out", (DIM, DIM), BF),
    ("ob", (ROWS, DIM), BF),
    ("x1", (ROWS, DIM), F32),
    ("a2", (ROWS, DIM), BF),
    ("gate", (8, 4, ROWS), F32),
    ("gates", (EXPERTS, 8, 128), F32),
    ("gates_to", (EXPERTS, 8, 128), F32),
    ("a2_to", ROW_SLOTS, BF),
    ("a_rows", (EXPERTS * CAP, DIM), BF),
    ("hid", (EXPERTS * CAP, FF), BF),
    ("dy", (EXPERTS * CAP, DIM), BF),
    ("dgu", (EXPERTS * CAP, 2 * FF), BF),
    ("dg_rows", (EXPERTS, 8, ROWS), F32),
    ("dg_to", (EXPERTS, 8, ROWS), F32),
    ("grad", (2, 4, 4, 32, WIDE), BF),
    ("grad_mid", (8, 32, WIDE), BF),
    ("stage", (8, CAP, DIM), BF),
    ("sum", (ROWS, DIM), F32),
    ("dl", (128, ROWS), BF),
    ("dx1", (ROWS, DIM), F32),
    ("db", (ROWS, DIM), BF),
    ("do_rows", (8, ROWS, 128), BF),
    ("do_to", (8, ROWS, 128), BF),
    ("gwo_mid", (16, 4, 8, DIM), BF),
    ("gwo_sum", (16, 8, DIM), BF),
    ("dq", (GTOK, 128), F32),
    ("dk", (GTOK, 128), F32),
    ("dv", (GTOK, 128), F32),
    ("dqkv", (GTOK, 256), BF),
    ("dq_to", (8, ROWS, 256), BF),
    ("dq_all", (ROWS, 2 * DIM), BF),
    ("wall_rows", (2, 16, 8, 2 * DIM), BF),
    ("gain_one_grad", (1, DIM), F32),
    ("gain_q_grad", (1, 128), F32),
    ("gain_k_grad", (1, 128), F32),
    ("hg_co", (8, 2, 4, 8, 384), BF),
    ("hg_mid", (8, 2, 4, 8, 384), BF),
    ("hg_z", (4, 8, 2, 8, 384), BF),
    ("hg_sum", (8, 2, 8, 384), BF),
)
SEMS = dict(s_stage=1, s_fetch=2, s_x=11)
PAIR_SEMS = ("s_dz", "s_a2", "s_gate", "s_da", "s_dg", "s_y")
SEMS.update(dict.fromkeys(PAIR_SEMS, 8))
SEND_SEMS = (
    "s_picks",
    "s_heads",
    "s_heads_pass",
    "s_heads_co",
    "s_gu",
    "s_dn",
    "s_wide",
    "s_out",
    "s_out_x",
    "s_out_co",
    "s_all",
    "s_all_x",
    "s_all_co",
    "s_o",
    "s_grad",
    "s_grad_last",
    "s_do",
    "s_dq",
    "s_gwo_co",
    "s_gwo_x",
    "s_gwo",
    "s_hg_co",
    "s_hg_z",
    "s_hg",
)
SEMS.update(dict.fromkeys(SEND_SEMS, 2))


def layer(*operands):
    names = [name for name, *_ in INPUTS + OUTPUTS + LANDING + SCRATCH] + list(SEMS)

    def body(*refs):
        layer_kernel(types.SimpleNamespace(**dict(zip(names, refs))))

    return pl.pallas_call(
        body,
        out_shape=[jax.ShapeDtypeStruct(shape, kind) for _, shape, kind in OUTPUTS + LANDING],
        in_specs=[pl.BlockSpec(memory_space=space) for _, space in INPUTS],
        out_specs=[pl.BlockSpec(memory_space=pltpu.VMEM)] * len(OUTPUTS)
        + [pl.BlockSpec(memory_space=pl.ANY)] * len(LANDING),
        scratch_shapes=[pltpu.VMEM(shape, kind) for _, shape, kind in SCRATCH]
        + [pltpu.SemaphoreType.DMA((n,)) for n in SEMS.values()],
        compiler_params=pltpu.CompilerParams(
            collective_id=0, has_side_effects=True, vmem_limit_bytes=VMEM_LIMIT
        ),
        name="layer",
    )(*operands)


VMEM_LIMIT = 63 << 20


def finish_kernel(
    output, grad_inputs, hg, gwo, experts, o_output, o_inputs, o_q, o_k, o_v, o_out, o_router, o_gains, o_gu, o_dn
):
    o_output[...] = output[...]
    o_inputs[...] = grad_inputs[...]
    heads = [hg[2 * c].astype(F32) + hg[2 * c + 1].astype(F32) for c in range(8)]
    for c in range(8):
        o_q[:, c * 128 : (c + 1) * 128] = heads[c][:, :128]
    for c in range(4):
        at, two = slice(c * 128, (c + 1) * 128), heads[2 * c : 2 * c + 2]
        o_k[:, at] = jnp.concatenate([head[:, 128:192] for head in two], axis=1)
        o_v[:, at] = jnp.concatenate([head[:, 192:256] for head in two], axis=1)
    side = sum(head[:, 256:] for head in heads)
    o_router[...] = side[:, :EXPERTS]
    o_gains[...] = side[:1, EXPERTS : EXPERTS + GAINS]
    o_out[...] = sum(gwo[n].astype(F32) for n in range(16))
    o_gu[...] = experts[:, :, : 2 * FF].astype(F32)
    o_dn[...] = experts[:, :, 2 * FF :].astype(F32)


def finish(*operands):
    shapes = (
        ((ROWS, DIM), BF),
        ((ROWS, DIM), BF),
        ((8, HEADS * HEAD), F32),
        ((8, KV_HEADS * HEAD), F32),
        ((8, KV_HEADS * HEAD), F32),
        ((8, DIM), F32),
        ((8, EXPERTS), F32),
        ((1, GAINS), F32),
        ((8, 32, 2 * FF), F32),
        ((8, 32, FF), F32),
    )
    vmem = pl.BlockSpec(memory_space=pltpu.VMEM)
    return pl.pallas_call(
        finish_kernel,
        out_shape=[jax.ShapeDtypeStruct(shape, kind) for shape, kind in shapes],
        in_specs=[vmem] * len(operands),
        out_specs=[vmem] * len(shapes),
        compiler_params=pltpu.CompilerParams(vmem_limit_bytes=VMEM_LIMIT),
        name="finish",
    )(*operands)


def shards(
    inputs,
    cotangent,
    w_query,
    key_weight,
    value_weight,
    w_output,
    w_router,
    norm_gains,
    w_gate_up,
    w_down,
    seq_lengths,
    block_map,
    routes,
    priority,
):
    output, grad_inputs, hg, gwo, experts, *_ = layer(
        seq_lengths[0],
        block_map[0],
        inputs[0],
        cotangent[0],
        w_query,
        key_weight,
        value_weight,
        w_router,
        norm_gains[None],
        w_output.T,
        routes[0].T,
        priority[0],
        w_gate_up,
        jnp.swapaxes(w_down, 1, 2),
    )
    output, grad_inputs, q, k, v, out, router, gains, gate_up, down = finish(
        output, grad_inputs, hg, gwo, experts
    )
    return (
        output[None],
        grad_inputs[None],
        q,
        k,
        v,
        out.T,
        router,
        gains[0],
        gate_up,
        jnp.swapaxes(down, 1, 2),
    )


def solution(mesh):
    groups = ("yh", "co", "z")
    specs = (
        P(groups, CTX, None),
        P(groups, CTX, None),
        P(ALL, None),
        P(ALL, None),
        P(ALL, None),
        P(None, ALL),
        P(ALL, None),
        P(ALL),
        P(("yh", "co"), WT, None),
        P(("yh", "co"), None, WT),
        P(groups, None),
        P(groups, None),
        P(groups, CTX, None),
        P(groups, CTX, None),
    )
    return jax.shard_map(
        shards,
        mesh=Mesh(mesh.devices.reshape(SIZES), ALL),
        in_specs=specs,
        out_specs=specs[:10],
        check_vma=False,
    )
```
